32 devices in a mesh: ctx: 8 (over z, x), head: 4 (over y, core).
Axes of the slice: x: 2, y: 2, z: 4, core: 2. Of those that a mesh axis runs over, the one named last changes fastest.
Arguments:
- queries: bfloat16 [1024, 4096], P('ctx', 'head'), may hold values from -4 to 4
- keys: bfloat16 [1024, 4096], P('ctx', 'head'), may hold values from -4 to 4
- values: bfloat16 [1024, 4096], P('ctx', 'head'), may hold values from -6 to 6
- outputs: bfloat16 [1024, 4096], P('ctx', 'head'), may hold values from -4 to 4
- grad_out: bfloat16 [1024, 4096], P(('ctx', 'head')), may hold values from -96 to 96
- log_norm: float32 [32, 1024], P('head', 'ctx'), may hold values from 6.5 to 7.5
- glob_keys: bfloat16 [256, 4096], P(None, 'head'), may hold values from -4 to 4
- glob_values: bfloat16 [256, 4096], P(None, 'head'), may hold values from -6 to 6
- key_lists: int32 [8, 6], replicated, may hold values from -1 to 7, as said below
Outputs:
- query_grads: bfloat16 [1024, 4096], P('ctx', 'head')
- key_grads: bfloat16 [1024, 4096], P('ctx', 'head')
- value_grads: bfloat16 [1024, 4096], P('ctx', 'head')
- glob_key_grads: float32 [256, 4096], P('ctx', 'head')
- glob_value_grads: float32 [256, 4096], P('ctx', 'head')
The draws below stay inside these ranges and needn't reach their ends.
Inputs may be any that keep to these rules, and one draw needn't show every extreme that they name: `key_lists`: row i holds i - 1, i, i + 1 (each -1 where that block lies outside 0 to 7) and then, for r = 1 to 3, one block of group (i + r * 2) mod 8, where group c holds blocks c * 1 to (c + 1) - 1.
All inputs are finite; a program needn't handle non-finite values.
Results may differ from the reference program's by a relative error of at most 0.0055.
Values may be sent and summed in bfloat16 or wider, within the bound.
A program may use at most 64 MiB of HBM per device.

```python
import jax
import jax.numpy as jnp
from jax import lax

HEADS = 32
HEAD_DIM = 128
BLOCK = 128
GLOB = 256
RAND = 3
LIST = 6
BLK_DEV = 1
GROUPS = 8
STRIDE = 2
NB = 8
SEQ = 1024


def draw_key_lists(key, part):
    block_ids = jnp.arange(NB, dtype=jnp.int32)
    window = block_ids[:, None] + jnp.arange(-1, 2, dtype=jnp.int32)[None, :]
    window = jnp.where((window >= 0) & (window < NB), window, -1)
    group_ids = block_ids // BLK_DEV
    rounds = jnp.arange(1, RAND + 1, dtype=jnp.int32)
    target = (group_ids[:, None] + rounds[None, :] * STRIDE) % GROUPS
    within = jax.random.randint(key, (NB, RAND), 0, BLK_DEV, dtype=jnp.int32)
    return jnp.concatenate([window, target * BLK_DEV + within], axis=1).astype(jnp.int32)


def block_scale(stream_key, extent, shards, least, largest):
    gain, own = 1.0, jax.random.fold_in(stream_key, 6)
    for axis_at, blocks in shards:
        heights = jnp.exp(jax.random.uniform(jax.random.fold_in(own, axis_at), (blocks,), jnp.float32, least / len(shards), largest / len(shards)))
        gain = gain * jnp.repeat(heights, extent[axis_at] // blocks).reshape([-1 if axis == axis_at else 1 for axis in range(len(extent))])
    return gain


def normal_values(own_key, dims, deviation, limit, cuts=(), kind=jnp.bfloat16):
    drawn = jax.random.normal(own_key, dims, jnp.float32) * deviation
    if len(cuts) > 0:
        drawn = block_scale(own_key, dims, cuts, -0.22, 0.18) * drawn
    return jnp.clip(drawn, min=-limit, max=limit).astype(kind)


def setup_inputs(seed: int = 0) -> dict:
    splits = jax.random.split(jax.random.key(seed), 10)
    return {
        "queries": normal_values(splits[0], (SEQ, HEADS * HEAD_DIM), 0.5, 4.0, ((0, 8), (1, 4))),
        "keys": normal_values(splits[1], (SEQ, HEADS * HEAD_DIM), 1.0, 4.0, ((0, 8), (1, 4))),
        "values": normal_values(splits[2], (SEQ, HEADS * HEAD_DIM), 1.0, 6.0, ((0, 8), (1, 4))),
        "outputs": normal_values(splits[3], (SEQ, HEADS * HEAD_DIM), 0.3, 4.0, ((0, 8), (1, 4))),
        "grad_out": normal_values(splits[4], (SEQ, HEADS * HEAD_DIM), 16.0, 96.0, ((0, 32),)),
        "log_norm": jnp.clip(6.5 + 1.0 * jax.random.uniform(splits[5], (HEADS, SEQ), jnp.float32) ** block_scale(splits[5], (HEADS, SEQ), ((0, 4), (1, 8)), -0.2, 0.2), 6.5, 7.5),
        "glob_keys": normal_values(splits[6], (GLOB, HEADS * HEAD_DIM), 1.0, 4.0, ((1, 4),)),
        "glob_values": normal_values(splits[7], (GLOB, HEADS * HEAD_DIM), 1.0, 6.0, ((1, 4),)),
        "key_lists": draw_key_lists(jax.random.fold_in(splits[9], 71), 0),
    }


def tile_grads(query_rows, grad_rows, norm_rows, delta_rows, key_rows, value_rows, keep_mask):
    att_scale = HEAD_DIM ** -0.5
    query_full = query_rows.astype(jnp.float32)
    grad_full = grad_rows.astype(jnp.float32)
    key_full = key_rows.astype(jnp.float32)
    value_full = value_rows.astype(jnp.float32)
    scores = jnp.einsum("nbd,nkd->nbk", query_full, key_full) * att_scale
    weights = jnp.exp(scores - norm_rows[:, :, None]) * keep_mask[:, None, :]
    dprobs = jnp.einsum("nbd,nkd->nbk", grad_full, value_full)
    dscores = weights * (dprobs - delta_rows[:, :, None])
    weights_low = lax.optimization_barrier(weights.astype(jnp.bfloat16)).astype(jnp.float32)
    dscores_low = lax.optimization_barrier(dscores.astype(jnp.bfloat16)).astype(jnp.float32)
    grad_values = jnp.einsum("nbk,nbd->nkd", weights_low, grad_full)
    grad_keys = jnp.einsum("nbk,nbd->nkd", dscores_low, query_full) * att_scale
    grad_queries = jnp.einsum("nbk,nkd->nbd", dscores_low, key_full) * att_scale
    return grad_queries, grad_keys, grad_values


def reference(queries, keys, values, outputs, grad_out, log_norm, glob_keys, glob_values, key_lists):
    num_blocks = key_lists.shape[0]
    live_mask = key_lists >= 0
    slot_ids = jnp.maximum(key_lists, 0).astype(jnp.int32)
    keep_all = jnp.concatenate([jnp.ones((num_blocks, GLOB), jnp.float32), jnp.repeat(live_mask.astype(jnp.float32), BLOCK, axis=1)], axis=1)

    def one_head(head_index):
        start = (head_index * HEAD_DIM).astype(jnp.int32)

        def head_cols(source):
            return lax.dynamic_slice_in_dim(source, start, HEAD_DIM, 1)

        def head_tiles(source):
            return head_cols(source).reshape(num_blocks, BLOCK, HEAD_DIM)

        query_tiles = head_tiles(queries)
        key_tiles = head_tiles(keys)
        value_tiles = head_tiles(values)
        grad_tiles = head_tiles(grad_out)
        output_tiles = head_tiles(outputs)
        glob_key_rows = head_cols(glob_keys)[None]
        glob_value_rows = head_cols(glob_values)[None]
        norm_tiles = lax.dynamic_index_in_dim(log_norm, head_index, 0, keepdims=False).reshape(num_blocks, BLOCK)
        delta_tiles = jnp.sum(grad_tiles.astype(jnp.float32) * output_tiles.astype(jnp.float32), axis=2)

        def visit(running, block_index):
            acc_keys, acc_values, acc_glob_keys, acc_glob_values = running
            list_row = lax.dynamic_index_in_dim(slot_ids, block_index, 0, keepdims=False)
            key_rows = jnp.concatenate([glob_key_rows, jnp.take(key_tiles, list_row, axis=0).reshape(1, LIST * BLOCK, HEAD_DIM)], axis=1)
            value_rows = jnp.concatenate([glob_value_rows, jnp.take(value_tiles, list_row, axis=0).reshape(1, LIST * BLOCK, HEAD_DIM)], axis=1)

            def pick(source):
                return lax.dynamic_slice_in_dim(source, block_index, 1, 0)

            grad_q, grad_k, grad_v = tile_grads(pick(query_tiles), pick(grad_tiles), pick(norm_tiles), pick(delta_tiles), key_rows, value_rows, pick(keep_all))
            acc_keys = acc_keys.at[list_row].add(grad_k[0, GLOB:].reshape(LIST, BLOCK, HEAD_DIM))
            acc_values = acc_values.at[list_row].add(grad_v[0, GLOB:].reshape(LIST, BLOCK, HEAD_DIM))
            acc_glob_keys = acc_glob_keys + grad_k[0, :GLOB]
            acc_glob_values = acc_glob_values + grad_v[0, :GLOB]
            return (acc_keys, acc_values, acc_glob_keys, acc_glob_values), grad_q[0].astype(jnp.bfloat16)

        zero_tiles = jnp.zeros((num_blocks, BLOCK, HEAD_DIM), jnp.float32)
        zero_glob = jnp.zeros((GLOB, HEAD_DIM), jnp.float32)
        running, dq_tiles = lax.scan(visit, (zero_tiles, zero_tiles, zero_glob, zero_glob), jnp.arange(num_blocks, dtype=jnp.int32))
        return dq_tiles, running[0].astype(jnp.bfloat16), running[1].astype(jnp.bfloat16), running[2], running[3]

    dq_all, dk_all, dv_all, gk_all, gv_all = lax.map(one_head, jnp.arange(HEADS, dtype=jnp.int32))

    def join_tokens(stacked):
        return jnp.transpose(stacked, (1, 2, 0, 3)).reshape(num_blocks * BLOCK, HEADS * HEAD_DIM)

    def join_glob(stacked):
        return jnp.transpose(stacked, (1, 0, 2)).reshape(GLOB, HEADS * HEAD_DIM)

    return join_tokens(dq_all), join_tokens(dk_all), join_tokens(dv_all), join_glob(gk_all), join_glob(gv_all)
```

```python
import functools
import math

import jax
import jax.numpy as jnp
from jax import lax
from jax.experimental import pallas as pl
from jax.experimental.pallas import tpu as pltpu
from jax.sharding import PartitionSpec as P

HEAD_DIM = 128
BLOCK = 128
GLOB = 256
RAND = 3
LOG2E = math.log2(math.e)


def extended_2(cells, sides, width):
    for axis, dim in sides:
        count = lax.axis_size(axis)
        ends = count - 1
        head = lax.slice_in_dim(cells, 0, width, axis=dim)
        tail = lax.slice_in_dim(cells, cells.shape[dim] - width, cells.shape[dim], axis=dim)
        cells = jnp.concatenate(
            [
                lax.ppermute(tail, axis, [(i, (i + 1) % count) for i in range(ends)]),
                cells,
                lax.ppermute(head, axis, [((i + 1) % count, i) for i in range(ends)]),
            ],
            axis=dim,
        )
    return cells


def passed_along(value, axis, by):
    peers = lax.axis_size(axis)
    pairs = [(i, i + by) for i in range(peers) if 0 <= i + by < peers]
    return lax.ppermute(value, axis, pairs)


def shifted(value, axis, by):
    peers = lax.axis_size(axis)
    return lax.ppermute(value, axis, [(i, (i + by) % peers) for i in range(peers)])


def tile_grads(query_rows, grad_rows, norm_rows, delta_rows, key_rows, value_rows, keep_mask):
    att_scale = HEAD_DIM ** (-0.5)
    scores = (
        jnp.einsum("nbd,nkd->nbk", query_rows, key_rows, preferred_element_type=jnp.float32)
        * att_scale
    )
    weights = jnp.exp(scores - norm_rows[:, :, None]) * keep_mask[:, None, :]
    dprobs = jnp.einsum("nbd,nkd->nbk", grad_rows, value_rows, preferred_element_type=jnp.float32)
    dscores = weights * (dprobs - delta_rows[:, :, None])
    weights_low = weights.astype(jnp.bfloat16)
    dscores_low = dscores.astype(jnp.bfloat16)
    grad_values = jnp.einsum(
        "nbk,nbd->nkd", weights_low, grad_rows, preferred_element_type=jnp.float32
    )
    grad_keys = (
        jnp.einsum("nbk,nbd->nkd", dscores_low, query_rows, preferred_element_type=jnp.float32)
        * att_scale
    )
    grad_queries = (
        jnp.einsum("nbk,nkd->nbd", dscores_low, key_rows, preferred_element_type=jnp.float32)
        * att_scale
    )
    return (grad_queries, grad_keys, grad_values)


def head_cols(source, head_index):
    return source[:, head_index * HEAD_DIM : (head_index + 1) * HEAD_DIM]


def head_blocks(source, head_index, num_blocks):
    return head_cols(source, head_index).reshape(num_blocks, BLOCK, HEAD_DIM)


def gather_tiles(tile_rows, slot_ids):
    picked = jnp.take(tile_rows, slot_ids, axis=0)
    return picked.reshape(slot_ids.shape[0], slot_ids.shape[1] * BLOCK, HEAD_DIM)


def tile_picker(slot_ids, hit_mask, num_blocks):
    one_hot = (
        slot_ids[:, :, None] == jnp.arange(num_blocks, dtype=jnp.int32)[None, None, :]
    ) & hit_mask[:, :, None]
    return one_hot.astype(jnp.float32)


def add_tiles(picker, flat_grads, num_blocks):
    tiled_grads = flat_grads.reshape(picker.shape[0], picker.shape[1], BLOCK, HEAD_DIM)
    summed = jnp.einsum("nle,nlbd->ebd", picker, tiled_grads, precision=lax.Precision.HIGHEST)
    return summed.reshape(num_blocks * BLOCK, HEAD_DIM)


def tile_keep(hit_mask, extra_cols):
    tile_cols = jnp.repeat(hit_mask.astype(jnp.float32), BLOCK, axis=1)
    return jnp.concatenate(
        [jnp.ones((hit_mask.shape[0], extra_cols), jnp.float32), tile_cols], axis=1
    )


def with_glob(glob_rows, tile_rows):
    spread = glob_rows[None]
    return jnp.concatenate([spread, tile_rows], axis=1)


def shards(queries, keys, values, outputs, grad_out, log_norm, glob_keys, glob_values, key_lists):
    row_count, col_count = queries.shape
    head_count = col_count // HEAD_DIM
    block_count = row_count // BLOCK
    group_count = lax.axis_size("ctx")
    my_group = lax.axis_index("ctx")
    first_block = my_group * block_count
    incoming = lax.all_to_all(grad_out, "head", split_axis=1, concat_axis=0, tiled=True)
    row_delta = jnp.sum(
        (incoming.astype(jnp.float32) * outputs.astype(jnp.float32)).reshape(
            row_count, head_count, HEAD_DIM
        ),
        axis=2,
    ).T
    own_lists = lax.dynamic_slice_in_dim(key_lists, first_block, block_count, 0)
    query_heads = [
        head_blocks(queries, head_index, block_count) for head_index in range(head_count)
    ]
    grad_heads = [
        head_blocks(incoming, head_index, block_count) for head_index in range(head_count)
    ]
    norm_heads = [
        log_norm[head_index].reshape(block_count, BLOCK) for head_index in range(head_count)
    ]
    delta_heads = [
        row_delta[head_index].reshape(block_count, BLOCK) for head_index in range(head_count)
    ]
    extended = extended_2(jnp.stack([keys, values]), (("ctx", 1),), BLOCK)
    ext_blocks = block_count + 2
    near_lists = own_lists[:, :3]
    near_live = near_lists >= 0
    near_slots = jnp.clip(near_lists - (first_block - 1), 0, ext_blocks - 1)
    near_keep = tile_keep(near_live, GLOB)
    near_picker = tile_picker(near_slots, near_live, ext_blocks)
    dq_parts, dk_parts, dv_parts, glob_dk_parts, glob_dv_parts = ([], [], [], [], [])
    for head_index in range(head_count):
        ext_keys = head_blocks(extended[0], head_index, ext_blocks)
        ext_values = head_blocks(extended[1], head_index, ext_blocks)
        key_rows = with_glob(head_cols(glob_keys, head_index), gather_tiles(ext_keys, near_slots))
        value_rows = with_glob(
            head_cols(glob_values, head_index), gather_tiles(ext_values, near_slots)
        )
        grad_q, grad_k, grad_v = tile_grads(
            query_heads[head_index],
            grad_heads[head_index],
            norm_heads[head_index],
            delta_heads[head_index],
            key_rows,
            value_rows,
            near_keep,
        )
        dq_parts.append(grad_q.reshape(row_count, HEAD_DIM))
        glob_dk_parts.append(jnp.sum(grad_k[:, :GLOB], axis=0))
        glob_dv_parts.append(jnp.sum(grad_v[:, :GLOB], axis=0))
        dk_parts.append(add_tiles(near_picker, grad_k[:, GLOB:], ext_blocks))
        dv_parts.append(add_tiles(near_picker, grad_v[:, GLOB:], ext_blocks))
    query_side = jnp.concatenate(dq_parts, axis=1)
    near_side = jnp.stack([jnp.concatenate(dk_parts, axis=1), jnp.concatenate(dv_parts, axis=1)])
    own_grads = near_side[:, BLOCK : BLOCK + row_count]
    for shift_by in (-1, 1):
        rim_piece = near_side[:, :BLOCK] if shift_by < 0 else near_side[:, BLOCK + row_count :]
        arrived = passed_along(rim_piece, "ctx", shift_by)
        if shift_by < 0:
            own_grads = own_grads.at[:, row_count - BLOCK :].add(arrived)
        else:
            own_grads = own_grads.at[:, :BLOCK].add(arrived)
    full_keep = jnp.ones((block_count, BLOCK), jnp.float32)
    all_hit = jnp.ones((block_count, 1), bool)
    own_pair = jnp.stack([keys, values])
    for round_index in range(RAND):
        hop = (round_index + 1) * group_count // (RAND + 1)
        fetched = shifted(own_pair, "ctx", -hop)
        target_first = (my_group + hop) % group_count * block_count
        far_slots = jnp.clip(own_lists[:, 3 + round_index] - target_first, 0, block_count - 1)[
            :, None
        ]
        far_picker = tile_picker(far_slots, all_hit, block_count)
        far_dq, far_dk, far_dv = ([], [], [])
        for head_index in range(head_count):
            far_keys = gather_tiles(head_blocks(fetched[0], head_index, block_count), far_slots)
            far_values = gather_tiles(head_blocks(fetched[1], head_index, block_count), far_slots)
            grad_q, grad_k, grad_v = tile_grads(
                query_heads[head_index],
                grad_heads[head_index],
                norm_heads[head_index],
                delta_heads[head_index],
                far_keys,
                far_values,
                full_keep,
            )
            far_dq.append(grad_q.reshape(row_count, HEAD_DIM))
            far_dk.append(add_tiles(far_picker, grad_k, block_count))
            far_dv.append(add_tiles(far_picker, grad_v, block_count))
        query_side = query_side + jnp.concatenate(far_dq, axis=1)
        far_pair = jnp.stack([jnp.concatenate(far_dk, axis=1), jnp.concatenate(far_dv, axis=1)])
        own_grads = own_grads + shifted(far_pair, "ctx", hop)
    glob_pair = jnp.stack(
        [jnp.concatenate(glob_dk_parts, axis=1), jnp.concatenate(glob_dv_parts, axis=1)]
    )
    summed_all = lax.psum(glob_pair, "ctx")
    share_rows = GLOB // group_count
    own_share = lax.dynamic_slice_in_dim(summed_all, my_group * share_rows, share_rows, 1)
    return (
        query_side.astype(jnp.bfloat16),
        own_grads[0].astype(jnp.bfloat16),
        own_grads[1].astype(jnp.bfloat16),
        own_share[0],
        own_share[1],
    )


K_IN, Q_IN, V_IN, G_IN, S_IN = range(5)
Q_OUT, K_OUT, V_OUT, GLOB_OUT = range(4)
CLASSES = 2
CONTRACT_LAST = (((1,), (1,)), ((), ()))


def start_order(peers):
    half = peers // 2
    return [half] + [half + sign * by for by in range(1, half) for sign in (-1, 1)]


def head_kernel(
    peers,
    q_hbm,
    k_hbm,
    v_hbm,
    o_hbm,
    g_hbm,
    norm_hbm,
    gk_hbm,
    gv_hbm,
    dq_out,
    dk_out,
    dv_out,
    glob_out,
    q_all,
    k_all,
    v_all,
    g_all,
    stat_all,
    g_own,
    o_own,
    norm_own,
    stat_own,
    dq_acc,
    dk_acc,
    dv_acc,
    dq_low,
    dk_low,
    dv_low,
    glob_low,
    load_sem,
    spread_send,
    spread_recv,
    in_send,
    in_recv,
    out_send,
    out_recv,
):
    me = lax.axis_index("ctx")
    my_head = lax.axis_index("head")
    head_peers = lax.axis_size("head")
    members = peers // CLASSES
    class_rows = members * BLOCK
    span = class_rows + GLOB
    share = GLOB // peers
    width = q_hbm.shape[1]
    part_rows = g_hbm.shape[0]
    order = start_order(peers)

    def cols(index):
        return pl.ds(pl.multiple_of(index * HEAD_DIM, HEAD_DIM), HEAD_DIM)

    def query_rows(index):
        at = (index % CLASSES) * class_rows + (index // CLASSES) * BLOCK
        return pl.ds(at if isinstance(at, int) else pl.multiple_of(at, BLOCK), BLOCK)

    def key_rows(index):
        at = (index % CLASSES) * span + (index // CLASSES) * BLOCK
        return pl.ds(at if isinstance(at, int) else pl.multiple_of(at, BLOCK), BLOCK)

    def remote(src, dst, send, recv, **device):
        return pltpu.make_async_remote_copy(
            src_ref=src,
            dst_ref=dst,
            send_sem=send,
            recv_sem=recv,
            device_id=device,
            device_id_type=pl.DeviceIdType.MESH,
        )

    loads = [
        pltpu.make_async_copy(o_hbm, o_own, load_sem.at[0]),
        pltpu.make_async_copy(norm_hbm, norm_own, load_sem.at[1]),
        pltpu.make_async_copy(
            gk_hbm.at[:, cols(me)], k_all.at[pl.ds(class_rows, GLOB)], load_sem.at[2]
        ),
        pltpu.make_async_copy(
            gv_hbm.at[:, cols(me)], v_all.at[pl.ds(class_rows, GLOB)], load_sem.at[3]
        ),
    ]
    for load in loads:
        load.start()

    barrier = pltpu.get_barrier_semaphore()
    for by in range(1, head_peers):
        pl.semaphore_signal(
            barrier,
            inc=1,
            device_id={"head": lax.rem(my_head + by, head_peers)},
            device_id_type=pl.DeviceIdType.MESH,
        )
    for by in order:
        pl.semaphore_signal(
            barrier,
            inc=1,
            device_id={"ctx": lax.rem(me + by, peers)},
            device_id_type=pl.DeviceIdType.MESH,
        )
    pl.semaphore_wait(barrier, head_peers - 1 + peers - 1)

    sends = []

    def my_part():
        return pl.ds(pl.multiple_of(my_head * part_rows, part_rows), part_rows)

    def wide(index):
        return pl.ds(pl.multiple_of(index * width, width), width)

    for by in range(1, head_peers):
        to = lax.rem(my_head + by, head_peers)
        copy = remote(
            g_hbm.at[:, wide(to)],
            g_own.at[my_part()],
            spread_send.at[by],
            spread_recv.at[my_head],
            head=to,
        )
        copy.start()
        sends.append(copy)
    pltpu.make_async_copy(
        g_hbm.at[:, wide(my_head)], g_own.at[my_part()], spread_recv.at[my_head]
    ).start()

    def spread_in(kind, src, dst, rows):
        for by in order:
            to = lax.rem(me + by, peers)
            copy = remote(
                src.at[:, cols(to)],
                dst.at[rows(me)],
                in_send.at[kind, by],
                in_recv.at[kind, me],
                ctx=to,
            )
            copy.start()
            sends.append(copy)
        pltpu.make_async_copy(
            src.at[:, cols(me)], dst.at[rows(me)], in_recv.at[kind, me]
        ).start()

    def arrived(kind, dst, rows):
        for index in range(peers):
            place = dst.at[rows(index)]
            pltpu.make_async_copy(place, place, in_recv.at[kind, index]).wait()

    spread_in(K_IN, k_hbm, k_all, key_rows)
    spread_in(Q_IN, q_hbm, q_all, query_rows)
    spread_in(V_IN, v_hbm, v_all, key_rows)

    loads[0].wait()
    loads[1].wait()
    for index in range(head_peers):
        place = g_own.at[pl.ds(index * part_rows, part_rows)]
        pltpu.make_async_copy(place, place, spread_recv.at[index]).wait()
    spread_in(G_IN, g_own, g_all, query_rows)
    ones = jnp.ones((8, HEAD_DIM), jnp.float32)
    first = lax.broadcasted_iota(jnp.int32, (8, BLOCK), 0) == 0
    for index in range(peers):
        lanes = pl.ds(index * HEAD_DIM, HEAD_DIM)
        product = g_own[:, lanes].astype(jnp.float32) * o_own[:, lanes].astype(jnp.float32)
        delta = lax.dot_general(
            ones,
            product,
            CONTRACT_LAST,
            precision=lax.Precision.HIGHEST,
            preferred_element_type=jnp.float32,
        )
        norm = jnp.broadcast_to(norm_own[pl.ds(index, 1), :], (8, BLOCK))
        stat_own[index] = jnp.where(first, norm * LOG2E, delta)
    for by in order:
        to = lax.rem(me + by, peers)
        copy = remote(
            stat_own.at[to], stat_all.at[me], in_send.at[S_IN, by], in_recv.at[S_IN, me], ctx=to
        )
        copy.start()
        sends.append(copy)
    pltpu.make_async_copy(stat_own.at[me], stat_all.at[me], in_recv.at[S_IN, me]).start()

    loads[2].wait()
    loads[3].wait()
    arrived(K_IN, k_all, key_rows)
    arrived(Q_IN, q_all, query_rows)
    arrived(V_IN, v_all, key_rows)
    arrived(G_IN, g_all, query_rows)
    for index in range(peers):
        place = stat_all.at[index]
        pltpu.make_async_copy(place, place, in_recv.at[S_IN, index]).wait()

    scale = HEAD_DIM**-0.5

    def dot(left, right):
        return jnp.dot(left, right, preferred_element_type=jnp.float32)

    def visit(blocks, key_at, key_count):
        first_rows = query_rows(blocks[0]).start
        rows = pl.ds(first_rows, len(blocks) * BLOCK)
        keys = pl.ds(key_at, key_count)
        norm = jnp.concatenate([stat_all[block, 0:1, :] for block in blocks], axis=1)
        delta = jnp.concatenate([stat_all[block, 1:2, :] for block in blocks], axis=1)
        scores = lax.dot_general(
            k_all[keys, :], q_all[rows, :], CONTRACT_LAST, preferred_element_type=jnp.float32
        )
        weights = jnp.exp2(scores * (scale * LOG2E) - norm)
        dprobs = lax.dot_general(
            v_all[keys, :], g_all[rows, :], CONTRACT_LAST, preferred_element_type=jnp.float32
        )
        dscores = (weights * (dprobs - delta)).astype(jnp.bfloat16)
        grad_v = dot(weights.astype(jnp.bfloat16), g_all[rows, :])
        grad_k = dot(dscores, q_all[rows, :])
        grad_q = dot(k_all[keys, :].T, dscores)
        return rows, keys, grad_q, grad_k, grad_v

    dk_acc[...] = jnp.zeros_like(dk_acc)
    dv_acc[...] = jnp.zeros_like(dv_acc)

    for block in range(peers):
        near = [at for at in (block - 1, block + 1) if 0 <= at < peers]
        rows, keys, grad_q, grad_k, grad_v = visit(
            [block], key_rows(near[0]).start, len(near) * BLOCK
        )
        dq_acc[:, rows] = grad_q
        dk_acc[keys, :] += grad_k
        dv_acc[keys, :] += grad_v

    pair = 2

    def put(kind, src, dst, rows, block):
        @pl.when(me == block)
        def _():
            pltpu.make_async_copy(
                src.at[rows(block)], dst.at[:, cols(me)], out_recv.at[kind, me]
            ).start()

        @pl.when(me != block)
        def _():
            remote(
                src.at[rows(block)],
                dst.at[:, cols(me)],
                out_send.at[kind, block],
                out_recv.at[kind, me],
                ctx=block,
            ).start()

    for part in range(CLASSES):
        for at in range(0, members, pair):
            blocks = [part + CLASSES * (at + step) for step in range(pair)]
            rows, keys, grad_q, grad_k, grad_v = visit(blocks, part * class_rows, span)
            dq_acc[:, rows] += grad_q
            dk_acc[keys, :] += grad_k
            dv_acc[keys, :] += grad_v
            dq_low[rows, :] = (dq_acc[:, rows] * scale).T.astype(jnp.bfloat16)
        own = pl.ds(part * span, class_rows)
        dk_low[own, :] = (dk_acc[own, :] * scale).astype(jnp.bfloat16)
        dv_low[own, :] = dv_acc[own, :].astype(jnp.bfloat16)
        for kind, src, dst, rows in (
            (Q_OUT, dq_low, dq_out, query_rows),
            (K_OUT, dk_low, dk_out, key_rows),
            (V_OUT, dv_low, dv_out, key_rows),
        ):
            for at in range(members):
                put(kind, src, dst, rows, part + CLASSES * at)

    middle = pl.ds(class_rows, GLOB)
    glob_low[0] = (dk_acc[middle, :] * scale).astype(jnp.bfloat16)
    glob_low[1] = dv_acc[middle, :].astype(jnp.bfloat16)

    def share_of(index):
        return glob_low.at[:, pl.ds(pl.multiple_of(index * share, share), share), :]

    for by in order:
        to = lax.rem(me + by, peers)
        copy = remote(
            share_of(to),
            glob_out.at[:, :, cols(me)],
            out_send.at[GLOB_OUT, to],
            out_recv.at[GLOB_OUT, me],
            ctx=to,
        )
        copy.start()
        sends.append(copy)
    pltpu.make_async_copy(
        share_of(me), glob_out.at[:, :, cols(me)], out_recv.at[GLOB_OUT, me]
    ).start()

    for copy in sends:
        copy.wait_send()
    for by in order:
        to = lax.rem(me + by, peers)
        for kind, src, rows in (
            (Q_OUT, dq_low, query_rows),
            (K_OUT, dk_low, key_rows),
            (V_OUT, dv_low, key_rows),
        ):
            place = src.at[rows(to)]
            pltpu.make_async_copy(place, place, out_send.at[kind, to]).wait()
    for index in range(peers):
        for kind, dst in ((Q_OUT, dq_out), (K_OUT, dk_out), (V_OUT, dv_out)):
            place = dst.at[:, cols(index)]
            pltpu.make_async_copy(place, place, out_recv.at[kind, index]).wait()
        place = glob_out.at[:, :, cols(index)]
        pltpu.make_async_copy(place, place, out_recv.at[GLOB_OUT, index]).wait()


def whole_heads(peers, queries, keys, values, outputs, grad_out, log_norm, glob_keys, glob_values):
    row_count, col_count = queries.shape
    tokens = peers * BLOCK
    low, full = jnp.bfloat16, jnp.float32
    head_peers = lax.axis_size("head")
    result = jax.ShapeDtypeStruct((row_count, col_count), low)
    scores = tokens * (GLOB + (RAND + 3) * BLOCK)
    dq, dk, dv, glob = pl.pallas_call(
        functools.partial(head_kernel, peers),
        out_shape=(
            result,
            result,
            result,
            jax.ShapeDtypeStruct((2, GLOB // peers, col_count), low),
        ),
        in_specs=[pl.BlockSpec(memory_space=pl.ANY)] * 8,
        out_specs=[pl.BlockSpec(memory_space=pl.ANY)] * 4,
        scratch_shapes=[
            pltpu.VMEM((tokens, HEAD_DIM), low),
            pltpu.VMEM((tokens + GLOB, HEAD_DIM), low),
            pltpu.VMEM((tokens + GLOB, HEAD_DIM), low),
            pltpu.VMEM((tokens, HEAD_DIM), low),
            pltpu.VMEM((peers, 8, BLOCK), full),
            pltpu.VMEM((row_count, col_count), low),
            pltpu.VMEM((row_count, col_count), low),
            pltpu.VMEM(log_norm.shape, full),
            pltpu.VMEM((peers, 8, BLOCK), full),
            pltpu.VMEM((HEAD_DIM, tokens), full),
            pltpu.VMEM((tokens + GLOB, HEAD_DIM), full),
            pltpu.VMEM((tokens + GLOB, HEAD_DIM), full),
            pltpu.VMEM((tokens, HEAD_DIM), low),
            pltpu.VMEM((tokens + GLOB, HEAD_DIM), low),
            pltpu.VMEM((tokens + GLOB, HEAD_DIM), low),
            pltpu.VMEM((2, GLOB, HEAD_DIM), low),
            pltpu.SemaphoreType.DMA((4,)),
            pltpu.SemaphoreType.DMA((head_peers,)),
            pltpu.SemaphoreType.DMA((head_peers,)),
            pltpu.SemaphoreType.DMA((5, peers)),
            pltpu.SemaphoreType.DMA((5, peers)),
            pltpu.SemaphoreType.DMA((4, peers)),
            pltpu.SemaphoreType.DMA((4, peers)),
        ],
        compiler_params=pltpu.CompilerParams(
            collective_id=0, has_side_effects=True, vmem_limit_bytes=48 * 1024 * 1024
        ),
        cost_estimate=pl.CostEstimate(
            flops=10 * scores * HEAD_DIM, bytes_accessed=4 * 1024 * 1024, transcendentals=scores
        ),
        name="whole_heads",
    )(queries, keys, values, outputs, grad_out, log_norm, glob_keys, glob_values)
    return dq, dk, dv, glob[0].astype(full), glob[1].astype(full)


def program(mesh):
    peers = mesh.shape["ctx"]

    def body(queries, keys, values, outputs, grad_out, log_norm, glob_keys, glob_values, key_lists):
        row_count, col_count = queries.shape
        one_head_each = (
            row_count == BLOCK
            and col_count == peers * HEAD_DIM
            and peers == CLASSES * (RAND + 1)
            and GLOB % (16 * peers) == 0
        )
        if one_head_each:
            return whole_heads(
                peers, queries, keys, values, outputs, grad_out, log_norm, glob_keys, glob_values
            )
        return shards(
            queries, keys, values, outputs, grad_out, log_norm, glob_keys, glob_values, key_lists
        )

    return body


def solution(mesh):
    in_specs = (
        P("ctx", "head"),
        P("ctx", "head"),
        P("ctx", "head"),
        P("ctx", "head"),
        P(("ctx", "head"), None),
        P("head", "ctx"),
        P(None, "head"),
        P(None, "head"),
        P(),
    )
    out_specs = (
        P("ctx", "head"),
        P("ctx", "head"),
        P("ctx", "head"),
        P("ctx", "head"),
        P("ctx", "head"),
    )
    return jax.shard_map(program(mesh), mesh=mesh, in_specs=in_specs, out_specs=out_specs, check_vma=False)
```

```python
import functools
import math

import jax
import jax.numpy as jnp
from jax import lax
from jax.experimental import pallas as pl
from jax.experimental.pallas import tpu as pltpu
from jax.sharding import PartitionSpec as P

HEAD_DIM = 128
BLOCK = 128
GLOB = 256
RAND = 3
LOG2E = math.log2(math.e)


def extended_2(cells, sides, width):
    for axis, dim in sides:
        count = lax.axis_size(axis)
        ends = count - 1
        head = lax.slice_in_dim(cells, 0, width, axis=dim)
        tail = lax.slice_in_dim(cells, cells.shape[dim] - width, cells.shape[dim], axis=dim)
        cells = jnp.concatenate(
            [
                lax.ppermute(tail, axis, [(i, (i + 1) % count) for i in range(ends)]),
                cells,
                lax.ppermute(head, axis, [((i + 1) % count, i) for i in range(ends)]),
            ],
            axis=dim,
        )
    return cells


def passed_along(value, axis, by):
    peers = lax.axis_size(axis)
    pairs = [(i, i + by) for i in range(peers) if 0 <= i + by < peers]
    return lax.ppermute(value, axis, pairs)


def shifted(value, axis, by):
    peers = lax.axis_size(axis)
    return lax.ppermute(value, axis, [(i, (i + by) % peers) for i in range(peers)])


def tile_grads(query_rows, grad_rows, norm_rows, delta_rows, key_rows, value_rows, keep_mask):
    att_scale = HEAD_DIM ** (-0.5)
    scores = (
        jnp.einsum("nbd,nkd->nbk", query_rows, key_rows, preferred_element_type=jnp.float32)
        * att_scale
    )
    weights = jnp.exp(scores - norm_rows[:, :, None]) * keep_mask[:, None, :]
    dprobs = jnp.einsum("nbd,nkd->nbk", grad_rows, value_rows, preferred_element_type=jnp.float32)
    dscores = weights * (dprobs - delta_rows[:, :, None])
    weights_low = weights.astype(jnp.bfloat16)
    dscores_low = dscores.astype(jnp.bfloat16)
    grad_values = jnp.einsum(
        "nbk,nbd->nkd", weights_low, grad_rows, preferred_element_type=jnp.float32
    )
    grad_keys = (
        jnp.einsum("nbk,nbd->nkd", dscores_low, query_rows, preferred_element_type=jnp.float32)
        * att_scale
    )
    grad_queries = (
        jnp.einsum("nbk,nkd->nbd", dscores_low, key_rows, preferred_element_type=jnp.float32)
        * att_scale
    )
    return (grad_queries, grad_keys, grad_values)


def head_cols(source, head_index):
    return source[:, head_index * HEAD_DIM : (head_index + 1) * HEAD_DIM]


def head_blocks(source, head_index, num_blocks):
    return head_cols(source, head_index).reshape(num_blocks, BLOCK, HEAD_DIM)


def gather_tiles(tile_rows, slot_ids):
    picked = jnp.take(tile_rows, slot_ids, axis=0)
    return picked.reshape(slot_ids.shape[0], slot_ids.shape[1] * BLOCK, HEAD_DIM)


def tile_picker(slot_ids, hit_mask, num_blocks):
    one_hot = (
        slot_ids[:, :, None] == jnp.arange(num_blocks, dtype=jnp.int32)[None, None, :]
    ) & hit_mask[:, :, None]
    return one_hot.astype(jnp.float32)


def add_tiles(picker, flat_grads, num_blocks):
    tiled_grads = flat_grads.reshape(picker.shape[0], picker.shape[1], BLOCK, HEAD_DIM)
    summed = jnp.einsum("nle,nlbd->ebd", picker, tiled_grads, precision=lax.Precision.HIGHEST)
    return summed.reshape(num_blocks * BLOCK, HEAD_DIM)


def tile_keep(hit_mask, extra_cols):
    tile_cols = jnp.repeat(hit_mask.astype(jnp.float32), BLOCK, axis=1)
    return jnp.concatenate(
        [jnp.ones((hit_mask.shape[0], extra_cols), jnp.float32), tile_cols], axis=1
    )


def with_glob(glob_rows, tile_rows):
    spread = glob_rows[None]
    return jnp.concatenate([spread, tile_rows], axis=1)


def shards(queries, keys, values, outputs, grad_out, log_norm, glob_keys, glob_values, key_lists):
    row_count, col_count = queries.shape
    head_count = col_count // HEAD_DIM
    block_count = row_count // BLOCK
    group_count = lax.axis_size("ctx")
    my_group = lax.axis_index("ctx")
    first_block = my_group * block_count
    incoming = lax.all_to_all(grad_out, "head", split_axis=1, concat_axis=0, tiled=True)
    row_delta = jnp.sum(
        (incoming.astype(jnp.float32) * outputs.astype(jnp.float32)).reshape(
            row_count, head_count, HEAD_DIM
        ),
        axis=2,
    ).T
    own_lists = lax.dynamic_slice_in_dim(key_lists, first_block, block_count, 0)
    query_heads = [
        head_blocks(queries, head_index, block_count) for head_index in range(head_count)
    ]
    grad_heads = [
        head_blocks(incoming, head_index, block_count) for head_index in range(head_count)
    ]
    norm_heads = [
        log_norm[head_index].reshape(block_count, BLOCK) for head_index in range(head_count)
    ]
    delta_heads = [
        row_delta[head_index].reshape(block_count, BLOCK) for head_index in range(head_count)
    ]
    extended = extended_2(jnp.stack([keys, values]), (("ctx", 1),), BLOCK)
    ext_blocks = block_count + 2
    near_lists = own_lists[:, :3]
    near_live = near_lists >= 0
    near_slots = jnp.clip(near_lists - (first_block - 1), 0, ext_blocks - 1)
    near_keep = tile_keep(near_live, GLOB)
    near_picker = tile_picker(near_slots, near_live, ext_blocks)
    dq_parts, dk_parts, dv_parts, glob_dk_parts, glob_dv_parts = ([], [], [], [], [])
    for head_index in range(head_count):
        ext_keys = head_blocks(extended[0], head_index, ext_blocks)
        ext_values = head_blocks(extended[1], head_index, ext_blocks)
        key_rows = with_glob(head_cols(glob_keys, head_index), gather_tiles(ext_keys, near_slots))
        value_rows = with_glob(
            head_cols(glob_values, head_index), gather_tiles(ext_values, near_slots)
        )
        grad_q, grad_k, grad_v = tile_grads(
            query_heads[head_index],
            grad_heads[head_index],
            norm_heads[head_index],
            delta_heads[head_index],
            key_rows,
            value_rows,
            near_keep,
        )
        dq_parts.append(grad_q.reshape(row_count, HEAD_DIM))
        glob_dk_parts.append(jnp.sum(grad_k[:, :GLOB], axis=0))
        glob_dv_parts.append(jnp.sum(grad_v[:, :GLOB], axis=0))
        dk_parts.append(add_tiles(near_picker, grad_k[:, GLOB:], ext_blocks))
        dv_parts.append(add_tiles(near_picker, grad_v[:, GLOB:], ext_blocks))
    query_side = jnp.concatenate(dq_parts, axis=1)
    near_side = jnp.stack([jnp.concatenate(dk_parts, axis=1), jnp.concatenate(dv_parts, axis=1)])
    own_grads = near_side[:, BLOCK : BLOCK + row_count]
    for shift_by in (-1, 1):
        rim_piece = near_side[:, :BLOCK] if shift_by < 0 else near_side[:, BLOCK + row_count :]
        arrived = passed_along(rim_piece, "ctx", shift_by)
        if shift_by < 0:
            own_grads = own_grads.at[:, row_count - BLOCK :].add(arrived)
        else:
            own_grads = own_grads.at[:, :BLOCK].add(arrived)
    full_keep = jnp.ones((block_count, BLOCK), jnp.float32)
    all_hit = jnp.ones((block_count, 1), bool)
    own_pair = jnp.stack([keys, values])
    for round_index in range(RAND):
        hop = (round_index + 1) * group_count // (RAND + 1)
        fetched = shifted(own_pair, "ctx", -hop)
        target_first = (my_group + hop) % group_count * block_count
        far_slots = jnp.clip(own_lists[:, 3 + round_index] - target_first, 0, block_count - 1)[
            :, None
        ]
        far_picker = tile_picker(far_slots, all_hit, block_count)
        far_dq, far_dk, far_dv = ([], [], [])
        for head_index in range(head_count):
            far_keys = gather_tiles(head_blocks(fetched[0], head_index, block_count), far_slots)
            far_values = gather_tiles(head_blocks(fetched[1], head_index, block_count), far_slots)
            grad_q, grad_k, grad_v = tile_grads(
                query_heads[head_index],
                grad_heads[head_index],
                norm_heads[head_index],
                delta_heads[head_index],
                far_keys,
                far_values,
                full_keep,
            )
            far_dq.append(grad_q.reshape(row_count, HEAD_DIM))
            far_dk.append(add_tiles(far_picker, grad_k, block_count))
            far_dv.append(add_tiles(far_picker, grad_v, block_count))
        query_side = query_side + jnp.concatenate(far_dq, axis=1)
        far_pair = jnp.stack([jnp.concatenate(far_dk, axis=1), jnp.concatenate(far_dv, axis=1)])
        own_grads = own_grads + shifted(far_pair, "ctx", hop)
    glob_pair = jnp.stack(
        [jnp.concatenate(glob_dk_parts, axis=1), jnp.concatenate(glob_dv_parts, axis=1)]
    )
    summed_all = lax.psum(glob_pair, "ctx")
    share_rows = GLOB // group_count
    own_share = lax.dynamic_slice_in_dim(summed_all, my_group * share_rows, share_rows, 1)
    return (
        query_side.astype(jnp.bfloat16),
        own_grads[0].astype(jnp.bfloat16),
        own_grads[1].astype(jnp.bfloat16),
        own_share[0],
        own_share[1],
    )


HALVES = 2
HALF = BLOCK // HALVES
K_IN, V_IN, S_IN, Q_IN, G_IN = 0, 1, 2, 3, 3 + HALVES
IN_KINDS = 3 + 2 * HALVES
K_OUT, V_OUT, GLOB_OUT, Q_OUT = 0, 1, 2, 3
OUT_KINDS = 3 + HALVES
CLASSES = 2
CONTRACT_LAST = (((1,), (1,)), ((), ()))


def start_order(peers):
    half = peers // 2
    return [half] + [half + sign * by for by in range(1, half) for sign in (-1, 1)]


def head_kernel(
    peers,
    q_hbm,
    k_hbm,
    v_hbm,
    o_hbm,
    g_hbm,
    norm_hbm,
    gk_hbm,
    gv_hbm,
    dq_out,
    dk_out,
    dv_out,
    glob_out,
    q_all,
    k_all,
    v_all,
    g_all,
    stat_all,
    g_own,
    o_own,
    norm_own,
    stat_own,
    kt_all,
    dq_acc,
    dk_acc,
    dv_acc,
    dq_low,
    dk_low,
    dv_low,
    glob_low,
    load_sem,
    spread_send,
    spread_recv,
    in_send,
    in_recv,
    out_send,
    out_recv,
):
    me = lax.axis_index("ctx")
    my_head = lax.axis_index("head")
    head_peers = lax.axis_size("head")
    members = peers // CLASSES
    class_rows = members * BLOCK
    span = class_rows + GLOB
    share = GLOB // peers
    width = q_hbm.shape[1]
    part_rows = g_hbm.shape[0]
    order = start_order(peers)

    def cols(index):
        return pl.ds(pl.multiple_of(index * HEAD_DIM, HEAD_DIM), HEAD_DIM)

    def query_rows(half, index):
        at = half * members * CLASSES * HALF + (index % CLASSES) * members * HALF + (index // CLASSES) * HALF
        return pl.ds(at if isinstance(at, int) else pl.multiple_of(at, HALF), HALF)

    def half_rows(half):
        return pl.ds(half * HALF, HALF)

    def key_rows(index):
        at = (index % CLASSES) * span + (index // CLASSES) * BLOCK
        return pl.ds(at if isinstance(at, int) else pl.multiple_of(at, BLOCK), BLOCK)

    def remote(src, dst, send, recv, **device):
        return pltpu.make_async_remote_copy(
            src_ref=src,
            dst_ref=dst,
            send_sem=send,
            recv_sem=recv,
            device_id=device,
            device_id_type=pl.DeviceIdType.MESH,
        )

    loads = [
        pltpu.make_async_copy(o_hbm, o_own, load_sem.at[0]),
        pltpu.make_async_copy(norm_hbm, norm_own, load_sem.at[1]),
        pltpu.make_async_copy(
            gk_hbm.at[:, cols(me)], k_all.at[pl.ds(class_rows, GLOB)], load_sem.at[2]
        ),
        pltpu.make_async_copy(
            gv_hbm.at[:, cols(me)], v_all.at[pl.ds(class_rows, GLOB)], load_sem.at[3]
        ),
    ]
    for load in loads:
        load.start()

    barrier = pltpu.get_barrier_semaphore()
    for by in range(1, head_peers):
        pl.semaphore_signal(
            barrier,
            inc=1,
            device_id={"head": lax.rem(my_head + by, head_peers)},
            device_id_type=pl.DeviceIdType.MESH,
        )
    for by in order:
        pl.semaphore_signal(
            barrier,
            inc=1,
            device_id={"ctx": lax.rem(me + by, peers)},
            device_id_type=pl.DeviceIdType.MESH,
        )
    pl.semaphore_wait(barrier, head_peers - 1 + peers - 1)

    sends = []

    def my_part():
        return pl.ds(pl.multiple_of(my_head * part_rows, part_rows), part_rows)

    def wide(index):
        return pl.ds(pl.multiple_of(index * width, width), width)

    for by in range(1, head_peers):
        to = lax.rem(my_head + by, head_peers)
        copy = remote(
            g_hbm.at[:, wide(to)],
            g_own.at[my_part()],
            spread_send.at[by],
            spread_recv.at[my_head],
            head=to,
        )
        copy.start()
        sends.append(copy)
    pltpu.make_async_copy(
        g_hbm.at[:, wide(my_head)], g_own.at[my_part()], spread_recv.at[my_head]
    ).start()

    def spread_in(kind, src, dst, from_rows, rows):
        for by in order:
            to = lax.rem(me + by, peers)
            copy = remote(
                src.at[from_rows, cols(to)],
                dst.at[rows(me)],
                in_send.at[kind, by],
                in_recv.at[kind, me],
                ctx=to,
            )
            copy.start()
            sends.append(copy)
        pltpu.make_async_copy(
            src.at[from_rows, cols(me)], dst.at[rows(me)], in_recv.at[kind, me]
        ).start()

    def arrived(kind, dst, rows):
        for index in range(peers):
            place = dst.at[rows(index)]
            pltpu.make_async_copy(place, place, in_recv.at[kind, index]).wait()

    places = [functools.partial(query_rows, half) for half in range(HALVES)]
    all_rows = pl.ds(0, BLOCK)
    spread_in(K_IN, k_hbm, k_all, all_rows, key_rows)
    spread_in(Q_IN, q_hbm, q_all, half_rows(0), places[0])
    spread_in(V_IN, v_hbm, v_all, all_rows, key_rows)

    loads[0].wait()
    loads[1].wait()
    for index in range(head_peers):
        place = g_own.at[pl.ds(index * part_rows, part_rows)]
        pltpu.make_async_copy(place, place, spread_recv.at[index]).wait()
    spread_in(G_IN, g_own, g_all, half_rows(0), places[0])
    ones = jnp.ones((8, HEAD_DIM), jnp.float32)
    first = lax.broadcasted_iota(jnp.int32, (8, BLOCK), 0) == 0
    for index in range(peers):
        lanes = pl.ds(index * HEAD_DIM, HEAD_DIM)
        product = g_own[:, lanes].astype(jnp.float32) * o_own[:, lanes].astype(jnp.float32)
        delta = lax.dot_general(
            ones,
            product,
            CONTRACT_LAST,
            precision=lax.Precision.HIGHEST,
            preferred_element_type=jnp.float32,
        )
        norm = jnp.broadcast_to(norm_own[pl.ds(index, 1), :], (8, BLOCK))
        stat_own[index] = jnp.where(first, norm * LOG2E, delta)
    for by in order:
        to = lax.rem(me + by, peers)
        copy = remote(
            stat_own.at[to], stat_all.at[me], in_send.at[S_IN, by], in_recv.at[S_IN, me], ctx=to
        )
        copy.start()
        sends.append(copy)
    pltpu.make_async_copy(stat_own.at[me], stat_all.at[me], in_recv.at[S_IN, me]).start()

    for half in range(1, HALVES):
        spread_in(Q_IN + half, q_hbm, q_all, half_rows(half), places[half])
        spread_in(G_IN + half, g_own, g_all, half_rows(half), places[half])

    scale = HEAD_DIM**-0.5

    def dot(left, right):
        return jnp.dot(left, right, preferred_element_type=jnp.float32)

    def visit(half, blocks, key_at, key_count, keep):
        rows = pl.ds(query_rows(half, blocks[0]).start, len(blocks) * HALF)
        keys = pl.ds(key_at, key_count)
        norm, delta = (
            jnp.concatenate(
                [stat_all[block, row : row + 1, half * HALF : (half + 1) * HALF] for block in blocks],
                axis=1,
            )
            for row in range(2)
        )
        scores = lax.dot_general(
            k_all[keys, :], q_all[rows, :], CONTRACT_LAST, preferred_element_type=jnp.float32
        )
        weights = jnp.exp2(scores * (scale * LOG2E) - norm)
        if keep is not None:
            weights = jnp.where(keep, weights, 0.0)
        dprobs = lax.dot_general(
            v_all[keys, :], g_all[rows, :], CONTRACT_LAST, preferred_element_type=jnp.float32
        )
        dscores = (weights * (dprobs - delta)).astype(jnp.bfloat16)
        dq_acc[:, rows] += dot(kt_all[:, keys], dscores)
        dk_acc[keys, :] += dot(dscores, q_all[rows, :])
        dv_acc[keys, :] += dot(weights.astype(jnp.bfloat16), g_all[rows, :])

    def visit_near(half, blocks):
        near = [at for at in range(blocks[0] - 1, blocks[-1] + 2, CLASSES) if 0 <= at < peers]
        shape = (len(near) * BLOCK, len(blocks) * HALF)
        key_block = near[0] + CLASSES * (lax.broadcasted_iota(jnp.int32, shape, 0) // BLOCK)
        query_block = blocks[0] + CLASSES * (lax.broadcasted_iota(jnp.int32, shape, 1) // HALF)
        keep = jnp.abs(key_block - query_block) == 1
        visit(half, blocks, key_rows(near[0]).start, len(near) * BLOCK, keep)

    def put(kind, src, dst, from_rows, to_rows, block):
        @pl.when(me == block)
        def _():
            pltpu.make_async_copy(
                src.at[from_rows], dst.at[to_rows, cols(me)], out_recv.at[kind, me]
            ).start()

        @pl.when(me != block)
        def _():
            remote(
                src.at[from_rows],
                dst.at[to_rows, cols(me)],
                out_send.at[kind, block],
                out_recv.at[kind, me],
                ctx=block,
            ).start()

    dk_acc[...] = jnp.zeros_like(dk_acc)
    dv_acc[...] = jnp.zeros_like(dv_acc)
    dq_acc[...] = jnp.zeros_like(dq_acc)

    loads[2].wait()
    loads[3].wait()
    arrived(K_IN, k_all, key_rows)
    kt_all[...] = k_all[...].T
    arrived(V_IN, v_all, key_rows)
    for index in range(peers):
        place = stat_all.at[index]
        pltpu.make_async_copy(place, place, in_recv.at[S_IN, index]).wait()

    pair = 2
    for half in range(HALVES):
        arrived(Q_IN + half, q_all, places[half])
        arrived(G_IN + half, g_all, places[half])
        for part in range(CLASSES):
            for at in range(0, members, pair):
                visit_near(half, [part + CLASSES * (at + step) for step in range(pair)])
        for part in range(CLASSES):
            blocks = [part + CLASSES * at for at in range(members)]
            visit(half, blocks, part * class_rows, span, None)
            rows = pl.ds(query_rows(half, part).start, members * HALF)
            dq_low[rows, :] = (dq_acc[:, rows] * scale).T.astype(jnp.bfloat16)
            for block in blocks:
                put(Q_OUT + half, dq_low, dq_out, query_rows(half, block), half_rows(half), block)
            if half == HALVES - 1:
                own = pl.ds(part * span, class_rows)
                dk_low[own, :] = (dk_acc[own, :] * scale).astype(jnp.bfloat16)
                for block in blocks:
                    put(K_OUT, dk_low, dk_out, key_rows(block), all_rows, block)
                dv_low[own, :] = dv_acc[own, :].astype(jnp.bfloat16)
                for block in blocks:
                    put(V_OUT, dv_low, dv_out, key_rows(block), all_rows, block)

    middle = pl.ds(class_rows, GLOB)
    glob_low[0] = (dk_acc[middle, :] * scale).astype(jnp.bfloat16)
    glob_low[1] = dv_acc[middle, :].astype(jnp.bfloat16)

    def share_of(index):
        return glob_low.at[:, pl.ds(pl.multiple_of(index * share, share), share), :]

    for by in order:
        to = lax.rem(me + by, peers)
        copy = remote(
            share_of(to),
            glob_out.at[:, :, cols(me)],
            out_send.at[GLOB_OUT, to],
            out_recv.at[GLOB_OUT, me],
            ctx=to,
        )
        copy.start()
        sends.append(copy)
    pltpu.make_async_copy(
        share_of(me), glob_out.at[:, :, cols(me)], out_recv.at[GLOB_OUT, me]
    ).start()

    for copy in sends:
        copy.wait_send()
    halves = [(Q_OUT + half, dq_low, places[half]) for half in range(HALVES)]
    for by in order:
        to = lax.rem(me + by, peers)
        for kind, src, rows in [(K_OUT, dk_low, key_rows), (V_OUT, dv_low, key_rows)] + halves:
            place = src.at[rows(to)]
            pltpu.make_async_copy(place, place, out_send.at[kind, to]).wait()
    halves = [(Q_OUT + half, dq_out, half_rows(half)) for half in range(HALVES)]
    for index in range(peers):
        for kind, dst, rows in [(K_OUT, dk_out, all_rows), (V_OUT, dv_out, all_rows)] + halves:
            place = dst.at[rows, cols(index)]
            pltpu.make_async_copy(place, place, out_recv.at[kind, index]).wait()
        place = glob_out.at[:, :, cols(index)]
        pltpu.make_async_copy(place, place, out_recv.at[GLOB_OUT, index]).wait()


def finish_kernel(dq_in, dk_in, dv_in, glob_in, dq_out, dk_out, dv_out, gk_out, gv_out, wide, sem):
    copies = [
        pltpu.make_async_copy(src, dst, sem.at[at])
        for at, (src, dst) in enumerate(((dq_in, dq_out), (dk_in, dk_out), (dv_in, dv_out)))
    ]
    for copy in copies:
        copy.start()
    wide[...] = glob_in[...].astype(jnp.float32)
    for at, dst in enumerate((gk_out, gv_out)):
        copy = pltpu.make_async_copy(wide.at[at], dst, sem.at[3 + at])
        copy.start()
        copies.append(copy)
    for copy in copies:
        copy.wait()


def whole_heads(peers, queries, keys, values, outputs, grad_out, log_norm, glob_keys, glob_values):
    row_count, col_count = queries.shape
    tokens = peers * BLOCK
    low, full = jnp.bfloat16, jnp.float32
    head_peers = lax.axis_size("head")
    result = jax.ShapeDtypeStruct((row_count, col_count), low)
    scores = tokens * (GLOB + (RAND + 3) * BLOCK)
    dq, dk, dv, glob = pl.pallas_call(
        functools.partial(head_kernel, peers),
        out_shape=(
            result,
            result,
            result,
            jax.ShapeDtypeStruct((2, GLOB // peers, col_count), low),
        ),
        in_specs=[pl.BlockSpec(memory_space=pl.ANY)] * 8,
        out_specs=[pl.BlockSpec(memory_space=pl.ANY)] * 4,
        scratch_shapes=[
            pltpu.VMEM((tokens, HEAD_DIM), low),
            pltpu.VMEM((tokens + GLOB, HEAD_DIM), low),
            pltpu.VMEM((tokens + GLOB, HEAD_DIM), low),
            pltpu.VMEM((tokens, HEAD_DIM), low),
            pltpu.VMEM((peers, 8, BLOCK), full),
            pltpu.VMEM((row_count, col_count), low),
            pltpu.VMEM((row_count, col_count), low),
            pltpu.VMEM(log_norm.shape, full),
            pltpu.VMEM((peers, 8, BLOCK), full),
            pltpu.VMEM((HEAD_DIM, tokens + GLOB), low),
            pltpu.VMEM((HEAD_DIM, tokens), full),
            pltpu.VMEM((tokens + GLOB, HEAD_DIM), full),
            pltpu.VMEM((tokens + GLOB, HEAD_DIM), full),
            pltpu.VMEM((tokens, HEAD_DIM), low),
            pltpu.VMEM((tokens + GLOB, HEAD_DIM), low),
            pltpu.VMEM((tokens + GLOB, HEAD_DIM), low),
            pltpu.VMEM((2, GLOB, HEAD_DIM), low),
            pltpu.SemaphoreType.DMA((4,)),
            pltpu.SemaphoreType.DMA((head_peers,)),
            pltpu.SemaphoreType.DMA((head_peers,)),
            pltpu.SemaphoreType.DMA((IN_KINDS, peers)),
            pltpu.SemaphoreType.DMA((IN_KINDS, peers)),
            pltpu.SemaphoreType.DMA((OUT_KINDS, peers)),
            pltpu.SemaphoreType.DMA((OUT_KINDS, peers)),
        ],
        compiler_params=pltpu.CompilerParams(
            collective_id=0, has_side_effects=True, vmem_limit_bytes=64 * 1024 * 1024
        ),
        cost_estimate=pl.CostEstimate(
            flops=10 * scores * HEAD_DIM, bytes_accessed=4 * 1024 * 1024, transcendentals=scores
        ),
        name="whole_heads",
    )(queries, keys, values, outputs, grad_out, log_norm, glob_keys, glob_values)
    share = jax.ShapeDtypeStruct((GLOB // peers, col_count), full)
    hbm = pl.BlockSpec(memory_space=pltpu.HBM)
    return pl.pallas_call(
        finish_kernel,
        out_shape=(result, result, result, share, share),
        in_specs=[pl.BlockSpec(memory_space=pl.ANY)] * 3 + [pl.BlockSpec(memory_space=pltpu.VMEM)],
        out_specs=[hbm] * 5,
        scratch_shapes=[
            pltpu.VMEM((2, GLOB // peers, col_count), full),
            pltpu.SemaphoreType.DMA((5,)),
        ],
        compiler_params=pltpu.CompilerParams(vmem_limit_bytes=64 * 1024 * 1024),
        cost_estimate=pl.CostEstimate(
            flops=0, bytes_accessed=2 * 1024 * 1024, transcendentals=0
        ),
        name="finish",
    )(dq, dk, dv, glob)


def program(mesh):
    peers = mesh.shape["ctx"]

    def body(queries, keys, values, outputs, grad_out, log_norm, glob_keys, glob_values, key_lists):
        row_count, col_count = queries.shape
        one_head_each = (
            row_count == BLOCK
            and col_count == peers * HEAD_DIM
            and peers == CLASSES * (RAND + 1)
            and GLOB % (16 * peers) == 0
        )
        if one_head_each:
            return whole_heads(
                peers, queries, keys, values, outputs, grad_out, log_norm, glob_keys, glob_values
            )
        return shards(
            queries, keys, values, outputs, grad_out, log_norm, glob_keys, glob_values, key_lists
        )

    return body


def solution(mesh):
    in_specs = (
        P("ctx", "head"),
        P("ctx", "head"),
        P("ctx", "head"),
        P("ctx", "head"),
        P(("ctx", "head"), None),
        P("head", "ctx"),
        P(None, "head"),
        P(None, "head"),
        P(),
    )
    out_specs = (
        P("ctx", "head"),
        P("ctx", "head"),
        P("ctx", "head"),
        P("ctx", "head"),
        P("ctx", "head"),
    )
    return jax.shard_map(program(mesh), mesh=mesh, in_specs=in_specs, out_specs=out_specs, check_vma=False)
```

```python
import functools
import math

import jax
import jax.numpy as jnp
from jax import lax
from jax.experimental import pallas as pl
from jax.experimental.pallas import tpu as pltpu
from jax.sharding import PartitionSpec as P

HEAD_DIM = 128
BLOCK = 128
GLOB = 256
RAND = 3
LOG2E = math.log2(math.e)


def extended_2(cells, sides, width):
    for axis, dim in sides:
        count = lax.axis_size(axis)
        ends = count - 1
        head = lax.slice_in_dim(cells, 0, width, axis=dim)
        tail = lax.slice_in_dim(cells, cells.shape[dim] - width, cells.shape[dim], axis=dim)
        cells = jnp.concatenate(
            [
                lax.ppermute(tail, axis, [(i, (i + 1) % count) for i in range(ends)]),
                cells,
                lax.ppermute(head, axis, [((i + 1) % count, i) for i in range(ends)]),
            ],
            axis=dim,
        )
    return cells


def passed_along(value, axis, by):
    peers = lax.axis_size(axis)
    pairs = [(i, i + by) for i in range(peers) if 0 <= i + by < peers]
    return lax.ppermute(value, axis, pairs)


def shifted(value, axis, by):
    peers = lax.axis_size(axis)
    return lax.ppermute(value, axis, [(i, (i + by) % peers) for i in range(peers)])


def tile_grads(query_rows, grad_rows, norm_rows, delta_rows, key_rows, value_rows, keep_mask):
    att_scale = HEAD_DIM ** (-0.5)
    scores = (
        jnp.einsum("nbd,nkd->nbk", query_rows, key_rows, preferred_element_type=jnp.float32)
        * att_scale
    )
    weights = jnp.exp(scores - norm_rows[:, :, None]) * keep_mask[:, None, :]
    dprobs = jnp.einsum("nbd,nkd->nbk", grad_rows, value_rows, preferred_element_type=jnp.float32)
    dscores = weights * (dprobs - delta_rows[:, :, None])
    weights_low = weights.astype(jnp.bfloat16)
    dscores_low = dscores.astype(jnp.bfloat16)
    grad_values = jnp.einsum(
        "nbk,nbd->nkd", weights_low, grad_rows, preferred_element_type=jnp.float32
    )
    grad_keys = (
        jnp.einsum("nbk,nbd->nkd", dscores_low, query_rows, preferred_element_type=jnp.float32)
        * att_scale
    )
    grad_queries = (
        jnp.einsum("nbk,nkd->nbd", dscores_low, key_rows, preferred_element_type=jnp.float32)
        * att_scale
    )
    return (grad_queries, grad_keys, grad_values)


def head_cols(source, head_index):
    return source[:, head_index * HEAD_DIM : (head_index + 1) * HEAD_DIM]


def head_blocks(source, head_index, num_blocks):
    return head_cols(source, head_index).reshape(num_blocks, BLOCK, HEAD_DIM)


def gather_tiles(tile_rows, slot_ids):
    picked = jnp.take(tile_rows, slot_ids, axis=0)
    return picked.reshape(slot_ids.shape[0], slot_ids.shape[1] * BLOCK, HEAD_DIM)


def tile_picker(slot_ids, hit_mask, num_blocks):
    one_hot = (
        slot_ids[:, :, None] == jnp.arange(num_blocks, dtype=jnp.int32)[None, None, :]
    ) & hit_mask[:, :, None]
    return one_hot.astype(jnp.float32)


def add_tiles(picker, flat_grads, num_blocks):
    tiled_grads = flat_grads.reshape(picker.shape[0], picker.shape[1], BLOCK, HEAD_DIM)
    summed = jnp.einsum("nle,nlbd->ebd", picker, tiled_grads, precision=lax.Precision.HIGHEST)
    return summed.reshape(num_blocks * BLOCK, HEAD_DIM)


def tile_keep(hit_mask, extra_cols):
    tile_cols = jnp.repeat(hit_mask.astype(jnp.float32), BLOCK, axis=1)
    return jnp.concatenate(
        [jnp.ones((hit_mask.shape[0], extra_cols), jnp.float32), tile_cols], axis=1
    )


def with_glob(glob_rows, tile_rows):
    spread = glob_rows[None]
    return jnp.concatenate([spread, tile_rows], axis=1)


def shards(queries, keys, values, outputs, grad_out, log_norm, glob_keys, glob_values, key_lists):
    row_count, col_count = queries.shape
    head_count = col_count // HEAD_DIM
    block_count = row_count // BLOCK
    group_count = lax.axis_size("ctx")
    my_group = lax.axis_index("ctx")
    first_block = my_group * block_count
    incoming = lax.all_to_all(grad_out, "head", split_axis=1, concat_axis=0, tiled=True)
    row_delta = jnp.sum(
        (incoming.astype(jnp.float32) * outputs.astype(jnp.float32)).reshape(
            row_count, head_count, HEAD_DIM
        ),
        axis=2,
    ).T
    own_lists = lax.dynamic_slice_in_dim(key_lists, first_block, block_count, 0)
    query_heads = [
        head_blocks(queries, head_index, block_count) for head_index in range(head_count)
    ]
    grad_heads = [
        head_blocks(incoming, head_index, block_count) for head_index in range(head_count)
    ]
    norm_heads = [
        log_norm[head_index].reshape(block_count, BLOCK) for head_index in range(head_count)
    ]
    delta_heads = [
        row_delta[head_index].reshape(block_count, BLOCK) for head_index in range(head_count)
    ]
    extended = extended_2(jnp.stack([keys, values]), (("ctx", 1),), BLOCK)
    ext_blocks = block_count + 2
    near_lists = own_lists[:, :3]
    near_live = near_lists >= 0
    near_slots = jnp.clip(near_lists - (first_block - 1), 0, ext_blocks - 1)
    near_keep = tile_keep(near_live, GLOB)
    near_picker = tile_picker(near_slots, near_live, ext_blocks)
    dq_parts, dk_parts, dv_parts, glob_dk_parts, glob_dv_parts = ([], [], [], [], [])
    for head_index in range(head_count):
        ext_keys = head_blocks(extended[0], head_index, ext_blocks)
        ext_values = head_blocks(extended[1], head_index, ext_blocks)
        key_rows = with_glob(head_cols(glob_keys, head_index), gather_tiles(ext_keys, near_slots))
        value_rows = with_glob(
            head_cols(glob_values, head_index), gather_tiles(ext_values, near_slots)
        )
        grad_q, grad_k, grad_v = tile_grads(
            query_heads[head_index],
            grad_heads[head_index],
            norm_heads[head_index],
            delta_heads[head_index],
            key_rows,
            value_rows,
            near_keep,
        )
        dq_parts.append(grad_q.reshape(row_count, HEAD_DIM))
        glob_dk_parts.append(jnp.sum(grad_k[:, :GLOB], axis=0))
        glob_dv_parts.append(jnp.sum(grad_v[:, :GLOB], axis=0))
        dk_parts.append(add_tiles(near_picker, grad_k[:, GLOB:], ext_blocks))
        dv_parts.append(add_tiles(near_picker, grad_v[:, GLOB:], ext_blocks))
    query_side = jnp.concatenate(dq_parts, axis=1)
    near_side = jnp.stack([jnp.concatenate(dk_parts, axis=1), jnp.concatenate(dv_parts, axis=1)])
    own_grads = near_side[:, BLOCK : BLOCK + row_count]
    for shift_by in (-1, 1):
        rim_piece = near_side[:, :BLOCK] if shift_by < 0 else near_side[:, BLOCK + row_count :]
        arrived = passed_along(rim_piece, "ctx", shift_by)
        if shift_by < 0:
            own_grads = own_grads.at[:, row_count - BLOCK :].add(arrived)
        else:
            own_grads = own_grads.at[:, :BLOCK].add(arrived)
    full_keep = jnp.ones((block_count, BLOCK), jnp.float32)
    all_hit = jnp.ones((block_count, 1), bool)
    own_pair = jnp.stack([keys, values])
    for round_index in range(RAND):
        hop = (round_index + 1) * group_count // (RAND + 1)
        fetched = shifted(own_pair, "ctx", -hop)
        target_first = (my_group + hop) % group_count * block_count
        far_slots = jnp.clip(own_lists[:, 3 + round_index] - target_first, 0, block_count - 1)[
            :, None
        ]
        far_picker = tile_picker(far_slots, all_hit, block_count)
        far_dq, far_dk, far_dv = ([], [], [])
        for head_index in range(head_count):
            far_keys = gather_tiles(head_blocks(fetched[0], head_index, block_count), far_slots)
            far_values = gather_tiles(head_blocks(fetched[1], head_index, block_count), far_slots)
            grad_q, grad_k, grad_v = tile_grads(
                query_heads[head_index],
                grad_heads[head_index],
                norm_heads[head_index],
                delta_heads[head_index],
                far_keys,
                far_values,
                full_keep,
            )
            far_dq.append(grad_q.reshape(row_count, HEAD_DIM))
            far_dk.append(add_tiles(far_picker, grad_k, block_count))
            far_dv.append(add_tiles(far_picker, grad_v, block_count))
        query_side = query_side + jnp.concatenate(far_dq, axis=1)
        far_pair = jnp.stack([jnp.concatenate(far_dk, axis=1), jnp.concatenate(far_dv, axis=1)])
        own_grads = own_grads + shifted(far_pair, "ctx", hop)
    glob_pair = jnp.stack(
        [jnp.concatenate(glob_dk_parts, axis=1), jnp.concatenate(glob_dv_parts, axis=1)]
    )
    summed_all = lax.psum(glob_pair, "ctx")
    share_rows = GLOB // group_count
    own_share = lax.dynamic_slice_in_dim(summed_all, my_group * share_rows, share_rows, 1)
    return (
        query_side.astype(jnp.bfloat16),
        own_grads[0].astype(jnp.bfloat16),
        own_grads[1].astype(jnp.bfloat16),
        own_share[0],
        own_share[1],
    )


HALVES = 2
HALF = BLOCK // HALVES
K_IN, V_IN, S_IN, Q_IN, G_IN = 0, 1, 2, 3, 3 + HALVES
IN_KINDS = 3 + 2 * HALVES
K_OUT, V_OUT, GLOB_OUT, Q_OUT = 0, 1, 2, 3
OUT_KINDS = 3 + HALVES
CLASSES = 2
CONTRACT_LAST = (((1,), (1,)), ((), ()))


def start_order(peers):
    half = peers // 2
    return [half] + [half + sign * by for by in range(1, half) for sign in (-1, 1)]


def head_kernel(
    peers,
    q_hbm,
    k_hbm,
    v_hbm,
    o_hbm,
    g_hbm,
    norm_hbm,
    gk_hbm,
    gv_hbm,
    dq_hbm,
    dk_hbm,
    dv_hbm,
    glob_hbm,
    q_own,
    k_own,
    v_own,
    g_part,
    dq_out,
    dk_out,
    dv_out,
    glob_out,
    q_all,
    k_all,
    v_all,
    g_all,
    stat_all,
    g_own,
    o_own,
    norm_own,
    stat_own,
    kt_all,
    dq_acc,
    dk_acc,
    dv_acc,
    dq_low,
    dk_low,
    dv_low,
    glob_low,
    load_sem,
    spread_send,
    spread_recv,
    in_send,
    in_recv,
    out_send,
    out_recv,
):
    me = lax.axis_index("ctx")
    my_head = lax.axis_index("head")
    head_peers = lax.axis_size("head")
    members = peers // CLASSES
    class_rows = members * BLOCK
    span = class_rows + GLOB
    share = GLOB // peers
    width = q_hbm.shape[1]
    part_rows = g_part.shape[0]
    order = start_order(peers)

    def cols(index):
        return pl.ds(pl.multiple_of(index * HEAD_DIM, HEAD_DIM), HEAD_DIM)

    def query_rows(half, index):
        at = half * members * CLASSES * HALF + (index % CLASSES) * members * HALF + (index // CLASSES) * HALF
        return pl.ds(at if isinstance(at, int) else pl.multiple_of(at, HALF), HALF)

    def half_rows(half):
        return pl.ds(half * HALF, HALF)

    def key_rows(index):
        at = (index % CLASSES) * span + (index // CLASSES) * BLOCK
        return pl.ds(at if isinstance(at, int) else pl.multiple_of(at, BLOCK), BLOCK)

    def remote(src, dst, send, recv, **device):
        return pltpu.make_async_remote_copy(
            src_ref=src,
            dst_ref=dst,
            send_sem=send,
            recv_sem=recv,
            device_id=device,
            device_id_type=pl.DeviceIdType.MESH,
        )

    loads = [
        pltpu.make_async_copy(o_hbm, o_own, load_sem.at[0]),
        pltpu.make_async_copy(norm_hbm, norm_own, load_sem.at[1]),
        pltpu.make_async_copy(
            gk_hbm.at[:, cols(me)], k_all.at[pl.ds(class_rows, GLOB)], load_sem.at[2]
        ),
        pltpu.make_async_copy(
            gv_hbm.at[:, cols(me)], v_all.at[pl.ds(class_rows, GLOB)], load_sem.at[3]
        ),
    ]
    firsts = [
        pltpu.make_async_copy(src, dst, load_sem.at[4 + at])
        for at, (src, dst) in enumerate(
            ((g_hbm, g_part), (k_hbm, k_own), (q_hbm, q_own), (v_hbm, v_own))
        )
    ]
    for load in firsts:
        load.start()
    for load in loads:
        load.start()

    barrier = pltpu.get_barrier_semaphore()
    for by in range(1, head_peers):
        pl.semaphore_signal(
            barrier,
            inc=1,
            device_id={"head": lax.rem(my_head + by, head_peers)},
            device_id_type=pl.DeviceIdType.MESH,
        )
    for by in order:
        pl.semaphore_signal(
            barrier,
            inc=1,
            device_id={"ctx": lax.rem(me + by, peers)},
            device_id_type=pl.DeviceIdType.MESH,
        )
    pl.semaphore_wait(barrier, head_peers - 1 + peers - 1)

    sends = []
    firsts[0].wait()

    def my_part():
        return pl.ds(pl.multiple_of(my_head * part_rows, part_rows), part_rows)

    def wide(index):
        return pl.ds(pl.multiple_of(index * width, width), width)

    for by in range(1, head_peers):
        to = lax.rem(my_head + by, head_peers)
        copy = remote(
            g_part.at[:, wide(to)],
            g_own.at[my_part()],
            spread_send.at[by],
            spread_recv.at[my_head],
            head=to,
        )
        copy.start()
        sends.append(copy)
    pltpu.make_async_copy(
        g_part.at[:, wide(my_head)], g_own.at[my_part()], spread_recv.at[my_head]
    ).start()

    def spread_in(kind, src, dst, from_rows, rows):
        for by in order:
            to = lax.rem(me + by, peers)
            copy = remote(
                src.at[from_rows, cols(to)],
                dst.at[rows(me)],
                in_send.at[kind, by],
                in_recv.at[kind, me],
                ctx=to,
            )
            copy.start()
            sends.append(copy)
        pltpu.make_async_copy(
            src.at[from_rows, cols(me)], dst.at[rows(me)], in_recv.at[kind, me]
        ).start()

    def arrived(kind, dst, rows):
        for index in range(peers):
            place = dst.at[rows(index)]
            pltpu.make_async_copy(place, place, in_recv.at[kind, index]).wait()

    places = [functools.partial(query_rows, half) for half in range(HALVES)]
    all_rows = pl.ds(0, BLOCK)
    firsts[1].wait()
    spread_in(K_IN, k_own, k_all, all_rows, key_rows)
    firsts[2].wait()
    spread_in(Q_IN, q_own, q_all, half_rows(0), places[0])
    firsts[3].wait()
    spread_in(V_IN, v_own, v_all, all_rows, key_rows)

    loads[0].wait()
    loads[1].wait()
    for index in range(head_peers):
        place = g_own.at[pl.ds(index * part_rows, part_rows)]
        pltpu.make_async_copy(place, place, spread_recv.at[index]).wait()
    spread_in(G_IN, g_own, g_all, half_rows(0), places[0])
    ones = jnp.ones((8, HEAD_DIM), jnp.float32)
    first = lax.broadcasted_iota(jnp.int32, (8, BLOCK), 0) == 0
    for index in range(peers):
        lanes = pl.ds(index * HEAD_DIM, HEAD_DIM)
        product = g_own[:, lanes].astype(jnp.float32) * o_own[:, lanes].astype(jnp.float32)
        delta = lax.dot_general(
            ones,
            product,
            CONTRACT_LAST,
            precision=lax.Precision.HIGHEST,
            preferred_element_type=jnp.float32,
        )
        norm = jnp.broadcast_to(norm_own[pl.ds(index, 1), :], (8, BLOCK))
        stat_own[index] = jnp.where(first, norm * LOG2E, delta)
    for by in order:
        to = lax.rem(me + by, peers)
        copy = remote(
            stat_own.at[to], stat_all.at[me], in_send.at[S_IN, by], in_recv.at[S_IN, me], ctx=to
        )
        copy.start()
        sends.append(copy)
    pltpu.make_async_copy(stat_own.at[me], stat_all.at[me], in_recv.at[S_IN, me]).start()

    for half in range(1, HALVES):
        spread_in(Q_IN + half, q_own, q_all, half_rows(half), places[half])
        spread_in(G_IN + half, g_own, g_all, half_rows(half), places[half])

    scale = HEAD_DIM**-0.5

    def dot(left, right):
        return jnp.dot(left, right, preferred_element_type=jnp.float32)

    def visit(half, blocks, key_at, key_count, keep):
        rows = pl.ds(query_rows(half, blocks[0]).start, len(blocks) * HALF)
        keys = pl.ds(key_at, key_count)
        norm, delta = (
            jnp.concatenate(
                [stat_all[block, row : row + 1, half * HALF : (half + 1) * HALF] for block in blocks],
                axis=1,
            )
            for row in range(2)
        )
        scores = lax.dot_general(
            k_all[keys, :], q_all[rows, :], CONTRACT_LAST, preferred_element_type=jnp.float32
        )
        weights = jnp.exp2(scores * (scale * LOG2E) - norm)
        if keep is not None:
            weights = jnp.where(keep, weights, 0.0)
        dprobs = lax.dot_general(
            v_all[keys, :], g_all[rows, :], CONTRACT_LAST, preferred_element_type=jnp.float32
        )
        dscores = (weights * (dprobs - delta)).astype(jnp.bfloat16)
        dq_acc[:, rows] += dot(kt_all[:, keys], dscores)
        dk_acc[keys, :] += dot(dscores, q_all[rows, :])
        dv_acc[keys, :] += dot(weights.astype(jnp.bfloat16), g_all[rows, :])

    def visit_near(half, blocks):
        near = [at for at in range(blocks[0] - 1, blocks[-1] + 2, CLASSES) if 0 <= at < peers]
        shape = (len(near) * BLOCK, len(blocks) * HALF)
        key_block = near[0] + CLASSES * (lax.broadcasted_iota(jnp.int32, shape, 0) // BLOCK)
        query_block = blocks[0] + CLASSES * (lax.broadcasted_iota(jnp.int32, shape, 1) // HALF)
        keep = jnp.abs(key_block - query_block) == 1
        visit(half, blocks, key_rows(near[0]).start, len(near) * BLOCK, keep)

    def put(kind, src, dst, from_rows, to_rows, block):
        @pl.when(me == block)
        def _():
            pltpu.make_async_copy(
                src.at[from_rows], dst.at[to_rows, cols(me)], out_recv.at[kind, me]
            ).start()

        @pl.when(me != block)
        def _():
            remote(
                src.at[from_rows],
                dst.at[to_rows, cols(me)],
                out_send.at[kind, block],
                out_recv.at[kind, me],
                ctx=block,
            ).start()

    dk_acc[...] = jnp.zeros_like(dk_acc)
    dv_acc[...] = jnp.zeros_like(dv_acc)
    dq_acc[...] = jnp.zeros_like(dq_acc)

    loads[2].wait()
    loads[3].wait()
    arrived(K_IN, k_all, key_rows)
    kt_all[...] = k_all[...].T
    arrived(V_IN, v_all, key_rows)
    for index in range(peers):
        place = stat_all.at[index]
        pltpu.make_async_copy(place, place, in_recv.at[S_IN, index]).wait()

    pair = 2
    for half in range(HALVES):
        arrived(Q_IN + half, q_all, places[half])
        arrived(G_IN + half, g_all, places[half])
        for part in range(CLASSES):
            for at in range(0, members, pair):
                visit_near(half, [part + CLASSES * (at + step) for step in range(pair)])
        for part in range(CLASSES):
            blocks = [part + CLASSES * at for at in range(members)]
            visit(half, blocks, part * class_rows, span, None)
            rows = pl.ds(query_rows(half, part).start, members * HALF)
            dq_low[rows, :] = (dq_acc[:, rows] * scale).T.astype(jnp.bfloat16)
            for block in blocks:
                put(Q_OUT + half, dq_low, dq_out, query_rows(half, block), half_rows(half), block)
            if half == HALVES - 1:
                own = pl.ds(part * span, class_rows)
                dk_low[own, :] = (dk_acc[own, :] * scale).astype(jnp.bfloat16)
                for block in blocks:
                    put(K_OUT, dk_low, dk_out, key_rows(block), all_rows, block)
                dv_low[own, :] = dv_acc[own, :].astype(jnp.bfloat16)
                for block in blocks:
                    put(V_OUT, dv_low, dv_out, key_rows(block), all_rows, block)

    middle = pl.ds(class_rows, GLOB)
    glob_low[0] = (dk_acc[middle, :] * scale).astype(jnp.bfloat16)
    glob_low[1] = dv_acc[middle, :].astype(jnp.bfloat16)

    def share_of(index):
        return glob_low.at[:, pl.ds(pl.multiple_of(index * share, share), share), :]

    for by in order:
        to = lax.rem(me + by, peers)
        copy = remote(
            share_of(to),
            glob_out.at[:, :, cols(me)],
            out_send.at[GLOB_OUT, to],
            out_recv.at[GLOB_OUT, me],
            ctx=to,
        )
        copy.start()
        sends.append(copy)
    pltpu.make_async_copy(
        share_of(me), glob_out.at[:, :, cols(me)], out_recv.at[GLOB_OUT, me]
    ).start()

    stores = []

    def store(at, src, dst):
        copy = pltpu.make_async_copy(src, dst, load_sem.at[8 + at])
        copy.start()
        stores.append(copy)

    for half in range(HALVES):
        for index in range(peers):
            place = dq_out.at[half_rows(half), cols(index)]
            pltpu.make_async_copy(place, place, out_recv.at[Q_OUT + half, index]).wait()
    store(0, dq_out, dq_hbm)
    for at, (kind, dst, home) in enumerate(((K_OUT, dk_out, dk_hbm), (V_OUT, dv_out, dv_hbm))):
        for index in range(peers):
            place = dst.at[:, cols(index)]
            pltpu.make_async_copy(place, place, out_recv.at[kind, index]).wait()
        store(1 + at, dst, home)
    for index in range(peers):
        place = glob_out.at[:, :, cols(index)]
        pltpu.make_async_copy(place, place, out_recv.at[GLOB_OUT, index]).wait()
    store(3, glob_out, glob_hbm)

    for copy in sends:
        copy.wait_send()
    halves = [(Q_OUT + half, dq_low, places[half]) for half in range(HALVES)]
    for by in order:
        to = lax.rem(me + by, peers)
        for kind, src, rows in [(K_OUT, dk_low, key_rows), (V_OUT, dv_low, key_rows)] + halves:
            place = src.at[rows(to)]
            pltpu.make_async_copy(place, place, out_send.at[kind, to]).wait()
    for copy in stores:
        copy.wait()


def finish_kernel(
    dq_in, dk_in, dv_in, glob_in, dq_out, dk_out, dv_out, gk_out, gv_out, held, low, wide, load, save
):
    loads = [
        pltpu.make_async_copy(src, dst, load.at[at])
        for at, (src, dst) in enumerate(
            ((glob_in, low), (dq_in, held.at[0]), (dk_in, held.at[1]), (dv_in, held.at[2]))
        )
    ]
    for copy in loads:
        copy.start()
    saves = [
        pltpu.make_async_copy(src, dst, save.at[at])
        for at, (src, dst) in enumerate(
            (
                (wide.at[0], gk_out),
                (wide.at[1], gv_out),
                (held.at[0], dq_out),
                (held.at[1], dk_out),
                (held.at[2], dv_out),
            )
        )
    ]
    loads[0].wait()
    wide[...] = low[...].astype(jnp.float32)
    saves[0].start()
    saves[1].start()
    for ready, copy in zip(loads[1:], saves[2:]):
        ready.wait()
        copy.start()
    for copy in saves:
        copy.wait()


def whole_heads(peers, queries, keys, values, outputs, grad_out, log_norm, glob_keys, glob_values):
    row_count, col_count = queries.shape
    tokens = peers * BLOCK
    low, full = jnp.bfloat16, jnp.float32
    head_peers = lax.axis_size("head")
    result = jax.ShapeDtypeStruct((row_count, col_count), low)
    scores = tokens * (GLOB + (RAND + 3) * BLOCK)
    dq, dk, dv, glob = pl.pallas_call(
        functools.partial(head_kernel, peers),
        out_shape=(
            result,
            result,
            result,
            jax.ShapeDtypeStruct((2, GLOB // peers, col_count), low),
        ),
        in_specs=[pl.BlockSpec(memory_space=pl.ANY)] * 8,
        out_specs=[pl.BlockSpec(memory_space=pl.ANY)] * 4,
        scratch_shapes=[
            pltpu.VMEM((row_count, col_count), low),
            pltpu.VMEM((row_count, col_count), low),
            pltpu.VMEM((row_count, col_count), low),
            pltpu.VMEM(grad_out.shape, low),
            pltpu.VMEM((row_count, col_count), low),
            pltpu.VMEM((row_count, col_count), low),
            pltpu.VMEM((row_count, col_count), low),
            pltpu.VMEM((2, GLOB // peers, col_count), low),
            pltpu.VMEM((tokens, HEAD_DIM), low),
            pltpu.VMEM((tokens + GLOB, HEAD_DIM), low),
            pltpu.VMEM((tokens + GLOB, HEAD_DIM), low),
            pltpu.VMEM((tokens, HEAD_DIM), low),
            pltpu.VMEM((peers, 8, BLOCK), full),
            pltpu.VMEM((row_count, col_count), low),
            pltpu.VMEM((row_count, col_count), low),
            pltpu.VMEM(log_norm.shape, full),
            pltpu.VMEM((peers, 8, BLOCK), full),
            pltpu.VMEM((HEAD_DIM, tokens + GLOB), low),
            pltpu.VMEM((HEAD_DIM, tokens), full),
            pltpu.VMEM((tokens + GLOB, HEAD_DIM), full),
            pltpu.VMEM((tokens + GLOB, HEAD_DIM), full),
            pltpu.VMEM((tokens, HEAD_DIM), low),
            pltpu.VMEM((tokens + GLOB, HEAD_DIM), low),
            pltpu.VMEM((tokens + GLOB, HEAD_DIM), low),
            pltpu.VMEM((2, GLOB, HEAD_DIM), low),
            pltpu.SemaphoreType.DMA((12,)),
            pltpu.SemaphoreType.DMA((head_peers,)),
            pltpu.SemaphoreType.DMA((head_peers,)),
            pltpu.SemaphoreType.DMA((IN_KINDS, peers)),
            pltpu.SemaphoreType.DMA((IN_KINDS, peers)),
            pltpu.SemaphoreType.DMA((OUT_KINDS, peers)),
            pltpu.SemaphoreType.DMA((OUT_KINDS, peers)),
        ],
        compiler_params=pltpu.CompilerParams(
            collective_id=0, has_side_effects=True, vmem_limit_bytes=64 * 1024 * 1024
        ),
        cost_estimate=pl.CostEstimate(
            flops=10 * scores * HEAD_DIM, bytes_accessed=4 * 1024 * 1024, transcendentals=scores
        ),
        name="whole_heads",
    )(queries, keys, values, outputs, grad_out, log_norm, glob_keys, glob_values)
    share = jax.ShapeDtypeStruct((GLOB // peers, col_count), full)
    hbm = pl.BlockSpec(memory_space=pltpu.HBM)
    return pl.pallas_call(
        finish_kernel,
        out_shape=(result, result, result, share, share),
        in_specs=[pl.BlockSpec(memory_space=pl.ANY)] * 4,
        out_specs=[hbm] * 5,
        scratch_shapes=[
            pltpu.VMEM((3, row_count, col_count), low),
            pltpu.VMEM((2, GLOB // peers, col_count), low),
            pltpu.VMEM((2, GLOB // peers, col_count), full),
            pltpu.SemaphoreType.DMA((4,)),
            pltpu.SemaphoreType.DMA((5,)),
        ],
        compiler_params=pltpu.CompilerParams(vmem_limit_bytes=64 * 1024 * 1024),
        cost_estimate=pl.CostEstimate(
            flops=0, bytes_accessed=2 * 1024 * 1024, transcendentals=0
        ),
        name="finish",
    )(dq, dk, dv, glob)


def program(mesh):
    peers = mesh.shape["ctx"]

    def body(queries, keys, values, outputs, grad_out, log_norm, glob_keys, glob_values, key_lists):
        row_count, col_count = queries.shape
        one_head_each = (
            row_count == BLOCK
            and col_count == peers * HEAD_DIM
            and peers == CLASSES * (RAND + 1)
            and GLOB % (16 * peers) == 0
        )
        if one_head_each:
            return whole_heads(
                peers, queries, keys, values, outputs, grad_out, log_norm, glob_keys, glob_values
            )
        return shards(
            queries, keys, values, outputs, grad_out, log_norm, glob_keys, glob_values, key_lists
        )

    return body


def solution(mesh):
    in_specs = (
        P("ctx", "head"),
        P("ctx", "head"),
        P("ctx", "head"),
        P("ctx", "head"),
        P(("ctx", "head"), None),
        P("head", "ctx"),
        P(None, "head"),
        P(None, "head"),
        P(),
    )
    out_specs = (
        P("ctx", "head"),
        P("ctx", "head"),
        P("ctx", "head"),
        P("ctx", "head"),
        P("ctx", "head"),
    )
    return jax.shard_map(program(mesh), mesh=mesh, in_specs=in_specs, out_specs=out_specs, check_vma=False)
```

```python
import functools
import math

import jax
import jax.numpy as jnp
from jax import lax
from jax.experimental import pallas as pl
from jax.experimental.pallas import tpu as pltpu
from jax.sharding import PartitionSpec as P

HEAD_DIM = 128
BLOCK = 128
GLOB = 256
RAND = 3
LOG2E = math.log2(math.e)


def extended_2(cells, sides, width):
    for axis, dim in sides:
        count = lax.axis_size(axis)
        ends = count - 1
        head = lax.slice_in_dim(cells, 0, width, axis=dim)
        tail = lax.slice_in_dim(cells, cells.shape[dim] - width, cells.shape[dim], axis=dim)
        cells = jnp.concatenate(
            [
                lax.ppermute(tail, axis, [(i, (i + 1) % count) for i in range(ends)]),
                cells,
                lax.ppermute(head, axis, [((i + 1) % count, i) for i in range(ends)]),
            ],
            axis=dim,
        )
    return cells


def passed_along(value, axis, by):
    peers = lax.axis_size(axis)
    pairs = [(i, i + by) for i in range(peers) if 0 <= i + by < peers]
    return lax.ppermute(value, axis, pairs)


def shifted(value, axis, by):
    peers = lax.axis_size(axis)
    return lax.ppermute(value, axis, [(i, (i + by) % peers) for i in range(peers)])


def tile_grads(query_rows, grad_rows, norm_rows, delta_rows, key_rows, value_rows, keep_mask):
    att_scale = HEAD_DIM ** (-0.5)
    scores = (
        jnp.einsum("nbd,nkd->nbk", query_rows, key_rows, preferred_element_type=jnp.float32)
        * att_scale
    )
    weights = jnp.exp(scores - norm_rows[:, :, None]) * keep_mask[:, None, :]
    dprobs = jnp.einsum("nbd,nkd->nbk", grad_rows, value_rows, preferred_element_type=jnp.float32)
    dscores = weights * (dprobs - delta_rows[:, :, None])
    weights_low = weights.astype(jnp.bfloat16)
    dscores_low = dscores.astype(jnp.bfloat16)
    grad_values = jnp.einsum(
        "nbk,nbd->nkd", weights_low, grad_rows, preferred_element_type=jnp.float32
    )
    grad_keys = (
        jnp.einsum("nbk,nbd->nkd", dscores_low, query_rows, preferred_element_type=jnp.float32)
        * att_scale
    )
    grad_queries = (
        jnp.einsum("nbk,nkd->nbd", dscores_low, key_rows, preferred_element_type=jnp.float32)
        * att_scale
    )
    return (grad_queries, grad_keys, grad_values)


def head_cols(source, head_index):
    return source[:, head_index * HEAD_DIM : (head_index + 1) * HEAD_DIM]


def head_blocks(source, head_index, num_blocks):
    return head_cols(source, head_index).reshape(num_blocks, BLOCK, HEAD_DIM)


def gather_tiles(tile_rows, slot_ids):
    picked = jnp.take(tile_rows, slot_ids, axis=0)
    return picked.reshape(slot_ids.shape[0], slot_ids.shape[1] * BLOCK, HEAD_DIM)


def tile_picker(slot_ids, hit_mask, num_blocks):
    one_hot = (
        slot_ids[:, :, None] == jnp.arange(num_blocks, dtype=jnp.int32)[None, None, :]
    ) & hit_mask[:, :, None]
    return one_hot.astype(jnp.float32)


def add_tiles(picker, flat_grads, num_blocks):
    tiled_grads = flat_grads.reshape(picker.shape[0], picker.shape[1], BLOCK, HEAD_DIM)
    summed = jnp.einsum("nle,nlbd->ebd", picker, tiled_grads, precision=lax.Precision.HIGHEST)
    return summed.reshape(num_blocks * BLOCK, HEAD_DIM)


def tile_keep(hit_mask, extra_cols):
    tile_cols = jnp.repeat(hit_mask.astype(jnp.float32), BLOCK, axis=1)
    return jnp.concatenate(
        [jnp.ones((hit_mask.shape[0], extra_cols), jnp.float32), tile_cols], axis=1
    )


def with_glob(glob_rows, tile_rows):
    spread = glob_rows[None]
    return jnp.concatenate([spread, tile_rows], axis=1)


def shards(queries, keys, values, outputs, grad_out, log_norm, glob_keys, glob_values, key_lists):
    row_count, col_count = queries.shape
    head_count = col_count // HEAD_DIM
    block_count = row_count // BLOCK
    group_count = lax.axis_size("ctx")
    my_group = lax.axis_index("ctx")
    first_block = my_group * block_count
    incoming = lax.all_to_all(grad_out, "head", split_axis=1, concat_axis=0, tiled=True)
    row_delta = jnp.sum(
        (incoming.astype(jnp.float32) * outputs.astype(jnp.float32)).reshape(
            row_count, head_count, HEAD_DIM
        ),
        axis=2,
    ).T
    own_lists = lax.dynamic_slice_in_dim(key_lists, first_block, block_count, 0)
    query_heads = [
        head_blocks(queries, head_index, block_count) for head_index in range(head_count)
    ]
    grad_heads = [
        head_blocks(incoming, head_index, block_count) for head_index in range(head_count)
    ]
    norm_heads = [
        log_norm[head_index].reshape(block_count, BLOCK) for head_index in range(head_count)
    ]
    delta_heads = [
        row_delta[head_index].reshape(block_count, BLOCK) for head_index in range(head_count)
    ]
    extended = extended_2(jnp.stack([keys, values]), (("ctx", 1),), BLOCK)
    ext_blocks = block_count + 2
    near_lists = own_lists[:, :3]
    near_live = near_lists >= 0
    near_slots = jnp.clip(near_lists - (first_block - 1), 0, ext_blocks - 1)
    near_keep = tile_keep(near_live, GLOB)
    near_picker = tile_picker(near_slots, near_live, ext_blocks)
    dq_parts, dk_parts, dv_parts, glob_dk_parts, glob_dv_parts = ([], [], [], [], [])
    for head_index in range(head_count):
        ext_keys = head_blocks(extended[0], head_index, ext_blocks)
        ext_values = head_blocks(extended[1], head_index, ext_blocks)
        key_rows = with_glob(head_cols(glob_keys, head_index), gather_tiles(ext_keys, near_slots))
        value_rows = with_glob(
            head_cols(glob_values, head_index), gather_tiles(ext_values, near_slots)
        )
        grad_q, grad_k, grad_v = tile_grads(
            query_heads[head_index],
            grad_heads[head_index],
            norm_heads[head_index],
            delta_heads[head_index],
            key_rows,
            value_rows,
            near_keep,
        )
        dq_parts.append(grad_q.reshape(row_count, HEAD_DIM))
        glob_dk_parts.append(jnp.sum(grad_k[:, :GLOB], axis=0))
        glob_dv_parts.append(jnp.sum(grad_v[:, :GLOB], axis=0))
        dk_parts.append(add_tiles(near_picker, grad_k[:, GLOB:], ext_blocks))
        dv_parts.append(add_tiles(near_picker, grad_v[:, GLOB:], ext_blocks))
    query_side = jnp.concatenate(dq_parts, axis=1)
    near_side = jnp.stack([jnp.concatenate(dk_parts, axis=1), jnp.concatenate(dv_parts, axis=1)])
    own_grads = near_side[:, BLOCK : BLOCK + row_count]
    for shift_by in (-1, 1):
        rim_piece = near_side[:, :BLOCK] if shift_by < 0 else near_side[:, BLOCK + row_count :]
        arrived = passed_along(rim_piece, "ctx", shift_by)
        if shift_by < 0:
            own_grads = own_grads.at[:, row_count - BLOCK :].add(arrived)
        else:
            own_grads = own_grads.at[:, :BLOCK].add(arrived)
    full_keep = jnp.ones((block_count, BLOCK), jnp.float32)
    all_hit = jnp.ones((block_count, 1), bool)
    own_pair = jnp.stack([keys, values])
    for round_index in range(RAND):
        hop = (round_index + 1) * group_count // (RAND + 1)
        fetched = shifted(own_pair, "ctx", -hop)
        target_first = (my_group + hop) % group_count * block_count
        far_slots = jnp.clip(own_lists[:, 3 + round_index] - target_first, 0, block_count - 1)[
            :, None
        ]
        far_picker = tile_picker(far_slots, all_hit, block_count)
        far_dq, far_dk, far_dv = ([], [], [])
        for head_index in range(head_count):
            far_keys = gather_tiles(head_blocks(fetched[0], head_index, block_count), far_slots)
            far_values = gather_tiles(head_blocks(fetched[1], head_index, block_count), far_slots)
            grad_q, grad_k, grad_v = tile_grads(
                query_heads[head_index],
                grad_heads[head_index],
                norm_heads[head_index],
                delta_heads[head_index],
                far_keys,
                far_values,
                full_keep,
            )
            far_dq.append(grad_q.reshape(row_count, HEAD_DIM))
            far_dk.append(add_tiles(far_picker, grad_k, block_count))
            far_dv.append(add_tiles(far_picker, grad_v, block_count))
        query_side = query_side + jnp.concatenate(far_dq, axis=1)
        far_pair = jnp.stack([jnp.concatenate(far_dk, axis=1), jnp.concatenate(far_dv, axis=1)])
        own_grads = own_grads + shifted(far_pair, "ctx", hop)
    glob_pair = jnp.stack(
        [jnp.concatenate(glob_dk_parts, axis=1), jnp.concatenate(glob_dv_parts, axis=1)]
    )
    summed_all = lax.psum(glob_pair, "ctx")
    share_rows = GLOB // group_count
    own_share = lax.dynamic_slice_in_dim(summed_all, my_group * share_rows, share_rows, 1)
    return (
        query_side.astype(jnp.bfloat16),
        own_grads[0].astype(jnp.bfloat16),
        own_grads[1].astype(jnp.bfloat16),
        own_share[0],
        own_share[1],
    )


HALVES = 2
HALF = BLOCK // HALVES
K_IN, V_IN, NORM_IN, DELTA_IN, Q_IN, G_IN = 0, 1, 2, 3, 4, 4 + HALVES
IN_KINDS = 4 + 2 * HALVES
PAIR = 2
K_OUT, V_OUT, GLOB_OUT, Q_OUT = 0, 1, 2, 3
OUT_KINDS = 3 + HALVES
CLASSES = 2
CONTRACT_LAST = (((1,), (1,)), ((), ()))


def start_order(peers):
    half = peers // 2
    return [half] + [half + sign * by for by in range(1, half) for sign in (-1, 1)]


def head_kernel(
    peers,
    q_hbm,
    k_hbm,
    v_hbm,
    o_hbm,
    g_hbm,
    norm_hbm,
    gk_hbm,
    gv_hbm,
    dq_hbm,
    dk_hbm,
    dv_hbm,
    glob_hbm,
    q_own,
    k_own,
    v_own,
    g_part,
    dq_out,
    dk_out,
    dv_out,
    glob_out,
    q_all,
    k_all,
    v_all,
    g_all,
    norm_all,
    delta_all,
    g_own,
    o_own,
    norm_own,
    norm_tiles,
    delta_tiles,
    kt_all,
    far_weights,
    far_low,
    near_weights,
    near_low,
    dq_acc,
    dk_acc,
    dv_acc,
    dq_low,
    dk_low,
    dv_low,
    glob_low,
    load_sem,
    spread_send,
    spread_recv,
    in_send,
    in_recv,
    out_send,
    out_recv,
):
    me = lax.axis_index("ctx")
    my_head = lax.axis_index("head")
    head_peers = lax.axis_size("head")
    members = peers // CLASSES
    class_rows = members * BLOCK
    span = class_rows + GLOB
    share = GLOB // peers
    width = q_hbm.shape[1]
    part_rows = g_part.shape[0]
    order = start_order(peers)

    def cols(index):
        return pl.ds(pl.multiple_of(index * HEAD_DIM, HEAD_DIM), HEAD_DIM)

    def query_rows(half, index):
        at = half * members * CLASSES * HALF + (index % CLASSES) * members * HALF + (index // CLASSES) * HALF
        return pl.ds(at if isinstance(at, int) else pl.multiple_of(at, HALF), HALF)

    def half_rows(half):
        return pl.ds(half * HALF, HALF)

    def key_rows(index):
        at = (index % CLASSES) * span + (index // CLASSES) * BLOCK
        return pl.ds(at if isinstance(at, int) else pl.multiple_of(at, BLOCK), BLOCK)

    def remote(src, dst, send, recv, **device):
        return pltpu.make_async_remote_copy(
            src_ref=src,
            dst_ref=dst,
            send_sem=send,
            recv_sem=recv,
            device_id=device,
            device_id_type=pl.DeviceIdType.MESH,
        )

    loads = [
        pltpu.make_async_copy(o_hbm, o_own, load_sem.at[0]),
        pltpu.make_async_copy(norm_hbm, norm_own, load_sem.at[1]),
        pltpu.make_async_copy(
            gk_hbm.at[:, cols(me)], k_all.at[pl.ds(class_rows, GLOB)], load_sem.at[2]
        ),
        pltpu.make_async_copy(
            gv_hbm.at[:, cols(me)], v_all.at[pl.ds(class_rows, GLOB)], load_sem.at[3]
        ),
    ]
    firsts = [
        pltpu.make_async_copy(src, dst, load_sem.at[4 + at])
        for at, (src, dst) in enumerate(
            ((g_hbm, g_part), (k_hbm, k_own), (q_hbm, q_own), (v_hbm, v_own))
        )
    ]
    for load in firsts:
        load.start()
    for load in loads:
        load.start()

    barrier = pltpu.get_barrier_semaphore()
    for by in range(1, head_peers):
        pl.semaphore_signal(
            barrier,
            inc=1,
            device_id={"head": lax.rem(my_head + by, head_peers)},
            device_id_type=pl.DeviceIdType.MESH,
        )
    for by in order:
        pl.semaphore_signal(
            barrier,
            inc=1,
            device_id={"ctx": lax.rem(me + by, peers)},
            device_id_type=pl.DeviceIdType.MESH,
        )
    pl.semaphore_wait(barrier, head_peers - 1 + peers - 1)

    sends = []
    firsts[0].wait()

    def my_part():
        return pl.ds(pl.multiple_of(my_head * part_rows, part_rows), part_rows)

    def wide(index):
        return pl.ds(pl.multiple_of(index * width, width), width)

    for by in range(1, head_peers):
        to = lax.rem(my_head + by, head_peers)
        copy = remote(
            g_part.at[:, wide(to)],
            g_own.at[my_part()],
            spread_send.at[by],
            spread_recv.at[my_head],
            head=to,
        )
        copy.start()
        sends.append(copy)
    pltpu.make_async_copy(
        g_part.at[:, wide(my_head)], g_own.at[my_part()], spread_recv.at[my_head]
    ).start()

    def spread_in(kind, src, dst, from_rows, rows):
        for by in order:
            to = lax.rem(me + by, peers)
            copy = remote(
                src.at[from_rows, cols(to)],
                dst.at[rows(me)],
                in_send.at[kind, by],
                in_recv.at[kind, me],
                ctx=to,
            )
            copy.start()
            sends.append(copy)
        pltpu.make_async_copy(
            src.at[from_rows, cols(me)], dst.at[rows(me)], in_recv.at[kind, me]
        ).start()

    def arrived(kind, dst, rows):
        for index in range(peers):
            place = dst.at[rows(index)]
            pltpu.make_async_copy(place, place, in_recv.at[kind, index]).wait()

    places = [functools.partial(query_rows, half) for half in range(HALVES)]
    all_rows = pl.ds(0, BLOCK)
    def tiles_in(kind, src, dst):
        for by in order:
            to = lax.rem(me + by, peers)
            copy = remote(
                src.at[to], dst.at[me], in_send.at[kind, by], in_recv.at[kind, me], ctx=to
            )
            copy.start()
            sends.append(copy)
        pltpu.make_async_copy(src.at[me], dst.at[me], in_recv.at[kind, me]).start()

    def tiles_arrived(kind, dst):
        for index in range(peers):
            place = dst.at[index]
            pltpu.make_async_copy(place, place, in_recv.at[kind, index]).wait()

    firsts[1].wait()
    spread_in(K_IN, k_own, k_all, all_rows, key_rows)
    firsts[2].wait()
    spread_in(Q_IN, q_own, q_all, half_rows(0), places[0])
    loads[1].wait()
    for index in range(peers):
        norm = norm_own[pl.ds(index, 1), :] * LOG2E
        norm_tiles[index] = jnp.broadcast_to(norm, (8, BLOCK))
    tiles_in(NORM_IN, norm_tiles, norm_all)
    for half in range(1, HALVES):
        spread_in(Q_IN + half, q_own, q_all, half_rows(half), places[half])
    firsts[3].wait()
    spread_in(V_IN, v_own, v_all, all_rows, key_rows)

    loads[0].wait()
    for index in range(head_peers):
        place = g_own.at[pl.ds(index * part_rows, part_rows)]
        pltpu.make_async_copy(place, place, spread_recv.at[index]).wait()
    spread_in(G_IN, g_own, g_all, half_rows(0), places[0])
    ones = jnp.ones((8, HEAD_DIM), jnp.float32)
    for index in range(peers):
        lanes = pl.ds(index * HEAD_DIM, HEAD_DIM)
        product = g_own[:, lanes].astype(jnp.float32) * o_own[:, lanes].astype(jnp.float32)
        delta_tiles[index] = lax.dot_general(
            ones,
            product,
            CONTRACT_LAST,
            precision=lax.Precision.HIGHEST,
            preferred_element_type=jnp.float32,
        )
    tiles_in(DELTA_IN, delta_tiles, delta_all)
    for half in range(1, HALVES):
        spread_in(G_IN + half, g_own, g_all, half_rows(half), places[half])

    scale = HEAD_DIM**-0.5

    def dot(left, right):
        return jnp.dot(left, right, preferred_element_type=jnp.float32)

    def row_of(tiles, half, blocks):
        return jnp.concatenate(
            [tiles[block, 0:1, half * HALF : (half + 1) * HALF] for block in blocks], axis=1
        )

    def rows_of(half, blocks):
        return pl.ds(query_rows(half, blocks[0]).start, len(blocks) * HALF)

    def weigh(half, blocks, key_at, key_count, keep, full, low):
        rows = rows_of(half, blocks)
        keys = pl.ds(key_at, key_count)
        scores = lax.dot_general(
            k_all[keys, :], q_all[rows, :], CONTRACT_LAST, preferred_element_type=jnp.float32
        )
        weights = jnp.exp2(scores * (scale * LOG2E) - row_of(norm_all, half, blocks))
        if keep is not None:
            weights = jnp.where(keep, weights, 0.0)
        full[pl.ds(0, key_count), :] = weights
        low[pl.ds(0, key_count), :] = weights.astype(jnp.bfloat16)

    def push(half, blocks, key_at, key_count, full, low):
        rows = rows_of(half, blocks)
        keys = pl.ds(key_at, key_count)
        dprobs = lax.dot_general(
            v_all[keys, :], g_all[rows, :], CONTRACT_LAST, preferred_element_type=jnp.float32
        )
        weights = full[pl.ds(0, key_count), :]
        dscores = (weights * (dprobs - row_of(delta_all, half, blocks))).astype(jnp.bfloat16)
        dv_acc[keys, :] += dot(low[pl.ds(0, key_count), :], g_all[rows, :])
        dk_acc[keys, :] += dot(dscores, q_all[rows, :])
        dq_acc[:, rows] += dot(kt_all[:, keys], dscores)

    def pairs(part):
        return [
            [part + CLASSES * (at + step) for step in range(PAIR)]
            for at in range(0, members, PAIR)
        ]

    def near_keys(blocks):
        return [at for at in range(blocks[0] - 1, blocks[-1] + 2, CLASSES) if 0 <= at < peers]

    def near_slot(half, blocks):
        part, at = blocks[0] % CLASSES, blocks[0] // CLASSES // PAIR
        slot = (half * CLASSES + part) * (members // PAIR) + at
        return near_weights.at[slot], near_low.at[slot]

    def weigh_near(half, blocks):
        near = near_keys(blocks)
        shape = (len(near) * BLOCK, len(blocks) * HALF)
        key_block = near[0] + CLASSES * (lax.broadcasted_iota(jnp.int32, shape, 0) // BLOCK)
        query_block = blocks[0] + CLASSES * (lax.broadcasted_iota(jnp.int32, shape, 1) // HALF)
        keep = jnp.abs(key_block - query_block) == 1
        at = key_rows(near[0]).start
        weigh(half, blocks, at, len(near) * BLOCK, keep, *near_slot(half, blocks))

    def push_near(half, part):
        for blocks in pairs(part):
            near = near_keys(blocks)
            at = key_rows(near[0]).start
            push(half, blocks, at, len(near) * BLOCK, *near_slot(half, blocks))

    def class_blocks(part):
        return [part + CLASSES * at for at in range(members)]

    def far_slot(half, part):
        return far_weights.at[half * CLASSES + part], far_low.at[half * CLASSES + part]

    def push_far(half, part):
        push(half, class_blocks(part), part * class_rows, span, *far_slot(half, part))

    def put(kind, src, dst, from_rows, to_rows, block):
        @pl.when(me == block)
        def _():
            pltpu.make_async_copy(
                src.at[from_rows], dst.at[to_rows, cols(me)], out_recv.at[kind, me]
            ).start()

        @pl.when(me != block)
        def _():
            remote(
                src.at[from_rows],
                dst.at[to_rows, cols(me)],
                out_send.at[kind, block],
                out_recv.at[kind, me],
                ctx=block,
            ).start()

    dk_acc[...] = jnp.zeros_like(dk_acc)
    dv_acc[...] = jnp.zeros_like(dv_acc)
    dq_acc[...] = jnp.zeros_like(dq_acc)

    def put_queries(half, part):
        rows = rows_of(half, class_blocks(part))
        dq_low[rows, :] = (dq_acc[:, rows] * scale).T.astype(jnp.bfloat16)
        for block in class_blocks(part):
            put(Q_OUT + half, dq_low, dq_out, query_rows(half, block), half_rows(half), block)

    def put_keys(part):
        own = pl.ds(part * span, class_rows)
        dk_low[own, :] = (dk_acc[own, :] * scale).astype(jnp.bfloat16)
        for block in class_blocks(part):
            put(K_OUT, dk_low, dk_out, key_rows(block), all_rows, block)
        dv_low[own, :] = dv_acc[own, :].astype(jnp.bfloat16)
        for block in class_blocks(part):
            put(V_OUT, dv_low, dv_out, key_rows(block), all_rows, block)

    loads[2].wait()
    loads[3].wait()
    arrived(K_IN, k_all, key_rows)
    kt_all[...] = k_all[...].T
    tiles_arrived(NORM_IN, norm_all)
    for half in range(HALVES):
        arrived(Q_IN + half, q_all, places[half])
        for part in range(CLASSES):
            weigh(
                half, class_blocks(part), part * class_rows, span, None, *far_slot(half, part)
            )
            for blocks in pairs(part):
                weigh_near(half, blocks)
    arrived(V_IN, v_all, key_rows)
    tiles_arrived(DELTA_IN, delta_all)

    for half in range(HALVES):
        arrived(G_IN + half, g_all, places[half])
        push_near(half, 1)
        push_far(half, 0)
        if half == HALVES - 1:
            put_keys(0)
        push_near(half, 0)
        put_queries(half, 0)
        push_far(half, 1)
        if half == HALVES - 1:
            put_keys(1)
        put_queries(half, 1)

    middle = pl.ds(class_rows, GLOB)
    glob_low[0] = (dk_acc[middle, :] * scale).astype(jnp.bfloat16)
    glob_low[1] = dv_acc[middle, :].astype(jnp.bfloat16)

    def share_of(index):
        return glob_low.at[:, pl.ds(pl.multiple_of(index * share, share), share), :]

    for by in order:
        to = lax.rem(me + by, peers)
        copy = remote(
            share_of(to),
            glob_out.at[:, :, cols(me)],
            out_send.at[GLOB_OUT, to],
            out_recv.at[GLOB_OUT, me],
            ctx=to,
        )
        copy.start()
        sends.append(copy)
    pltpu.make_async_copy(
        share_of(me), glob_out.at[:, :, cols(me)], out_recv.at[GLOB_OUT, me]
    ).start()

    stores = []

    def store(at, src, dst):
        copy = pltpu.make_async_copy(src, dst, load_sem.at[8 + at])
        copy.start()
        stores.append(copy)

    for half in range(HALVES):
        for index in range(peers):
            place = dq_out.at[half_rows(half), cols(index)]
            pltpu.make_async_copy(place, place, out_recv.at[Q_OUT + half, index]).wait()
    store(0, dq_out, dq_hbm)
    for at, (kind, dst, home) in enumerate(((K_OUT, dk_out, dk_hbm), (V_OUT, dv_out, dv_hbm))):
        for index in range(peers):
            place = dst.at[:, cols(index)]
            pltpu.make_async_copy(place, place, out_recv.at[kind, index]).wait()
        store(1 + at, dst, home)
    for index in range(peers):
        place = glob_out.at[:, :, cols(index)]
        pltpu.make_async_copy(place, place, out_recv.at[GLOB_OUT, index]).wait()
    store(3, glob_out, glob_hbm)

    for copy in sends:
        copy.wait_send()
    halves = [(Q_OUT + half, dq_low, places[half]) for half in range(HALVES)]
    for by in order:
        to = lax.rem(me + by, peers)
        for kind, src, rows in [(K_OUT, dk_low, key_rows), (V_OUT, dv_low, key_rows)] + halves:
            place = src.at[rows(to)]
            pltpu.make_async_copy(place, place, out_send.at[kind, to]).wait()
    for copy in stores:
        copy.wait()


def finish_kernel(
    dq_in, dk_in, dv_in, glob_in, dq_out, dk_out, dv_out, gk_out, gv_out, held, low, wide, load, save
):
    loads = [
        pltpu.make_async_copy(src, dst, load.at[at])
        for at, (src, dst) in enumerate(
            ((glob_in, low), (dq_in, held.at[0]), (dk_in, held.at[1]), (dv_in, held.at[2]))
        )
    ]
    for copy in loads:
        copy.start()
    saves = [
        pltpu.make_async_copy(src, dst, save.at[at])
        for at, (src, dst) in enumerate(
            (
                (wide.at[0], gk_out),
                (wide.at[1], gv_out),
                (held.at[0], dq_out),
                (held.at[1], dk_out),
                (held.at[2], dv_out),
            )
        )
    ]
    loads[0].wait()
    wide[...] = low[...].astype(jnp.float32)
    saves[0].start()
    saves[1].start()
    for ready, copy in zip(loads[1:], saves[2:]):
        ready.wait()
        copy.start()
    for copy in saves:
        copy.wait()


def whole_heads(peers, queries, keys, values, outputs, grad_out, log_norm, glob_keys, glob_values):
    row_count, col_count = queries.shape
    tokens = peers * BLOCK
    low, full = jnp.bfloat16, jnp.float32
    head_peers = lax.axis_size("head")
    members = peers // CLASSES
    far = (HALVES * CLASSES, members * BLOCK + GLOB, members * HALF)
    near = (HALVES * peers // PAIR, (PAIR + 1) * BLOCK, PAIR * HALF)
    result = jax.ShapeDtypeStruct((row_count, col_count), low)
    scores = tokens * (GLOB + (RAND + 3) * BLOCK)
    dq, dk, dv, glob = pl.pallas_call(
        functools.partial(head_kernel, peers),
        out_shape=(
            result,
            result,
            result,
            jax.ShapeDtypeStruct((2, GLOB // peers, col_count), low),
        ),
        in_specs=[pl.BlockSpec(memory_space=pl.ANY)] * 8,
        out_specs=[pl.BlockSpec(memory_space=pl.ANY)] * 4,
        scratch_shapes=[
            pltpu.VMEM((row_count, col_count), low),
            pltpu.VMEM((row_count, col_count), low),
            pltpu.VMEM((row_count, col_count), low),
            pltpu.VMEM(grad_out.shape, low),
            pltpu.VMEM((row_count, col_count), low),
            pltpu.VMEM((row_count, col_count), low),
            pltpu.VMEM((row_count, col_count), low),
            pltpu.VMEM((2, GLOB // peers, col_count), low),
            pltpu.VMEM((tokens, HEAD_DIM), low),
            pltpu.VMEM((tokens + GLOB, HEAD_DIM), low),
            pltpu.VMEM((tokens + GLOB, HEAD_DIM), low),
            pltpu.VMEM((tokens, HEAD_DIM), low),
            pltpu.VMEM((peers, 8, BLOCK), full),
            pltpu.VMEM((peers, 8, BLOCK), full),
            pltpu.VMEM((row_count, col_count), low),
            pltpu.VMEM((row_count, col_count), low),
            pltpu.VMEM(log_norm.shape, full),
            pltpu.VMEM((peers, 8, BLOCK), full),
            pltpu.VMEM((peers, 8, BLOCK), full),
            pltpu.VMEM((HEAD_DIM, tokens + GLOB), low),
            pltpu.VMEM(far, full),
            pltpu.VMEM(far, low),
            pltpu.VMEM(near, full),
            pltpu.VMEM(near, low),
            pltpu.VMEM((HEAD_DIM, tokens), full),
            pltpu.VMEM((tokens + GLOB, HEAD_DIM), full),
            pltpu.VMEM((tokens + GLOB, HEAD_DIM), full),
            pltpu.VMEM((tokens, HEAD_DIM), low),
            pltpu.VMEM((tokens + GLOB, HEAD_DIM), low),
            pltpu.VMEM((tokens + GLOB, HEAD_DIM), low),
            pltpu.VMEM((2, GLOB, HEAD_DIM), low),
            pltpu.SemaphoreType.DMA((12,)),
            pltpu.SemaphoreType.DMA((head_peers,)),
            pltpu.SemaphoreType.DMA((head_peers,)),
            pltpu.SemaphoreType.DMA((IN_KINDS, peers)),
            pltpu.SemaphoreType.DMA((IN_KINDS, peers)),
            pltpu.SemaphoreType.DMA((OUT_KINDS, peers)),
            pltpu.SemaphoreType.DMA((OUT_KINDS, peers)),
        ],
        compiler_params=pltpu.CompilerParams(
            collective_id=0, has_side_effects=True, vmem_limit_bytes=64 * 1024 * 1024
        ),
        cost_estimate=pl.CostEstimate(
            flops=10 * scores * HEAD_DIM, bytes_accessed=4 * 1024 * 1024, transcendentals=scores
        ),
        name="whole_heads",
    )(queries, keys, values, outputs, grad_out, log_norm, glob_keys, glob_values)
    share = jax.ShapeDtypeStruct((GLOB // peers, col_count), full)
    hbm = pl.BlockSpec(memory_space=pltpu.HBM)
    return pl.pallas_call(
        finish_kernel,
        out_shape=(result, result, result, share, share),
        in_specs=[pl.BlockSpec(memory_space=pl.ANY)] * 4,
        out_specs=[hbm] * 5,
        scratch_shapes=[
            pltpu.VMEM((3, row_count, col_count), low),
            pltpu.VMEM((2, GLOB // peers, col_count), low),
            pltpu.VMEM((2, GLOB // peers, col_count), full),
            pltpu.SemaphoreType.DMA((4,)),
            pltpu.SemaphoreType.DMA((5,)),
        ],
        compiler_params=pltpu.CompilerParams(vmem_limit_bytes=64 * 1024 * 1024),
        cost_estimate=pl.CostEstimate(
            flops=0, bytes_accessed=2 * 1024 * 1024, transcendentals=0
        ),
        name="finish",
    )(dq, dk, dv, glob)


def program(mesh):
    peers = mesh.shape["ctx"]

    def body(queries, keys, values, outputs, grad_out, log_norm, glob_keys, glob_values, key_lists):
        row_count, col_count = queries.shape
        one_head_each = (
            row_count == BLOCK
            and col_count == peers * HEAD_DIM
            and peers == CLASSES * (RAND + 1)
            and GLOB % (16 * peers) == 0
        )
        if one_head_each:
            return whole_heads(
                peers, queries, keys, values, outputs, grad_out, log_norm, glob_keys, glob_values
            )
        return shards(
            queries, keys, values, outputs, grad_out, log_norm, glob_keys, glob_values, key_lists
        )

    return body


def solution(mesh):
    in_specs = (
        P("ctx", "head"),
        P("ctx", "head"),
        P("ctx", "head"),
        P("ctx", "head"),
        P(("ctx", "head"), None),
        P("head", "ctx"),
        P(None, "head"),
        P(None, "head"),
        P(),
    )
    out_specs = (
        P("ctx", "head"),
        P("ctx", "head"),
        P("ctx", "head"),
        P("ctx", "head"),
        P("ctx", "head"),
    )
    return jax.shard_map(program(mesh), mesh=mesh, in_specs=in_specs, out_specs=out_specs, check_vma=False)
```

```python
import functools
import math

import jax
import jax.numpy as jnp
from jax import lax
from jax.experimental import pallas as pl
from jax.experimental.pallas import tpu as pltpu
from jax.sharding import PartitionSpec as P

HEAD_DIM = 128
BLOCK = 128
GLOB = 256
RAND = 3
LOG2E = math.log2(math.e)


def extended_2(cells, sides, width):
    for axis, dim in sides:
        count = lax.axis_size(axis)
        ends = count - 1
        head = lax.slice_in_dim(cells, 0, width, axis=dim)
        tail = lax.slice_in_dim(cells, cells.shape[dim] - width, cells.shape[dim], axis=dim)
        cells = jnp.concatenate(
            [
                lax.ppermute(tail, axis, [(i, (i + 1) % count) for i in range(ends)]),
                cells,
                lax.ppermute(head, axis, [((i + 1) % count, i) for i in range(ends)]),
            ],
            axis=dim,
        )
    return cells


def passed_along(value, axis, by):
    peers = lax.axis_size(axis)
    pairs = [(i, i + by) for i in range(peers) if 0 <= i + by < peers]
    return lax.ppermute(value, axis, pairs)


def shifted(value, axis, by):
    peers = lax.axis_size(axis)
    return lax.ppermute(value, axis, [(i, (i + by) % peers) for i in range(peers)])


def tile_grads(query_rows, grad_rows, norm_rows, delta_rows, key_rows, value_rows, keep_mask):
    att_scale = HEAD_DIM ** (-0.5)
    scores = (
        jnp.einsum("nbd,nkd->nbk", query_rows, key_rows, preferred_element_type=jnp.float32)
        * att_scale
    )
    weights = jnp.exp(scores - norm_rows[:, :, None]) * keep_mask[:, None, :]
    dprobs = jnp.einsum("nbd,nkd->nbk", grad_rows, value_rows, preferred_element_type=jnp.float32)
    dscores = weights * (dprobs - delta_rows[:, :, None])
    weights_low = weights.astype(jnp.bfloat16)
    dscores_low = dscores.astype(jnp.bfloat16)
    grad_values = jnp.einsum(
        "nbk,nbd->nkd", weights_low, grad_rows, preferred_element_type=jnp.float32
    )
    grad_keys = (
        jnp.einsum("nbk,nbd->nkd", dscores_low, query_rows, preferred_element_type=jnp.float32)
        * att_scale
    )
    grad_queries = (
        jnp.einsum("nbk,nkd->nbd", dscores_low, key_rows, preferred_element_type=jnp.float32)
        * att_scale
    )
    return (grad_queries, grad_keys, grad_values)


def head_cols(source, head_index):
    return source[:, head_index * HEAD_DIM : (head_index + 1) * HEAD_DIM]


def head_blocks(source, head_index, num_blocks):
    return head_cols(source, head_index).reshape(num_blocks, BLOCK, HEAD_DIM)


def gather_tiles(tile_rows, slot_ids):
    picked = jnp.take(tile_rows, slot_ids, axis=0)
    return picked.reshape(slot_ids.shape[0], slot_ids.shape[1] * BLOCK, HEAD_DIM)


def tile_picker(slot_ids, hit_mask, num_blocks):
    one_hot = (
        slot_ids[:, :, None] == jnp.arange(num_blocks, dtype=jnp.int32)[None, None, :]
    ) & hit_mask[:, :, None]
    return one_hot.astype(jnp.float32)


def add_tiles(picker, flat_grads, num_blocks):
    tiled_grads = flat_grads.reshape(picker.shape[0], picker.shape[1], BLOCK, HEAD_DIM)
    summed = jnp.einsum("nle,nlbd->ebd", picker, tiled_grads, precision=lax.Precision.HIGHEST)
    return summed.reshape(num_blocks * BLOCK, HEAD_DIM)


def tile_keep(hit_mask, extra_cols):
    tile_cols = jnp.repeat(hit_mask.astype(jnp.float32), BLOCK, axis=1)
    return jnp.concatenate(
        [jnp.ones((hit_mask.shape[0], extra_cols), jnp.float32), tile_cols], axis=1
    )


def with_glob(glob_rows, tile_rows):
    spread = glob_rows[None]
    return jnp.concatenate([spread, tile_rows], axis=1)


def shards(queries, keys, values, outputs, grad_out, log_norm, glob_keys, glob_values, key_lists):
    row_count, col_count = queries.shape
    head_count = col_count // HEAD_DIM
    block_count = row_count // BLOCK
    group_count = lax.axis_size("ctx")
    my_group = lax.axis_index("ctx")
    first_block = my_group * block_count
    incoming = lax.all_to_all(grad_out, "head", split_axis=1, concat_axis=0, tiled=True)
    row_delta = jnp.sum(
        (incoming.astype(jnp.float32) * outputs.astype(jnp.float32)).reshape(
            row_count, head_count, HEAD_DIM
        ),
        axis=2,
    ).T
    own_lists = lax.dynamic_slice_in_dim(key_lists, first_block, block_count, 0)
    query_heads = [
        head_blocks(queries, head_index, block_count) for head_index in range(head_count)
    ]
    grad_heads = [
        head_blocks(incoming, head_index, block_count) for head_index in range(head_count)
    ]
    norm_heads = [
        log_norm[head_index].reshape(block_count, BLOCK) for head_index in range(head_count)
    ]
    delta_heads = [
        row_delta[head_index].reshape(block_count, BLOCK) for head_index in range(head_count)
    ]
    extended = extended_2(jnp.stack([keys, values]), (("ctx", 1),), BLOCK)
    ext_blocks = block_count + 2
    near_lists = own_lists[:, :3]
    near_live = near_lists >= 0
    near_slots = jnp.clip(near_lists - (first_block - 1), 0, ext_blocks - 1)
    near_keep = tile_keep(near_live, GLOB)
    near_picker = tile_picker(near_slots, near_live, ext_blocks)
    dq_parts, dk_parts, dv_parts, glob_dk_parts, glob_dv_parts = ([], [], [], [], [])
    for head_index in range(head_count):
        ext_keys = head_blocks(extended[0], head_index, ext_blocks)
        ext_values = head_blocks(extended[1], head_index, ext_blocks)
        key_rows = with_glob(head_cols(glob_keys, head_index), gather_tiles(ext_keys, near_slots))
        value_rows = with_glob(
            head_cols(glob_values, head_index), gather_tiles(ext_values, near_slots)
        )
        grad_q, grad_k, grad_v = tile_grads(
            query_heads[head_index],
            grad_heads[head_index],
            norm_heads[head_index],
            delta_heads[head_index],
            key_rows,
            value_rows,
            near_keep,
        )
        dq_parts.append(grad_q.reshape(row_count, HEAD_DIM))
        glob_dk_parts.append(jnp.sum(grad_k[:, :GLOB], axis=0))
        glob_dv_parts.append(jnp.sum(grad_v[:, :GLOB], axis=0))
        dk_parts.append(add_tiles(near_picker, grad_k[:, GLOB:], ext_blocks))
        dv_parts.append(add_tiles(near_picker, grad_v[:, GLOB:], ext_blocks))
    query_side = jnp.concatenate(dq_parts, axis=1)
    near_side = jnp.stack([jnp.concatenate(dk_parts, axis=1), jnp.concatenate(dv_parts, axis=1)])
    own_grads = near_side[:, BLOCK : BLOCK + row_count]
    for shift_by in (-1, 1):
        rim_piece = near_side[:, :BLOCK] if shift_by < 0 else near_side[:, BLOCK + row_count :]
        arrived = passed_along(rim_piece, "ctx", shift_by)
        if shift_by < 0:
            own_grads = own_grads.at[:, row_count - BLOCK :].add(arrived)
        else:
            own_grads = own_grads.at[:, :BLOCK].add(arrived)
    full_keep = jnp.ones((block_count, BLOCK), jnp.float32)
    all_hit = jnp.ones((block_count, 1), bool)
    own_pair = jnp.stack([keys, values])
    for round_index in range(RAND):
        hop = (round_index + 1) * group_count // (RAND + 1)
        fetched = shifted(own_pair, "ctx", -hop)
        target_first = (my_group + hop) % group_count * block_count
        far_slots = jnp.clip(own_lists[:, 3 + round_index] - target_first, 0, block_count - 1)[
            :, None
        ]
        far_picker = tile_picker(far_slots, all_hit, block_count)
        far_dq, far_dk, far_dv = ([], [], [])
        for head_index in range(head_count):
            far_keys = gather_tiles(head_blocks(fetched[0], head_index, block_count), far_slots)
            far_values = gather_tiles(head_blocks(fetched[1], head_index, block_count), far_slots)
            grad_q, grad_k, grad_v = tile_grads(
                query_heads[head_index],
                grad_heads[head_index],
                norm_heads[head_index],
                delta_heads[head_index],
                far_keys,
                far_values,
                full_keep,
            )
            far_dq.append(grad_q.reshape(row_count, HEAD_DIM))
            far_dk.append(add_tiles(far_picker, grad_k, block_count))
            far_dv.append(add_tiles(far_picker, grad_v, block_count))
        query_side = query_side + jnp.concatenate(far_dq, axis=1)
        far_pair = jnp.stack([jnp.concatenate(far_dk, axis=1), jnp.concatenate(far_dv, axis=1)])
        own_grads = own_grads + shifted(far_pair, "ctx", hop)
    glob_pair = jnp.stack(
        [jnp.concatenate(glob_dk_parts, axis=1), jnp.concatenate(glob_dv_parts, axis=1)]
    )
    summed_all = lax.psum(glob_pair, "ctx")
    share_rows = GLOB // group_count
    own_share = lax.dynamic_slice_in_dim(summed_all, my_group * share_rows, share_rows, 1)
    return (
        query_side.astype(jnp.bfloat16),
        own_grads[0].astype(jnp.bfloat16),
        own_grads[1].astype(jnp.bfloat16),
        own_share[0],
        own_share[1],
    )


HALVES = 2
HALF = BLOCK // HALVES
K_IN, V_IN, NORM_IN, DELTA_IN, Q_IN, G_IN = 0, 1, 2, 3, 4, 4 + HALVES
IN_KINDS = 4 + 2 * HALVES
PAIR = 2
K_OUT, V_OUT, GLOB_OUT, Q_OUT = 0, 1, 2, 3
OUT_KINDS = 3 + HALVES
CLASSES = 2
CONTRACT_LAST = (((1,), (1,)), ((), ()))


def partner(me, flips, peers):
    found, weight = 0, 1
    while weight < peers:
        mine = lax.rem(lax.div(me, weight), 2)
        flip = lax.rem(lax.div(flips, weight), 2)
        found = found + weight * (mine + flip - 2 * mine * flip)
        weight *= 2
    return found


def partners(me, my_head, peers):
    half = peers // 2
    across, beside = list(range(half, peers)), list(range(1, half))
    early, late = [], []
    for step in range(half - 1):
        early += [across[step], beside[step]]
        late += [beside[step], across[step]]
    early, late = early + across[-1:], late + across[-1:]
    turn = lax.rem(lax.div(me, 2) + my_head, 2)
    return [partner(me, first + turn * (second - first), peers) for first, second in zip(early, late)]


def head_kernel(
    peers,
    q_hbm,
    k_hbm,
    v_hbm,
    o_hbm,
    g_hbm,
    norm_hbm,
    gk_hbm,
    gv_hbm,
    dq_hbm,
    dk_hbm,
    dv_hbm,
    glob_hbm,
    q_own,
    k_own,
    v_own,
    g_part,
    dq_out,
    dk_out,
    dv_out,
    glob_out,
    q_all,
    k_all,
    v_all,
    g_all,
    norm_all,
    delta_all,
    g_own,
    o_own,
    norm_own,
    norm_tiles,
    delta_tiles,
    kt_all,
    far_weights,
    far_low,
    near_weights,
    near_low,
    dq_acc,
    dk_acc,
    dv_acc,
    dq_low,
    dk_low,
    dv_low,
    glob_low,
    load_sem,
    spread_send,
    spread_recv,
    in_send,
    in_recv,
    out_send,
    out_recv,
):
    me = lax.axis_index("ctx")
    my_head = lax.axis_index("head")
    head_peers = lax.axis_size("head")
    members = peers // CLASSES
    class_rows = members * BLOCK
    span = class_rows + GLOB
    share = GLOB // peers
    width = q_hbm.shape[1]
    part_rows = g_part.shape[0]
    order = partners(me, my_head, peers)

    def cols(index):
        return pl.ds(pl.multiple_of(index * HEAD_DIM, HEAD_DIM), HEAD_DIM)

    def query_rows(half, index):
        at = half * members * CLASSES * HALF + (index % CLASSES) * members * HALF + (index // CLASSES) * HALF
        return pl.ds(at if isinstance(at, int) else pl.multiple_of(at, HALF), HALF)

    def half_rows(half):
        return pl.ds(half * HALF, HALF)

    def key_rows(index):
        at = (index % CLASSES) * span + (index // CLASSES) * BLOCK
        return pl.ds(at if isinstance(at, int) else pl.multiple_of(at, BLOCK), BLOCK)

    def remote(src, dst, send, recv, **device):
        return pltpu.make_async_remote_copy(
            src_ref=src,
            dst_ref=dst,
            send_sem=send,
            recv_sem=recv,
            device_id=device,
            device_id_type=pl.DeviceIdType.MESH,
        )

    loads = [
        pltpu.make_async_copy(o_hbm, o_own, load_sem.at[0]),
        pltpu.make_async_copy(norm_hbm, norm_own, load_sem.at[1]),
        pltpu.make_async_copy(
            gk_hbm.at[:, cols(me)], k_all.at[pl.ds(class_rows, GLOB)], load_sem.at[2]
        ),
        pltpu.make_async_copy(
            gv_hbm.at[:, cols(me)], v_all.at[pl.ds(class_rows, GLOB)], load_sem.at[3]
        ),
    ]
    firsts = [
        pltpu.make_async_copy(src, dst, load_sem.at[4 + at])
        for at, (src, dst) in enumerate(
            ((g_hbm, g_part), (k_hbm, k_own), (q_hbm, q_own), (v_hbm, v_own))
        )
    ]
    for load in firsts:
        load.start()
    for load in loads:
        load.start()

    barrier = pltpu.get_barrier_semaphore()
    for by in range(1, head_peers):
        pl.semaphore_signal(
            barrier,
            inc=1,
            device_id={"head": lax.rem(my_head + by, head_peers)},
            device_id_type=pl.DeviceIdType.MESH,
        )
    for to in order:
        pl.semaphore_signal(
            barrier,
            inc=1,
            device_id={"ctx": to},
            device_id_type=pl.DeviceIdType.MESH,
        )
    pl.semaphore_wait(barrier, head_peers - 1 + peers - 1)

    sends = []
    firsts[0].wait()

    def my_part():
        return pl.ds(pl.multiple_of(my_head * part_rows, part_rows), part_rows)

    def wide(index):
        return pl.ds(pl.multiple_of(index * width, width), width)

    for by in range(1, head_peers):
        to = lax.rem(my_head + by, head_peers)
        copy = remote(
            g_part.at[:, wide(to)],
            g_own.at[my_part()],
            spread_send.at[by],
            spread_recv.at[my_head],
            head=to,
        )
        copy.start()
        sends.append(copy)
    pltpu.make_async_copy(
        g_part.at[:, wide(my_head)], g_own.at[my_part()], spread_recv.at[my_head]
    ).start()

    def spread_in(kind, src, dst, from_rows, rows):
        for by, to in enumerate(order):
            copy = remote(
                src.at[from_rows, cols(to)],
                dst.at[rows(me)],
                in_send.at[kind, by],
                in_recv.at[kind, me],
                ctx=to,
            )
            copy.start()
            sends.append(copy)
        pltpu.make_async_copy(
            src.at[from_rows, cols(me)], dst.at[rows(me)], in_recv.at[kind, me]
        ).start()

    def arrived(kind, dst, rows):
        for index in range(peers):
            place = dst.at[rows(index)]
            pltpu.make_async_copy(place, place, in_recv.at[kind, index]).wait()

    places = [functools.partial(query_rows, half) for half in range(HALVES)]
    all_rows = pl.ds(0, BLOCK)
    def tiles_in(kind, src, dst):
        for by, to in enumerate(order):
            copy = remote(
                src.at[to], dst.at[me], in_send.at[kind, by], in_recv.at[kind, me], ctx=to
            )
            copy.start()
            sends.append(copy)
        pltpu.make_async_copy(src.at[me], dst.at[me], in_recv.at[kind, me]).start()

    def tiles_arrived(kind, dst):
        for index in range(peers):
            place = dst.at[index]
            pltpu.make_async_copy(place, place, in_recv.at[kind, index]).wait()

    firsts[1].wait()
    spread_in(K_IN, k_own, k_all, all_rows, key_rows)
    firsts[2].wait()
    spread_in(Q_IN, q_own, q_all, half_rows(0), places[0])
    loads[1].wait()
    for index in range(peers):
        norm = norm_own[pl.ds(index, 1), :] * LOG2E
        norm_tiles[index] = jnp.broadcast_to(norm, (8, BLOCK))
    tiles_in(NORM_IN, norm_tiles, norm_all)
    for half in range(1, HALVES):
        spread_in(Q_IN + half, q_own, q_all, half_rows(half), places[half])
    firsts[3].wait()
    spread_in(V_IN, v_own, v_all, all_rows, key_rows)

    loads[0].wait()
    for index in range(head_peers):
        place = g_own.at[pl.ds(index * part_rows, part_rows)]
        pltpu.make_async_copy(place, place, spread_recv.at[index]).wait()
    spread_in(G_IN, g_own, g_all, half_rows(0), places[0])
    ones = jnp.ones((8, HEAD_DIM), jnp.float32)
    for index in range(peers):
        lanes = pl.ds(index * HEAD_DIM, HEAD_DIM)
        product = g_own[:, lanes].astype(jnp.float32) * o_own[:, lanes].astype(jnp.float32)
        delta_tiles[index] = lax.dot_general(
            ones,
            product,
            CONTRACT_LAST,
            precision=lax.Precision.HIGHEST,
            preferred_element_type=jnp.float32,
        )
    tiles_in(DELTA_IN, delta_tiles, delta_all)
    for half in range(1, HALVES):
        spread_in(G_IN + half, g_own, g_all, half_rows(half), places[half])

    scale = HEAD_DIM**-0.5

    def dot(left, right):
        return jnp.dot(left, right, preferred_element_type=jnp.float32)

    def row_of(tiles, half, blocks):
        return jnp.concatenate(
            [tiles[block, 0:1, half * HALF : (half + 1) * HALF] for block in blocks], axis=1
        )

    def rows_of(half, blocks):
        return pl.ds(query_rows(half, blocks[0]).start, len(blocks) * HALF)

    def weigh(half, blocks, key_at, key_count, keep, full, low):
        rows = rows_of(half, blocks)
        keys = pl.ds(key_at, key_count)
        scores = lax.dot_general(
            k_all[keys, :], q_all[rows, :], CONTRACT_LAST, preferred_element_type=jnp.float32
        )
        weights = jnp.exp2(scores * (scale * LOG2E) - row_of(norm_all, half, blocks))
        if keep is not None:
            weights = jnp.where(keep, weights, 0.0)
        full[pl.ds(0, key_count), :] = weights
        low[pl.ds(0, key_count), :] = weights.astype(jnp.bfloat16)

    def push_values(half, blocks, key_at, key_count, full, low):
        rows = rows_of(half, blocks)
        keys = pl.ds(key_at, key_count)
        dv_acc[keys, :] += dot(low[pl.ds(0, key_count), :], g_all[rows, :])

    def push_scores(half, blocks, key_at, key_count, full, low):
        rows = rows_of(half, blocks)
        keys = pl.ds(key_at, key_count)
        dprobs = lax.dot_general(
            v_all[keys, :], g_all[rows, :], CONTRACT_LAST, preferred_element_type=jnp.float32
        )
        weights = full[pl.ds(0, key_count), :]
        dscores = (weights * (dprobs - row_of(delta_all, half, blocks))).astype(jnp.bfloat16)
        dk_acc[keys, :] += dot(dscores, q_all[rows, :])
        dq_acc[:, rows] += dot(kt_all[:, keys], dscores)

    def pairs(part):
        return [
            [part + CLASSES * (at + step) for step in range(PAIR)]
            for at in range(0, members, PAIR)
        ]

    def near_keys(blocks):
        return [at for at in range(blocks[0] - 1, blocks[-1] + 2, CLASSES) if 0 <= at < peers]

    def near_slot(half, blocks):
        part, at = blocks[0] % CLASSES, blocks[0] // CLASSES // PAIR
        slot = (half * CLASSES + part) * (members // PAIR) + at
        return near_weights.at[slot], near_low.at[slot]

    def weigh_near(half, blocks):
        near = near_keys(blocks)
        shape = (len(near) * BLOCK, len(blocks) * HALF)
        key_block = near[0] + CLASSES * (lax.broadcasted_iota(jnp.int32, shape, 0) // BLOCK)
        query_block = blocks[0] + CLASSES * (lax.broadcasted_iota(jnp.int32, shape, 1) // HALF)
        keep = jnp.abs(key_block - query_block) == 1
        at = key_rows(near[0]).start
        weigh(half, blocks, at, len(near) * BLOCK, keep, *near_slot(half, blocks))

    def push_near(push, half, part):
        for blocks in pairs(part):
            near = near_keys(blocks)
            at = key_rows(near[0]).start
            push(half, blocks, at, len(near) * BLOCK, *near_slot(half, blocks))

    def class_blocks(part):
        return [part + CLASSES * at for at in range(members)]

    def far_slot(half, part):
        return far_weights.at[half * CLASSES + part], far_low.at[half * CLASSES + part]

    def put(kind, src, dst, from_rows, to_rows):
        for by, to in enumerate(order):
            copy = remote(
                src.at[from_rows(to)],
                dst.at[to_rows, cols(me)],
                out_send.at[kind, by],
                out_recv.at[kind, me],
                ctx=to,
            )
            copy.start()
            sends.append(copy)
        pltpu.make_async_copy(
            src.at[from_rows(me)], dst.at[to_rows, cols(me)], out_recv.at[kind, me]
        ).start()

    def push_all(push, half):
        for part in range(CLASSES):
            push_near(push, half, part)
            push(half, class_blocks(part), part * class_rows, span, *far_slot(half, part))

    dk_acc[...] = jnp.zeros_like(dk_acc)
    dv_acc[...] = jnp.zeros_like(dv_acc)
    dq_acc[...] = jnp.zeros_like(dq_acc)

    loads[2].wait()
    loads[3].wait()
    arrived(K_IN, k_all, key_rows)
    kt_all[...] = k_all[...].T
    tiles_arrived(NORM_IN, norm_all)
    for half in range(HALVES):
        arrived(Q_IN + half, q_all, places[half])
        for part in range(CLASSES):
            weigh(
                half, class_blocks(part), part * class_rows, span, None, *far_slot(half, part)
            )
            for blocks in pairs(part):
                weigh_near(half, blocks)
    arrived(V_IN, v_all, key_rows)
    tiles_arrived(DELTA_IN, delta_all)

    for half in range(HALVES):
        arrived(G_IN + half, g_all, places[half])
        push_all(push_values, half)
        if half == HALVES - 1:
            dv_low[...] = dv_acc[...].astype(jnp.bfloat16)
            put(V_OUT, dv_low, dv_out, key_rows, all_rows)
        push_all(push_scores, half)
        if half == HALVES - 1:
            dk_low[...] = (dk_acc[...] * scale).astype(jnp.bfloat16)
            put(K_OUT, dk_low, dk_out, key_rows, all_rows)
        rows = pl.ds(half * peers * HALF, peers * HALF)
        dq_low[rows, :] = (dq_acc[:, rows] * scale).T.astype(jnp.bfloat16)
        put(Q_OUT + half, dq_low, dq_out, places[half], half_rows(half))

    middle = pl.ds(class_rows, GLOB)

    def share_of(index):
        return glob_low.at[:, pl.ds(pl.multiple_of(index * share, share), share), :]

    glob_low[0] = dk_low[middle, :]
    glob_low[1] = dv_low[middle, :]
    for by, to in enumerate(order):
        copy = remote(
            share_of(to),
            glob_out.at[:, :, cols(me)],
            out_send.at[GLOB_OUT, by],
            out_recv.at[GLOB_OUT, me],
            ctx=to,
        )
        copy.start()
        sends.append(copy)
    pltpu.make_async_copy(
        share_of(me), glob_out.at[:, :, cols(me)], out_recv.at[GLOB_OUT, me]
    ).start()

    stores = []

    def store(at, src, dst):
        copy = pltpu.make_async_copy(src, dst, load_sem.at[8 + at])
        copy.start()
        stores.append(copy)

    for at, (kind, dst, home) in enumerate(((V_OUT, dv_out, dv_hbm), (K_OUT, dk_out, dk_hbm))):
        for index in range(peers):
            place = dst.at[:, cols(index)]
            pltpu.make_async_copy(place, place, out_recv.at[kind, index]).wait()
        store(1 + at, dst, home)
    for half in range(HALVES):
        for index in range(peers):
            place = dq_out.at[half_rows(half), cols(index)]
            pltpu.make_async_copy(place, place, out_recv.at[Q_OUT + half, index]).wait()
    store(0, dq_out, dq_hbm)
    for index in range(peers):
        place = glob_out.at[:, :, cols(index)]
        pltpu.make_async_copy(place, place, out_recv.at[GLOB_OUT, index]).wait()
    store(3, glob_out, glob_hbm)

    for copy in sends:
        copy.wait_send()
    for copy in stores:
        copy.wait()


def finish_kernel(
    dq_in, dk_in, dv_in, glob_in, dq_out, dk_out, dv_out, gk_out, gv_out, held, low, wide, load, save
):
    loads = [
        pltpu.make_async_copy(src, dst, load.at[at])
        for at, (src, dst) in enumerate(
            ((glob_in, low), (dq_in, held.at[0]), (dk_in, held.at[1]), (dv_in, held.at[2]))
        )
    ]
    for copy in loads:
        copy.start()
    saves = [
        pltpu.make_async_copy(src, dst, save.at[at])
        for at, (src, dst) in enumerate(
            (
                (wide.at[0], gk_out),
                (wide.at[1], gv_out),
                (held.at[0], dq_out),
                (held.at[1], dk_out),
                (held.at[2], dv_out),
            )
        )
    ]
    loads[0].wait()
    wide[...] = low[...].astype(jnp.float32)
    saves[0].start()
    saves[1].start()
    for ready, copy in zip(loads[1:], saves[2:]):
        ready.wait()
        copy.start()
    for copy in saves:
        copy.wait()


def whole_heads(peers, queries, keys, values, outputs, grad_out, log_norm, glob_keys, glob_values):
    row_count, col_count = queries.shape
    tokens = peers * BLOCK
    low, full = jnp.bfloat16, jnp.float32
    head_peers = lax.axis_size("head")
    members = peers // CLASSES
    far = (HALVES * CLASSES, members * BLOCK + GLOB, members * HALF)
    near = (HALVES * peers // PAIR, (PAIR + 1) * BLOCK, PAIR * HALF)
    result = jax.ShapeDtypeStruct((row_count, col_count), low)
    scores = tokens * (GLOB + (RAND + 3) * BLOCK)
    dq, dk, dv, glob = pl.pallas_call(
        functools.partial(head_kernel, peers),
        out_shape=(
            result,
            result,
            result,
            jax.ShapeDtypeStruct((2, GLOB // peers, col_count), low),
        ),
        in_specs=[pl.BlockSpec(memory_space=pl.ANY)] * 8,
        out_specs=[pl.BlockSpec(memory_space=pl.ANY)] * 4,
        scratch_shapes=[
            pltpu.VMEM((row_count, col_count), low),
            pltpu.VMEM((row_count, col_count), low),
            pltpu.VMEM((row_count, col_count), low),
            pltpu.VMEM(grad_out.shape, low),
            pltpu.VMEM((row_count, col_count), low),
            pltpu.VMEM((row_count, col_count), low),
            pltpu.VMEM((row_count, col_count), low),
            pltpu.VMEM((2, GLOB // peers, col_count), low),
            pltpu.VMEM((tokens, HEAD_DIM), low),
            pltpu.VMEM((tokens + GLOB, HEAD_DIM), low),
            pltpu.VMEM((tokens + GLOB, HEAD_DIM), low),
            pltpu.VMEM((tokens, HEAD_DIM), low),
            pltpu.VMEM((peers, 8, BLOCK), full),
            pltpu.VMEM((peers, 8, BLOCK), full),
            pltpu.VMEM((row_count, col_count), low),
            pltpu.VMEM((row_count, col_count), low),
            pltpu.VMEM(log_norm.shape, full),
            pltpu.VMEM((peers, 8, BLOCK), full),
            pltpu.VMEM((peers, 8, BLOCK), full),
            pltpu.VMEM((HEAD_DIM, tokens + GLOB), low),
            pltpu.VMEM(far, full),
            pltpu.VMEM(far, low),
            pltpu.VMEM(near, full),
            pltpu.VMEM(near, low),
            pltpu.VMEM((HEAD_DIM, tokens), full),
            pltpu.VMEM((tokens + GLOB, HEAD_DIM), full),
            pltpu.VMEM((tokens + GLOB, HEAD_DIM), full),
            pltpu.VMEM((tokens, HEAD_DIM), low),
            pltpu.VMEM((tokens + GLOB, HEAD_DIM), low),
            pltpu.VMEM((tokens + GLOB, HEAD_DIM), low),
            pltpu.VMEM((2, GLOB, HEAD_DIM), low),
            pltpu.SemaphoreType.DMA((12,)),
            pltpu.SemaphoreType.DMA((head_peers,)),
            pltpu.SemaphoreType.DMA((head_peers,)),
            pltpu.SemaphoreType.DMA((IN_KINDS, peers)),
            pltpu.SemaphoreType.DMA((IN_KINDS, peers)),
            pltpu.SemaphoreType.DMA((OUT_KINDS, peers)),
            pltpu.SemaphoreType.DMA((OUT_KINDS, peers)),
        ],
        compiler_params=pltpu.CompilerParams(
            collective_id=0, has_side_effects=True, vmem_limit_bytes=64 * 1024 * 1024
        ),
        cost_estimate=pl.CostEstimate(
            flops=10 * scores * HEAD_DIM, bytes_accessed=4 * 1024 * 1024, transcendentals=scores
        ),
        name="whole_heads",
    )(queries, keys, values, outputs, grad_out, log_norm, glob_keys, glob_values)
    share = jax.ShapeDtypeStruct((GLOB // peers, col_count), full)
    hbm = pl.BlockSpec(memory_space=pltpu.HBM)
    return pl.pallas_call(
        finish_kernel,
        out_shape=(result, result, result, share, share),
        in_specs=[pl.BlockSpec(memory_space=pl.ANY)] * 4,
        out_specs=[hbm] * 5,
        scratch_shapes=[
            pltpu.VMEM((3, row_count, col_count), low),
            pltpu.VMEM((2, GLOB // peers, col_count), low),
            pltpu.VMEM((2, GLOB // peers, col_count), full),
            pltpu.SemaphoreType.DMA((4,)),
            pltpu.SemaphoreType.DMA((5,)),
        ],
        compiler_params=pltpu.CompilerParams(vmem_limit_bytes=64 * 1024 * 1024),
        cost_estimate=pl.CostEstimate(
            flops=0, bytes_accessed=2 * 1024 * 1024, transcendentals=0
        ),
        name="finish",
    )(dq, dk, dv, glob)


def program(mesh):
    peers = mesh.shape["ctx"]

    def body(queries, keys, values, outputs, grad_out, log_norm, glob_keys, glob_values, key_lists):
        row_count, col_count = queries.shape
        one_head_each = (
            row_count == BLOCK
            and col_count == peers * HEAD_DIM
            and peers == CLASSES * (RAND + 1)
            and GLOB % (16 * peers) == 0
        )
        if one_head_each:
            return whole_heads(
                peers, queries, keys, values, outputs, grad_out, log_norm, glob_keys, glob_values
            )
        return shards(
            queries, keys, values, outputs, grad_out, log_norm, glob_keys, glob_values, key_lists
        )

    return body


def solution(mesh):
    in_specs = (
        P("ctx", "head"),
        P("ctx", "head"),
        P("ctx", "head"),
        P("ctx", "head"),
        P(("ctx", "head"), None),
        P("head", "ctx"),
        P(None, "head"),
        P(None, "head"),
        P(),
    )
    out_specs = (
        P("ctx", "head"),
        P("ctx", "head"),
        P("ctx", "head"),
        P("ctx", "head"),
        P("ctx", "head"),
    )
    return jax.shard_map(program(mesh), mesh=mesh, in_specs=in_specs, out_specs=out_specs, check_vma=False)
```

```python
import functools
import math

import jax
import jax.numpy as jnp
from jax import lax
from jax.experimental import pallas as pl
from jax.experimental.pallas import tpu as pltpu
from jax.sharding import PartitionSpec as P

HEAD_DIM = 128
BLOCK = 128
GLOB = 256
RAND = 3
LOG2E = math.log2(math.e)


def extended_2(cells, sides, width):
    for axis, dim in sides:
        count = lax.axis_size(axis)
        ends = count - 1
        head = lax.slice_in_dim(cells, 0, width, axis=dim)
        tail = lax.slice_in_dim(cells, cells.shape[dim] - width, cells.shape[dim], axis=dim)
        cells = jnp.concatenate(
            [
                lax.ppermute(tail, axis, [(i, (i + 1) % count) for i in range(ends)]),
                cells,
                lax.ppermute(head, axis, [((i + 1) % count, i) for i in range(ends)]),
            ],
            axis=dim,
        )
    return cells


def passed_along(value, axis, by):
    peers = lax.axis_size(axis)
    pairs = [(i, i + by) for i in range(peers) if 0 <= i + by < peers]
    return lax.ppermute(value, axis, pairs)


def shifted(value, axis, by):
    peers = lax.axis_size(axis)
    return lax.ppermute(value, axis, [(i, (i + by) % peers) for i in range(peers)])


def tile_grads(query_rows, grad_rows, norm_rows, delta_rows, key_rows, value_rows, keep_mask):
    att_scale = HEAD_DIM ** (-0.5)
    scores = (
        jnp.einsum("nbd,nkd->nbk", query_rows, key_rows, preferred_element_type=jnp.float32)
        * att_scale
    )
    weights = jnp.exp(scores - norm_rows[:, :, None]) * keep_mask[:, None, :]
    dprobs = jnp.einsum("nbd,nkd->nbk", grad_rows, value_rows, preferred_element_type=jnp.float32)
    dscores = weights * (dprobs - delta_rows[:, :, None])
    weights_low = weights.astype(jnp.bfloat16)
    dscores_low = dscores.astype(jnp.bfloat16)
    grad_values = jnp.einsum(
        "nbk,nbd->nkd", weights_low, grad_rows, preferred_element_type=jnp.float32
    )
    grad_keys = (
        jnp.einsum("nbk,nbd->nkd", dscores_low, query_rows, preferred_element_type=jnp.float32)
        * att_scale
    )
    grad_queries = (
        jnp.einsum("nbk,nkd->nbd", dscores_low, key_rows, preferred_element_type=jnp.float32)
        * att_scale
    )
    return (grad_queries, grad_keys, grad_values)


def head_cols(source, head_index):
    return source[:, head_index * HEAD_DIM : (head_index + 1) * HEAD_DIM]


def head_blocks(source, head_index, num_blocks):
    return head_cols(source, head_index).reshape(num_blocks, BLOCK, HEAD_DIM)


def gather_tiles(tile_rows, slot_ids):
    picked = jnp.take(tile_rows, slot_ids, axis=0)
    return picked.reshape(slot_ids.shape[0], slot_ids.shape[1] * BLOCK, HEAD_DIM)


def tile_picker(slot_ids, hit_mask, num_blocks):
    one_hot = (
        slot_ids[:, :, None] == jnp.arange(num_blocks, dtype=jnp.int32)[None, None, :]
    ) & hit_mask[:, :, None]
    return one_hot.astype(jnp.float32)


def add_tiles(picker, flat_grads, num_blocks):
    tiled_grads = flat_grads.reshape(picker.shape[0], picker.shape[1], BLOCK, HEAD_DIM)
    summed = jnp.einsum("nle,nlbd->ebd", picker, tiled_grads, precision=lax.Precision.HIGHEST)
    return summed.reshape(num_blocks * BLOCK, HEAD_DIM)


def tile_keep(hit_mask, extra_cols):
    tile_cols = jnp.repeat(hit_mask.astype(jnp.float32), BLOCK, axis=1)
    return jnp.concatenate(
        [jnp.ones((hit_mask.shape[0], extra_cols), jnp.float32), tile_cols], axis=1
    )


def with_glob(glob_rows, tile_rows):
    spread = glob_rows[None]
    return jnp.concatenate([spread, tile_rows], axis=1)


def shards(queries, keys, values, outputs, grad_out, log_norm, glob_keys, glob_values, key_lists):
    row_count, col_count = queries.shape
    head_count = col_count // HEAD_DIM
    block_count = row_count // BLOCK
    group_count = lax.axis_size("ctx")
    my_group = lax.axis_index("ctx")
    first_block = my_group * block_count
    incoming = lax.all_to_all(grad_out, "head", split_axis=1, concat_axis=0, tiled=True)
    row_delta = jnp.sum(
        (incoming.astype(jnp.float32) * outputs.astype(jnp.float32)).reshape(
            row_count, head_count, HEAD_DIM
        ),
        axis=2,
    ).T
    own_lists = lax.dynamic_slice_in_dim(key_lists, first_block, block_count, 0)
    query_heads = [
        head_blocks(queries, head_index, block_count) for head_index in range(head_count)
    ]
    grad_heads = [
        head_blocks(incoming, head_index, block_count) for head_index in range(head_count)
    ]
    norm_heads = [
        log_norm[head_index].reshape(block_count, BLOCK) for head_index in range(head_count)
    ]
    delta_heads = [
        row_delta[head_index].reshape(block_count, BLOCK) for head_index in range(head_count)
    ]
    extended = extended_2(jnp.stack([keys, values]), (("ctx", 1),), BLOCK)
    ext_blocks = block_count + 2
    near_lists = own_lists[:, :3]
    near_live = near_lists >= 0
    near_slots = jnp.clip(near_lists - (first_block - 1), 0, ext_blocks - 1)
    near_keep = tile_keep(near_live, GLOB)
    near_picker = tile_picker(near_slots, near_live, ext_blocks)
    dq_parts, dk_parts, dv_parts, glob_dk_parts, glob_dv_parts = ([], [], [], [], [])
    for head_index in range(head_count):
        ext_keys = head_blocks(extended[0], head_index, ext_blocks)
        ext_values = head_blocks(extended[1], head_index, ext_blocks)
        key_rows = with_glob(head_cols(glob_keys, head_index), gather_tiles(ext_keys, near_slots))
        value_rows = with_glob(
            head_cols(glob_values, head_index), gather_tiles(ext_values, near_slots)
        )
        grad_q, grad_k, grad_v = tile_grads(
            query_heads[head_index],
            grad_heads[head_index],
            norm_heads[head_index],
            delta_heads[head_index],
            key_rows,
            value_rows,
            near_keep,
        )
        dq_parts.append(grad_q.reshape(row_count, HEAD_DIM))
        glob_dk_parts.append(jnp.sum(grad_k[:, :GLOB], axis=0))
        glob_dv_parts.append(jnp.sum(grad_v[:, :GLOB], axis=0))
        dk_parts.append(add_tiles(near_picker, grad_k[:, GLOB:], ext_blocks))
        dv_parts.append(add_tiles(near_picker, grad_v[:, GLOB:], ext_blocks))
    query_side = jnp.concatenate(dq_parts, axis=1)
    near_side = jnp.stack([jnp.concatenate(dk_parts, axis=1), jnp.concatenate(dv_parts, axis=1)])
    own_grads = near_side[:, BLOCK : BLOCK + row_count]
    for shift_by in (-1, 1):
        rim_piece = near_side[:, :BLOCK] if shift_by < 0 else near_side[:, BLOCK + row_count :]
        arrived = passed_along(rim_piece, "ctx", shift_by)
        if shift_by < 0:
            own_grads = own_grads.at[:, row_count - BLOCK :].add(arrived)
        else:
            own_grads = own_grads.at[:, :BLOCK].add(arrived)
    full_keep = jnp.ones((block_count, BLOCK), jnp.float32)
    all_hit = jnp.ones((block_count, 1), bool)
    own_pair = jnp.stack([keys, values])
    for round_index in range(RAND):
        hop = (round_index + 1) * group_count // (RAND + 1)
        fetched = shifted(own_pair, "ctx", -hop)
        target_first = (my_group + hop) % group_count * block_count
        far_slots = jnp.clip(own_lists[:, 3 + round_index] - target_first, 0, block_count - 1)[
            :, None
        ]
        far_picker = tile_picker(far_slots, all_hit, block_count)
        far_dq, far_dk, far_dv = ([], [], [])
        for head_index in range(head_count):
            far_keys = gather_tiles(head_blocks(fetched[0], head_index, block_count), far_slots)
            far_values = gather_tiles(head_blocks(fetched[1], head_index, block_count), far_slots)
            grad_q, grad_k, grad_v = tile_grads(
                query_heads[head_index],
                grad_heads[head_index],
                norm_heads[head_index],
                delta_heads[head_index],
                far_keys,
                far_values,
                full_keep,
            )
            far_dq.append(grad_q.reshape(row_count, HEAD_DIM))
            far_dk.append(add_tiles(far_picker, grad_k, block_count))
            far_dv.append(add_tiles(far_picker, grad_v, block_count))
        query_side = query_side + jnp.concatenate(far_dq, axis=1)
        far_pair = jnp.stack([jnp.concatenate(far_dk, axis=1), jnp.concatenate(far_dv, axis=1)])
        own_grads = own_grads + shifted(far_pair, "ctx", hop)
    glob_pair = jnp.stack(
        [jnp.concatenate(glob_dk_parts, axis=1), jnp.concatenate(glob_dv_parts, axis=1)]
    )
    summed_all = lax.psum(glob_pair, "ctx")
    share_rows = GLOB // group_count
    own_share = lax.dynamic_slice_in_dim(summed_all, my_group * share_rows, share_rows, 1)
    return (
        query_side.astype(jnp.bfloat16),
        own_grads[0].astype(jnp.bfloat16),
        own_grads[1].astype(jnp.bfloat16),
        own_share[0],
        own_share[1],
    )


HALVES = 2
HALF = BLOCK // HALVES
K_IN, V_IN, S_IN, Q_IN, G_IN = 0, 1, 2, 3, 3 + HALVES
IN_KINDS = 3 + 2 * HALVES
K_OUT, V_OUT, GLOB_OUT, Q_OUT = 0, 1, 2, 3
OUT_KINDS = 3 + HALVES
CLASSES = 2
CONTRACT_LAST = (((1,), (1,)), ((), ()))


def start_order(peers):
    half = peers // 2
    return [half] + [half + sign * by for by in range(1, half) for sign in (-1, 1)]


def head_kernel(
    peers,
    q_hbm,
    k_hbm,
    v_hbm,
    o_hbm,
    g_hbm,
    norm_hbm,
    gk_hbm,
    gv_hbm,
    dq_hbm,
    dk_hbm,
    dv_hbm,
    glob_hbm,
    q_own,
    k_own,
    v_own,
    g_part,
    dq_out,
    dk_out,
    dv_out,
    glob_out,
    q_all,
    k_all,
    v_all,
    g_all,
    stat_all,
    g_own,
    o_own,
    norm_own,
    stat_own,
    g_tiles,
    kt_all,
    dq_acc,
    dk_acc,
    dv_acc,
    dq_low,
    dk_low,
    dv_low,
    glob_low,
    load_sem,
    tile_sem,
    store_sem,
    spread_send,
    spread_recv,
    in_send,
    in_recv,
    out_send,
    out_recv,
):
    me = lax.axis_index("ctx")
    my_head = lax.axis_index("head")
    head_peers = lax.axis_size("head")
    members = peers // CLASSES
    class_rows = members * BLOCK
    span = class_rows + GLOB
    share = GLOB // peers
    width = q_hbm.shape[1]
    part_rows = g_part.shape[0]
    order = start_order(peers)

    def cols(index):
        return pl.ds(pl.multiple_of(index * HEAD_DIM, HEAD_DIM), HEAD_DIM)

    def query_rows(half, index):
        at = half * members * CLASSES * HALF + (index % CLASSES) * members * HALF + (index // CLASSES) * HALF
        return pl.ds(at if isinstance(at, int) else pl.multiple_of(at, HALF), HALF)

    def half_rows(half):
        return pl.ds(half * HALF, HALF)

    def key_rows(index):
        at = (index % CLASSES) * span + (index // CLASSES) * BLOCK
        return pl.ds(at if isinstance(at, int) else pl.multiple_of(at, BLOCK), BLOCK)

    def remote(src, dst, send, recv, **device):
        return pltpu.make_async_remote_copy(
            src_ref=src,
            dst_ref=dst,
            send_sem=send,
            recv_sem=recv,
            device_id=device,
            device_id_type=pl.DeviceIdType.MESH,
        )

    loads = [
        pltpu.make_async_copy(o_hbm, o_own, load_sem.at[0]),
        pltpu.make_async_copy(norm_hbm, norm_own, load_sem.at[1]),
        pltpu.make_async_copy(
            gk_hbm.at[:, cols(me)], k_all.at[pl.ds(class_rows, GLOB)], load_sem.at[2]
        ),
        pltpu.make_async_copy(
            gv_hbm.at[:, cols(me)], v_all.at[pl.ds(class_rows, GLOB)], load_sem.at[3]
        ),
    ]
    for load in loads:
        load.start()
    spread_load = pltpu.make_async_copy(g_hbm, g_part, load_sem.at[4])
    spread_load.start()

    def tile_loads(at, src, dst):
        copies = [
            pltpu.make_async_copy(src.at[:, cols(index)], dst.at[index], tile_sem.at[at, index])
            for index in range(peers)
        ]
        for copy in copies:
            copy.start()
        return copies

    k_loads = tile_loads(0, k_hbm, k_own)
    q_loads = tile_loads(1, q_hbm, q_own)
    v_loads = tile_loads(2, v_hbm, v_own)

    barrier = pltpu.get_barrier_semaphore()
    for by in range(1, head_peers):
        pl.semaphore_signal(
            barrier,
            inc=1,
            device_id={"head": lax.rem(my_head + by, head_peers)},
            device_id_type=pl.DeviceIdType.MESH,
        )
    for by in order:
        pl.semaphore_signal(
            barrier,
            inc=1,
            device_id={"ctx": lax.rem(me + by, peers)},
            device_id_type=pl.DeviceIdType.MESH,
        )
    pl.semaphore_wait(barrier, head_peers - 1 + peers - 1)

    sends = []
    spread_load.wait()

    def my_part():
        return pl.ds(pl.multiple_of(my_head * part_rows, part_rows), part_rows)

    def wide(index):
        return pl.ds(pl.multiple_of(index * width, width), width)

    for by in range(1, head_peers):
        to = lax.rem(my_head + by, head_peers)
        copy = remote(
            g_part.at[:, wide(to)],
            g_own.at[my_part()],
            spread_send.at[by],
            spread_recv.at[my_head],
            head=to,
        )
        copy.start()
        sends.append(copy)
    pltpu.make_async_copy(
        g_part.at[:, wide(my_head)], g_own.at[my_part()], spread_recv.at[my_head]
    ).start()

    def spread_in(kind, src, dst, from_rows, rows):
        for by in order:
            to = lax.rem(me + by, peers)
            copy = remote(
                src.at[to, from_rows],
                dst.at[rows(me)],
                in_send.at[kind, by],
                in_recv.at[kind, me],
                ctx=to,
            )
            copy.start()
            sends.append(copy)
        pltpu.make_async_copy(
            src.at[me, from_rows], dst.at[rows(me)], in_recv.at[kind, me]
        ).start()

    def arrived(kind, dst, rows):
        for index in range(peers):
            place = dst.at[rows(index)]
            pltpu.make_async_copy(place, place, in_recv.at[kind, index]).wait()

    places = [functools.partial(query_rows, half) for half in range(HALVES)]
    all_rows = pl.ds(0, BLOCK)
    for load in k_loads:
        load.wait()
    spread_in(K_IN, k_own, k_all, all_rows, key_rows)
    for load in q_loads:
        load.wait()
    spread_in(Q_IN, q_own, q_all, half_rows(0), places[0])
    for load in v_loads:
        load.wait()
    spread_in(V_IN, v_own, v_all, all_rows, key_rows)

    loads[0].wait()
    loads[1].wait()
    for index in range(head_peers):
        place = g_own.at[pl.ds(index * part_rows, part_rows)]
        pltpu.make_async_copy(place, place, spread_recv.at[index]).wait()
    for index in range(peers):
        g_tiles[index] = g_own[:, pl.ds(index * HEAD_DIM, HEAD_DIM)]
    spread_in(G_IN, g_tiles, g_all, half_rows(0), places[0])
    ones = jnp.ones((8, HEAD_DIM), jnp.float32)
    first = lax.broadcasted_iota(jnp.int32, (8, BLOCK), 0) == 0
    for index in range(peers):
        lanes = pl.ds(index * HEAD_DIM, HEAD_DIM)
        product = g_own[:, lanes].astype(jnp.float32) * o_own[:, lanes].astype(jnp.float32)
        delta = lax.dot_general(
            ones,
            product,
            CONTRACT_LAST,
            precision=lax.Precision.HIGHEST,
            preferred_element_type=jnp.float32,
        )
        norm = jnp.broadcast_to(norm_own[pl.ds(index, 1), :], (8, BLOCK))
        stat_own[index] = jnp.where(first, norm * LOG2E, delta)
    for by in order:
        to = lax.rem(me + by, peers)
        copy = remote(
            stat_own.at[to], stat_all.at[me], in_send.at[S_IN, by], in_recv.at[S_IN, me], ctx=to
        )
        copy.start()
        sends.append(copy)
    pltpu.make_async_copy(stat_own.at[me], stat_all.at[me], in_recv.at[S_IN, me]).start()

    for half in range(1, HALVES):
        spread_in(Q_IN + half, q_own, q_all, half_rows(half), places[half])
        spread_in(G_IN + half, g_tiles, g_all, half_rows(half), places[half])

    scale = HEAD_DIM**-0.5

    def dot(left, right):
        return jnp.dot(left, right, preferred_element_type=jnp.float32)

    def visit(half, blocks, key_at, key_count, keep):
        rows = pl.ds(query_rows(half, blocks[0]).start, len(blocks) * HALF)
        keys = pl.ds(key_at, key_count)
        norm, delta = (
            jnp.concatenate(
                [stat_all[block, row : row + 1, half * HALF : (half + 1) * HALF] for block in blocks],
                axis=1,
            )
            for row in range(2)
        )
        scores = lax.dot_general(
            k_all[keys, :], q_all[rows, :], CONTRACT_LAST, preferred_element_type=jnp.float32
        )
        weights = jnp.exp2(scores * (scale * LOG2E) - norm)
        if keep is not None:
            weights = jnp.where(keep, weights, 0.0)
        dprobs = lax.dot_general(
            v_all[keys, :], g_all[rows, :], CONTRACT_LAST, preferred_element_type=jnp.float32
        )
        dscores = (weights * (dprobs - delta)).astype(jnp.bfloat16)
        dq_acc[:, rows] += dot(kt_all[:, keys], dscores)
        dk_acc[keys, :] += dot(dscores, q_all[rows, :])
        dv_acc[keys, :] += dot(weights.astype(jnp.bfloat16), g_all[rows, :])

    def visit_near(half, blocks):
        near = [at for at in range(blocks[0] - 1, blocks[-1] + 2, CLASSES) if 0 <= at < peers]
        shape = (len(near) * BLOCK, len(blocks) * HALF)
        key_block = near[0] + CLASSES * (lax.broadcasted_iota(jnp.int32, shape, 0) // BLOCK)
        query_block = blocks[0] + CLASSES * (lax.broadcasted_iota(jnp.int32, shape, 1) // HALF)
        keep = jnp.abs(key_block - query_block) == 1
        visit(half, blocks, key_rows(near[0]).start, len(near) * BLOCK, keep)

    def put(kind, src, dst, from_rows, to_rows, block):
        @pl.when(me == block)
        def _():
            pltpu.make_async_copy(
                src.at[from_rows], dst.at[me, to_rows], out_recv.at[kind, me]
            ).start()

        @pl.when(me != block)
        def _():
            remote(
                src.at[from_rows],
                dst.at[me, to_rows],
                out_send.at[kind, block],
                out_recv.at[kind, me],
                ctx=block,
            ).start()

    dk_acc[...] = jnp.zeros_like(dk_acc)
    dv_acc[...] = jnp.zeros_like(dv_acc)
    dq_acc[...] = jnp.zeros_like(dq_acc)

    loads[2].wait()
    loads[3].wait()
    arrived(K_IN, k_all, key_rows)
    kt_all[...] = k_all[...].T
    arrived(V_IN, v_all, key_rows)
    for index in range(peers):
        place = stat_all.at[index]
        pltpu.make_async_copy(place, place, in_recv.at[S_IN, index]).wait()

    pair = 2
    for half in range(HALVES):
        arrived(Q_IN + half, q_all, places[half])
        arrived(G_IN + half, g_all, places[half])
        for part in range(CLASSES):
            for at in range(0, members, pair):
                visit_near(half, [part + CLASSES * (at + step) for step in range(pair)])
        for part in range(CLASSES):
            blocks = [part + CLASSES * at for at in range(members)]
            visit(half, blocks, part * class_rows, span, None)
            rows = pl.ds(query_rows(half, part).start, members * HALF)
            dq_low[rows, :] = (dq_acc[:, rows] * scale).T.astype(jnp.bfloat16)
            for block in blocks:
                put(Q_OUT + half, dq_low, dq_out, query_rows(half, block), half_rows(half), block)
            if half == HALVES - 1:
                own = pl.ds(part * span, class_rows)
                dk_low[own, :] = (dk_acc[own, :] * scale).astype(jnp.bfloat16)
                for block in blocks:
                    put(K_OUT, dk_low, dk_out, key_rows(block), all_rows, block)
                dv_low[own, :] = dv_acc[own, :].astype(jnp.bfloat16)
                for block in blocks:
                    put(V_OUT, dv_low, dv_out, key_rows(block), all_rows, block)

    middle = pl.ds(class_rows, GLOB)
    glob_low[0] = (dk_acc[middle, :] * scale).astype(jnp.bfloat16)
    glob_low[1] = dv_acc[middle, :].astype(jnp.bfloat16)

    def share_of(index):
        return glob_low.at[:, pl.ds(pl.multiple_of(index * share, share), share), :]

    for by in order:
        to = lax.rem(me + by, peers)
        copy = remote(
            share_of(to),
            glob_out.at[me],
            out_send.at[GLOB_OUT, to],
            out_recv.at[GLOB_OUT, me],
            ctx=to,
        )
        copy.start()
        sends.append(copy)
    pltpu.make_async_copy(
        share_of(me), glob_out.at[me], out_recv.at[GLOB_OUT, me]
    ).start()

    stores = []

    def land(kind, src, dst):
        for index in range(peers):
            place = src(index)
            pltpu.make_async_copy(place, place, out_recv.at[kind, index]).wait()
            copy = pltpu.make_async_copy(place, dst(index), store_sem.at[kind, index])
            copy.start()
            stores.append(copy)

    def land_rows(kind, src, dst, rows):
        land(kind, lambda index: src.at[index, rows], lambda index: dst.at[rows, cols(index)])

    for half in range(HALVES):
        land_rows(Q_OUT + half, dq_out, dq_hbm, half_rows(half))
    land_rows(K_OUT, dk_out, dk_hbm, all_rows)
    land_rows(V_OUT, dv_out, dv_hbm, all_rows)
    land(
        GLOB_OUT,
        lambda index: glob_out.at[index],
        lambda index: glob_hbm.at[:, :, cols(index)],
    )

    for copy in sends:
        copy.wait_send()
    halves = [(Q_OUT + half, dq_low, places[half]) for half in range(HALVES)]
    for by in order:
        to = lax.rem(me + by, peers)
        for kind, src, rows in [(K_OUT, dk_low, key_rows), (V_OUT, dv_low, key_rows)] + halves:
            place = src.at[rows(to)]
            pltpu.make_async_copy(place, place, out_send.at[kind, to]).wait()
    for copy in stores:
        copy.wait()


def finish_kernel(
    dq_in, dk_in, dv_in, glob_in, dq_out, dk_out, dv_out, gk_out, gv_out, held, low, wide, load, save
):
    loads = [
        pltpu.make_async_copy(src, dst, load.at[at])
        for at, (src, dst) in enumerate(
            ((glob_in, low), (dq_in, held.at[0]), (dk_in, held.at[1]), (dv_in, held.at[2]))
        )
    ]
    for copy in loads:
        copy.start()
    saves = [
        pltpu.make_async_copy(src, dst, save.at[at])
        for at, (src, dst) in enumerate(
            (
                (wide.at[0], gk_out),
                (wide.at[1], gv_out),
                (held.at[0], dq_out),
                (held.at[1], dk_out),
                (held.at[2], dv_out),
            )
        )
    ]
    loads[0].wait()
    wide[...] = low[...].astype(jnp.float32)
    saves[0].start()
    saves[1].start()
    for ready, copy in zip(loads[1:], saves[2:]):
        ready.wait()
        copy.start()
    for copy in saves:
        copy.wait()


def whole_heads(peers, queries, keys, values, outputs, grad_out, log_norm, glob_keys, glob_values):
    row_count, col_count = queries.shape
    tokens = peers * BLOCK
    low, full = jnp.bfloat16, jnp.float32
    head_peers = lax.axis_size("head")
    tiles = (peers, row_count, HEAD_DIM)
    result = jax.ShapeDtypeStruct((row_count, col_count), low)
    scores = tokens * (GLOB + (RAND + 3) * BLOCK)
    dq, dk, dv, glob = pl.pallas_call(
        functools.partial(head_kernel, peers),
        out_shape=(
            result,
            result,
            result,
            jax.ShapeDtypeStruct((2, GLOB // peers, col_count), low),
        ),
        in_specs=[pl.BlockSpec(memory_space=pl.ANY)] * 8,
        out_specs=[pl.BlockSpec(memory_space=pl.ANY)] * 4,
        scratch_shapes=[
            pltpu.VMEM(tiles, low),
            pltpu.VMEM(tiles, low),
            pltpu.VMEM(tiles, low),
            pltpu.VMEM(grad_out.shape, low),
            pltpu.VMEM(tiles, low),
            pltpu.VMEM(tiles, low),
            pltpu.VMEM(tiles, low),
            pltpu.VMEM((peers, 2, GLOB // peers, HEAD_DIM), low),
            pltpu.VMEM((tokens, HEAD_DIM), low),
            pltpu.VMEM((tokens + GLOB, HEAD_DIM), low),
            pltpu.VMEM((tokens + GLOB, HEAD_DIM), low),
            pltpu.VMEM((tokens, HEAD_DIM), low),
            pltpu.VMEM((peers, 8, BLOCK), full),
            pltpu.VMEM((row_count, col_count), low),
            pltpu.VMEM((row_count, col_count), low),
            pltpu.VMEM(log_norm.shape, full),
            pltpu.VMEM((peers, 8, BLOCK), full),
            pltpu.VMEM(tiles, low),
            pltpu.VMEM((HEAD_DIM, tokens + GLOB), low),
            pltpu.VMEM((HEAD_DIM, tokens), full),
            pltpu.VMEM((tokens + GLOB, HEAD_DIM), full),
            pltpu.VMEM((tokens + GLOB, HEAD_DIM), full),
            pltpu.VMEM((tokens, HEAD_DIM), low),
            pltpu.VMEM((tokens + GLOB, HEAD_DIM), low),
            pltpu.VMEM((tokens + GLOB, HEAD_DIM), low),
            pltpu.VMEM((2, GLOB, HEAD_DIM), low),
            pltpu.SemaphoreType.DMA((5,)),
            pltpu.SemaphoreType.DMA((3, peers)),
            pltpu.SemaphoreType.DMA((OUT_KINDS, peers)),
            pltpu.SemaphoreType.DMA((head_peers,)),
            pltpu.SemaphoreType.DMA((head_peers,)),
            pltpu.SemaphoreType.DMA((IN_KINDS, peers)),
            pltpu.SemaphoreType.DMA((IN_KINDS, peers)),
            pltpu.SemaphoreType.DMA((OUT_KINDS, peers)),
            pltpu.SemaphoreType.DMA((OUT_KINDS, peers)),
        ],
        compiler_params=pltpu.CompilerParams(
            collective_id=0, has_side_effects=True, vmem_limit_bytes=64 * 1024 * 1024
        ),
        cost_estimate=pl.CostEstimate(
            flops=10 * scores * HEAD_DIM, bytes_accessed=4 * 1024 * 1024, transcendentals=scores
        ),
        name="whole_heads",
    )(queries, keys, values, outputs, grad_out, log_norm, glob_keys, glob_values)
    share = jax.ShapeDtypeStruct((GLOB // peers, col_count), full)
    hbm = pl.BlockSpec(memory_space=pltpu.HBM)
    return pl.pallas_call(
        finish_kernel,
        out_shape=(result, result, result, share, share),
        in_specs=[pl.BlockSpec(memory_space=pl.ANY)] * 4,
        out_specs=[hbm] * 5,
        scratch_shapes=[
            pltpu.VMEM((3, row_count, col_count), low),
            pltpu.VMEM((2, GLOB // peers, col_count), low),
            pltpu.VMEM((2, GLOB // peers, col_count), full),
            pltpu.SemaphoreType.DMA((4,)),
            pltpu.SemaphoreType.DMA((5,)),
        ],
        compiler_params=pltpu.CompilerParams(vmem_limit_bytes=64 * 1024 * 1024),
        cost_estimate=pl.CostEstimate(
            flops=0, bytes_accessed=2 * 1024 * 1024, transcendentals=0
        ),
        name="finish",
    )(dq, dk, dv, glob)


def program(mesh):
    peers = mesh.shape["ctx"]

    def body(queries, keys, values, outputs, grad_out, log_norm, glob_keys, glob_values, key_lists):
        row_count, col_count = queries.shape
        one_head_each = (
            row_count == BLOCK
            and col_count == peers * HEAD_DIM
            and peers == CLASSES * (RAND + 1)
            and GLOB % (16 * peers) == 0
        )
        if one_head_each:
            return whole_heads(
                peers, queries, keys, values, outputs, grad_out, log_norm, glob_keys, glob_values
            )
        return shards(
            queries, keys, values, outputs, grad_out, log_norm, glob_keys, glob_values, key_lists
        )

    return body


def solution(mesh):
    in_specs = (
        P("ctx", "head"),
        P("ctx", "head"),
        P("ctx", "head"),
        P("ctx", "head"),
        P(("ctx", "head"), None),
        P("head", "ctx"),
        P(None, "head"),
        P(None, "head"),
        P(),
    )
    out_specs = (
        P("ctx", "head"),
        P("ctx", "head"),
        P("ctx", "head"),
        P("ctx", "head"),
        P("ctx", "head"),
    )
    return jax.shard_map(program(mesh), mesh=mesh, in_specs=in_specs, out_specs=out_specs, check_vma=False)
```

```python
import functools
import math

import jax
import jax.numpy as jnp
from jax import lax
from jax.experimental import pallas as pl
from jax.experimental.pallas import tpu as pltpu
from jax.sharding import PartitionSpec as P

HEAD_DIM = 128
BLOCK = 128
GLOB = 256
RAND = 3
LOG2E = math.log2(math.e)


def extended_2(cells, sides, width):
    for axis, dim in sides:
        count = lax.axis_size(axis)
        ends = count - 1
        head = lax.slice_in_dim(cells, 0, width, axis=dim)
        tail = lax.slice_in_dim(cells, cells.shape[dim] - width, cells.shape[dim], axis=dim)
        cells = jnp.concatenate(
            [
                lax.ppermute(tail, axis, [(i, (i + 1) % count) for i in range(ends)]),
                cells,
                lax.ppermute(head, axis, [((i + 1) % count, i) for i in range(ends)]),
            ],
            axis=dim,
        )
    return cells


def passed_along(value, axis, by):
    peers = lax.axis_size(axis)
    pairs = [(i, i + by) for i in range(peers) if 0 <= i + by < peers]
    return lax.ppermute(value, axis, pairs)


def shifted(value, axis, by):
    peers = lax.axis_size(axis)
    return lax.ppermute(value, axis, [(i, (i + by) % peers) for i in range(peers)])


def tile_grads(query_rows, grad_rows, norm_rows, delta_rows, key_rows, value_rows, keep_mask):
    att_scale = HEAD_DIM ** (-0.5)
    scores = (
        jnp.einsum("nbd,nkd->nbk", query_rows, key_rows, preferred_element_type=jnp.float32)
        * att_scale
    )
    weights = jnp.exp(scores - norm_rows[:, :, None]) * keep_mask[:, None, :]
    dprobs = jnp.einsum("nbd,nkd->nbk", grad_rows, value_rows, preferred_element_type=jnp.float32)
    dscores = weights * (dprobs - delta_rows[:, :, None])
    weights_low = weights.astype(jnp.bfloat16)
    dscores_low = dscores.astype(jnp.bfloat16)
    grad_values = jnp.einsum(
        "nbk,nbd->nkd", weights_low, grad_rows, preferred_element_type=jnp.float32
    )
    grad_keys = (
        jnp.einsum("nbk,nbd->nkd", dscores_low, query_rows, preferred_element_type=jnp.float32)
        * att_scale
    )
    grad_queries = (
        jnp.einsum("nbk,nkd->nbd", dscores_low, key_rows, preferred_element_type=jnp.float32)
        * att_scale
    )
    return (grad_queries, grad_keys, grad_values)


def head_cols(source, head_index):
    return source[:, head_index * HEAD_DIM : (head_index + 1) * HEAD_DIM]


def head_blocks(source, head_index, num_blocks):
    return head_cols(source, head_index).reshape(num_blocks, BLOCK, HEAD_DIM)


def gather_tiles(tile_rows, slot_ids):
    picked = jnp.take(tile_rows, slot_ids, axis=0)
    return picked.reshape(slot_ids.shape[0], slot_ids.shape[1] * BLOCK, HEAD_DIM)


def tile_picker(slot_ids, hit_mask, num_blocks):
    one_hot = (
        slot_ids[:, :, None] == jnp.arange(num_blocks, dtype=jnp.int32)[None, None, :]
    ) & hit_mask[:, :, None]
    return one_hot.astype(jnp.float32)


def add_tiles(picker, flat_grads, num_blocks):
    tiled_grads = flat_grads.reshape(picker.shape[0], picker.shape[1], BLOCK, HEAD_DIM)
    summed = jnp.einsum("nle,nlbd->ebd", picker, tiled_grads, precision=lax.Precision.HIGHEST)
    return summed.reshape(num_blocks * BLOCK, HEAD_DIM)


def tile_keep(hit_mask, extra_cols):
    tile_cols = jnp.repeat(hit_mask.astype(jnp.float32), BLOCK, axis=1)
    return jnp.concatenate(
        [jnp.ones((hit_mask.shape[0], extra_cols), jnp.float32), tile_cols], axis=1
    )


def with_glob(glob_rows, tile_rows):
    spread = glob_rows[None]
    return jnp.concatenate([spread, tile_rows], axis=1)


def shards(queries, keys, values, outputs, grad_out, log_norm, glob_keys, glob_values, key_lists):
    row_count, col_count = queries.shape
    head_count = col_count // HEAD_DIM
    block_count = row_count // BLOCK
    group_count = lax.axis_size("ctx")
    my_group = lax.axis_index("ctx")
    first_block = my_group * block_count
    incoming = lax.all_to_all(grad_out, "head", split_axis=1, concat_axis=0, tiled=True)
    row_delta = jnp.sum(
        (incoming.astype(jnp.float32) * outputs.astype(jnp.float32)).reshape(
            row_count, head_count, HEAD_DIM
        ),
        axis=2,
    ).T
    own_lists = lax.dynamic_slice_in_dim(key_lists, first_block, block_count, 0)
    query_heads = [
        head_blocks(queries, head_index, block_count) for head_index in range(head_count)
    ]
    grad_heads = [
        head_blocks(incoming, head_index, block_count) for head_index in range(head_count)
    ]
    norm_heads = [
        log_norm[head_index].reshape(block_count, BLOCK) for head_index in range(head_count)
    ]
    delta_heads = [
        row_delta[head_index].reshape(block_count, BLOCK) for head_index in range(head_count)
    ]
    extended = extended_2(jnp.stack([keys, values]), (("ctx", 1),), BLOCK)
    ext_blocks = block_count + 2
    near_lists = own_lists[:, :3]
    near_live = near_lists >= 0
    near_slots = jnp.clip(near_lists - (first_block - 1), 0, ext_blocks - 1)
    near_keep = tile_keep(near_live, GLOB)
    near_picker = tile_picker(near_slots, near_live, ext_blocks)
    dq_parts, dk_parts, dv_parts, glob_dk_parts, glob_dv_parts = ([], [], [], [], [])
    for head_index in range(head_count):
        ext_keys = head_blocks(extended[0], head_index, ext_blocks)
        ext_values = head_blocks(extended[1], head_index, ext_blocks)
        key_rows = with_glob(head_cols(glob_keys, head_index), gather_tiles(ext_keys, near_slots))
        value_rows = with_glob(
            head_cols(glob_values, head_index), gather_tiles(ext_values, near_slots)
        )
        grad_q, grad_k, grad_v = tile_grads(
            query_heads[head_index],
            grad_heads[head_index],
            norm_heads[head_index],
            delta_heads[head_index],
            key_rows,
            value_rows,
            near_keep,
        )
        dq_parts.append(grad_q.reshape(row_count, HEAD_DIM))
        glob_dk_parts.append(jnp.sum(grad_k[:, :GLOB], axis=0))
        glob_dv_parts.append(jnp.sum(grad_v[:, :GLOB], axis=0))
        dk_parts.append(add_tiles(near_picker, grad_k[:, GLOB:], ext_blocks))
        dv_parts.append(add_tiles(near_picker, grad_v[:, GLOB:], ext_blocks))
    query_side = jnp.concatenate(dq_parts, axis=1)
    near_side = jnp.stack([jnp.concatenate(dk_parts, axis=1), jnp.concatenate(dv_parts, axis=1)])
    own_grads = near_side[:, BLOCK : BLOCK + row_count]
    for shift_by in (-1, 1):
        rim_piece = near_side[:, :BLOCK] if shift_by < 0 else near_side[:, BLOCK + row_count :]
        arrived = passed_along(rim_piece, "ctx", shift_by)
        if shift_by < 0:
            own_grads = own_grads.at[:, row_count - BLOCK :].add(arrived)
        else:
            own_grads = own_grads.at[:, :BLOCK].add(arrived)
    full_keep = jnp.ones((block_count, BLOCK), jnp.float32)
    all_hit = jnp.ones((block_count, 1), bool)
    own_pair = jnp.stack([keys, values])
    for round_index in range(RAND):
        hop = (round_index + 1) * group_count // (RAND + 1)
        fetched = shifted(own_pair, "ctx", -hop)
        target_first = (my_group + hop) % group_count * block_count
        far_slots = jnp.clip(own_lists[:, 3 + round_index] - target_first, 0, block_count - 1)[
            :, None
        ]
        far_picker = tile_picker(far_slots, all_hit, block_count)
        far_dq, far_dk, far_dv = ([], [], [])
        for head_index in range(head_count):
            far_keys = gather_tiles(head_blocks(fetched[0], head_index, block_count), far_slots)
            far_values = gather_tiles(head_blocks(fetched[1], head_index, block_count), far_slots)
            grad_q, grad_k, grad_v = tile_grads(
                query_heads[head_index],
                grad_heads[head_index],
                norm_heads[head_index],
                delta_heads[head_index],
                far_keys,
                far_values,
                full_keep,
            )
            far_dq.append(grad_q.reshape(row_count, HEAD_DIM))
            far_dk.append(add_tiles(far_picker, grad_k, block_count))
            far_dv.append(add_tiles(far_picker, grad_v, block_count))
        query_side = query_side + jnp.concatenate(far_dq, axis=1)
        far_pair = jnp.stack([jnp.concatenate(far_dk, axis=1), jnp.concatenate(far_dv, axis=1)])
        own_grads = own_grads + shifted(far_pair, "ctx", hop)
    glob_pair = jnp.stack(
        [jnp.concatenate(glob_dk_parts, axis=1), jnp.concatenate(glob_dv_parts, axis=1)]
    )
    summed_all = lax.psum(glob_pair, "ctx")
    share_rows = GLOB // group_count
    own_share = lax.dynamic_slice_in_dim(summed_all, my_group * share_rows, share_rows, 1)
    return (
        query_side.astype(jnp.bfloat16),
        own_grads[0].astype(jnp.bfloat16),
        own_grads[1].astype(jnp.bfloat16),
        own_share[0],
        own_share[1],
    )


HALVES = 1
HALF = BLOCK // HALVES
K_IN, V_IN, S_IN, Q_IN, G_IN = 0, 1, 2, 3, 3 + HALVES
IN_KINDS = 3 + 2 * HALVES
K_OUT, V_OUT, GLOB_OUT, Q_OUT = 0, 1, 2, 3
OUT_KINDS = 3 + HALVES
CLASSES = 2
CONTRACT_LAST = (((1,), (1,)), ((), ()))


def start_order(peers):
    half = peers // 2
    return [half] + [half + sign * by for by in range(1, half) for sign in (-1, 1)]


def head_kernel(
    peers,
    q_hbm,
    k_hbm,
    v_hbm,
    o_hbm,
    g_hbm,
    norm_hbm,
    gk_hbm,
    gv_hbm,
    dq_hbm,
    dk_hbm,
    dv_hbm,
    glob_hbm,
    q_own,
    k_own,
    v_own,
    g_part,
    dq_out,
    dk_out,
    dv_out,
    glob_out,
    q_all,
    k_all,
    v_all,
    g_all,
    stat_all,
    g_own,
    o_own,
    norm_own,
    stat_own,
    kt_all,
    dq_acc,
    dk_acc,
    dv_acc,
    dq_low,
    dk_low,
    dv_low,
    glob_low,
    load_sem,
    spread_send,
    spread_recv,
    in_send,
    in_recv,
    out_send,
    out_recv,
):
    me = lax.axis_index("ctx")
    my_head = lax.axis_index("head")
    head_peers = lax.axis_size("head")
    members = peers // CLASSES
    class_rows = members * BLOCK
    span = class_rows + GLOB
    share = GLOB // peers
    width = q_hbm.shape[1]
    part_rows = g_part.shape[0]
    order = start_order(peers)

    def cols(index):
        return pl.ds(pl.multiple_of(index * HEAD_DIM, HEAD_DIM), HEAD_DIM)

    def query_rows(half, index):
        at = half * members * CLASSES * HALF + (index % CLASSES) * members * HALF + (index // CLASSES) * HALF
        return pl.ds(at if isinstance(at, int) else pl.multiple_of(at, HALF), HALF)

    def half_rows(half):
        return pl.ds(half * HALF, HALF)

    def key_rows(index):
        at = (index % CLASSES) * span + (index // CLASSES) * BLOCK
        return pl.ds(at if isinstance(at, int) else pl.multiple_of(at, BLOCK), BLOCK)

    def remote(src, dst, send, recv, **device):
        return pltpu.make_async_remote_copy(
            src_ref=src,
            dst_ref=dst,
            send_sem=send,
            recv_sem=recv,
            device_id=device,
            device_id_type=pl.DeviceIdType.MESH,
        )

    loads = [
        pltpu.make_async_copy(o_hbm, o_own, load_sem.at[0]),
        pltpu.make_async_copy(norm_hbm, norm_own, load_sem.at[1]),
        pltpu.make_async_copy(
            gk_hbm.at[:, cols(me)], k_all.at[pl.ds(class_rows, GLOB)], load_sem.at[2]
        ),
        pltpu.make_async_copy(
            gv_hbm.at[:, cols(me)], v_all.at[pl.ds(class_rows, GLOB)], load_sem.at[3]
        ),
    ]
    firsts = [
        pltpu.make_async_copy(src, dst, load_sem.at[4 + at])
        for at, (src, dst) in enumerate(
            ((g_hbm, g_part), (k_hbm, k_own), (q_hbm, q_own), (v_hbm, v_own))
        )
    ]
    for load in firsts:
        load.start()
    for load in loads:
        load.start()

    barrier = pltpu.get_barrier_semaphore()
    for by in range(1, head_peers):
        pl.semaphore_signal(
            barrier,
            inc=1,
            device_id={"head": lax.rem(my_head + by, head_peers)},
            device_id_type=pl.DeviceIdType.MESH,
        )
    for by in order:
        pl.semaphore_signal(
            barrier,
            inc=1,
            device_id={"ctx": lax.rem(me + by, peers)},
            device_id_type=pl.DeviceIdType.MESH,
        )
    pl.semaphore_wait(barrier, head_peers - 1 + peers - 1)

    sends = []
    firsts[0].wait()

    def my_part():
        return pl.ds(pl.multiple_of(my_head * part_rows, part_rows), part_rows)

    def wide(index):
        return pl.ds(pl.multiple_of(index * width, width), width)

    for by in range(1, head_peers):
        to = lax.rem(my_head + by, head_peers)
        copy = remote(
            g_part.at[:, wide(to)],
            g_own.at[my_part()],
            spread_send.at[by],
            spread_recv.at[my_head],
            head=to,
        )
        copy.start()
        sends.append(copy)
    pltpu.make_async_copy(
        g_part.at[:, wide(my_head)], g_own.at[my_part()], spread_recv.at[my_head]
    ).start()

    def spread_in(kind, src, dst, from_rows, rows):
        for by in order:
            to = lax.rem(me + by, peers)
            copy = remote(
                src.at[from_rows, cols(to)],
                dst.at[rows(me)],
                in_send.at[kind, by],
                in_recv.at[kind, me],
                ctx=to,
            )
            copy.start()
            sends.append(copy)
        pltpu.make_async_copy(
            src.at[from_rows, cols(me)], dst.at[rows(me)], in_recv.at[kind, me]
        ).start()

    def arrived(kind, dst, rows):
        for index in range(peers):
            place = dst.at[rows(index)]
            pltpu.make_async_copy(place, place, in_recv.at[kind, index]).wait()

    places = [functools.partial(query_rows, half) for half in range(HALVES)]
    all_rows = pl.ds(0, BLOCK)
    firsts[1].wait()
    spread_in(K_IN, k_own, k_all, all_rows, key_rows)
    firsts[2].wait()
    spread_in(Q_IN, q_own, q_all, half_rows(0), places[0])
    firsts[3].wait()
    spread_in(V_IN, v_own, v_all, all_rows, key_rows)

    loads[0].wait()
    loads[1].wait()
    for index in range(head_peers):
        place = g_own.at[pl.ds(index * part_rows, part_rows)]
        pltpu.make_async_copy(place, place, spread_recv.at[index]).wait()
    spread_in(G_IN, g_own, g_all, half_rows(0), places[0])
    ones = jnp.ones((8, HEAD_DIM), jnp.float32)
    first = lax.broadcasted_iota(jnp.int32, (8, BLOCK), 0) == 0
    for index in range(peers):
        lanes = pl.ds(index * HEAD_DIM, HEAD_DIM)
        product = g_own[:, lanes].astype(jnp.float32) * o_own[:, lanes].astype(jnp.float32)
        delta = lax.dot_general(
            ones,
            product,
            CONTRACT_LAST,
            precision=lax.Precision.HIGHEST,
            preferred_element_type=jnp.float32,
        )
        norm = jnp.broadcast_to(norm_own[pl.ds(index, 1), :], (8, BLOCK))
        stat_own[index] = jnp.where(first, norm * LOG2E, delta)
    for by in order:
        to = lax.rem(me + by, peers)
        copy = remote(
            stat_own.at[to], stat_all.at[me], in_send.at[S_IN, by], in_recv.at[S_IN, me], ctx=to
        )
        copy.start()
        sends.append(copy)
    pltpu.make_async_copy(stat_own.at[me], stat_all.at[me], in_recv.at[S_IN, me]).start()

    for half in range(1, HALVES):
        spread_in(Q_IN + half, q_own, q_all, half_rows(half), places[half])
        spread_in(G_IN + half, g_own, g_all, half_rows(half), places[half])

    scale = HEAD_DIM**-0.5

    def dot(left, right):
        return jnp.dot(left, right, preferred_element_type=jnp.float32)

    def visit(half, blocks, key_at, key_count, keep):
        rows = pl.ds(query_rows(half, blocks[0]).start, len(blocks) * HALF)
        keys = pl.ds(key_at, key_count)
        norm, delta = (
            jnp.concatenate(
                [stat_all[block, row : row + 1, half * HALF : (half + 1) * HALF] for block in blocks],
                axis=1,
            )
            for row in range(2)
        )
        scores = lax.dot_general(
            k_all[keys, :], q_all[rows, :], CONTRACT_LAST, preferred_element_type=jnp.float32
        )
        weights = jnp.exp2(scores * (scale * LOG2E) - norm)
        if keep is not None:
            weights = jnp.where(keep, weights, 0.0)
        dprobs = lax.dot_general(
            v_all[keys, :], g_all[rows, :], CONTRACT_LAST, preferred_element_type=jnp.float32
        )
        dscores = (weights * (dprobs - delta)).astype(jnp.bfloat16)
        dq_acc[:, rows] += dot(kt_all[:, keys], dscores)
        dk_acc[keys, :] += dot(dscores, q_all[rows, :])
        dv_acc[keys, :] += dot(weights.astype(jnp.bfloat16), g_all[rows, :])

    def visit_near(half, blocks):
        near = [at for at in range(blocks[0] - 1, blocks[-1] + 2, CLASSES) if 0 <= at < peers]
        shape = (len(near) * BLOCK, len(blocks) * HALF)
        key_block = near[0] + CLASSES * (lax.broadcasted_iota(jnp.int32, shape, 0) // BLOCK)
        query_block = blocks[0] + CLASSES * (lax.broadcasted_iota(jnp.int32, shape, 1) // HALF)
        keep = jnp.abs(key_block - query_block) == 1
        visit(half, blocks, key_rows(near[0]).start, len(near) * BLOCK, keep)

    def put(kind, src, dst, from_rows, to_rows, block):
        @pl.when(me == block)
        def _():
            pltpu.make_async_copy(
                src.at[from_rows], dst.at[to_rows, cols(me)], out_recv.at[kind, me]
            ).start()

        @pl.when(me != block)
        def _():
            remote(
                src.at[from_rows],
                dst.at[to_rows, cols(me)],
                out_send.at[kind, block],
                out_recv.at[kind, me],
                ctx=block,
            ).start()

    dk_acc[...] = jnp.zeros_like(dk_acc)
    dv_acc[...] = jnp.zeros_like(dv_acc)
    dq_acc[...] = jnp.zeros_like(dq_acc)

    loads[2].wait()
    loads[3].wait()
    arrived(K_IN, k_all, key_rows)
    kt_all[...] = k_all[...].T
    arrived(V_IN, v_all, key_rows)
    for index in range(peers):
        place = stat_all.at[index]
        pltpu.make_async_copy(place, place, in_recv.at[S_IN, index]).wait()

    pair = 2
    for half in range(HALVES):
        arrived(Q_IN + half, q_all, places[half])
        arrived(G_IN + half, g_all, places[half])
        for part in range(CLASSES):
            for at in range(0, members, pair):
                visit_near(half, [part + CLASSES * (at + step) for step in range(pair)])
        for part in range(CLASSES):
            blocks = [part + CLASSES * at for at in range(members)]
            visit(half, blocks, part * class_rows, span, None)
            rows = pl.ds(query_rows(half, part).start, members * HALF)
            dq_low[rows, :] = (dq_acc[:, rows] * scale).T.astype(jnp.bfloat16)
            for block in blocks:
                put(Q_OUT + half, dq_low, dq_out, query_rows(half, block), half_rows(half), block)
            if half == HALVES - 1:
                own = pl.ds(part * span, class_rows)
                dk_low[own, :] = (dk_acc[own, :] * scale).astype(jnp.bfloat16)
                for block in blocks:
                    put(K_OUT, dk_low, dk_out, key_rows(block), all_rows, block)
                dv_low[own, :] = dv_acc[own, :].astype(jnp.bfloat16)
                for block in blocks:
                    put(V_OUT, dv_low, dv_out, key_rows(block), all_rows, block)

    middle = pl.ds(class_rows, GLOB)
    glob_low[0] = (dk_acc[middle, :] * scale).astype(jnp.bfloat16)
    glob_low[1] = dv_acc[middle, :].astype(jnp.bfloat16)

    def share_of(index):
        return glob_low.at[:, pl.ds(pl.multiple_of(index * share, share), share), :]

    for by in order:
        to = lax.rem(me + by, peers)
        copy = remote(
            share_of(to),
            glob_out.at[:, :, cols(me)],
            out_send.at[GLOB_OUT, to],
            out_recv.at[GLOB_OUT, me],
            ctx=to,
        )
        copy.start()
        sends.append(copy)
    pltpu.make_async_copy(
        share_of(me), glob_out.at[:, :, cols(me)], out_recv.at[GLOB_OUT, me]
    ).start()

    stores = []

    def store(at, src, dst):
        copy = pltpu.make_async_copy(src, dst, load_sem.at[8 + at])
        copy.start()
        stores.append(copy)

    for half in range(HALVES):
        for index in range(peers):
            place = dq_out.at[half_rows(half), cols(index)]
            pltpu.make_async_copy(place, place, out_recv.at[Q_OUT + half, index]).wait()
    store(0, dq_out, dq_hbm)
    for at, (kind, dst, home) in enumerate(((K_OUT, dk_out, dk_hbm), (V_OUT, dv_out, dv_hbm))):
        for index in range(peers):
            place = dst.at[:, cols(index)]
            pltpu.make_async_copy(place, place, out_recv.at[kind, index]).wait()
        store(1 + at, dst, home)
    for index in range(peers):
        place = glob_out.at[:, :, cols(index)]
        pltpu.make_async_copy(place, place, out_recv.at[GLOB_OUT, index]).wait()
    store(3, glob_out, glob_hbm)

    for copy in sends:
        copy.wait_send()
    halves = [(Q_OUT + half, dq_low, places[half]) for half in range(HALVES)]
    for by in order:
        to = lax.rem(me + by, peers)
        for kind, src, rows in [(K_OUT, dk_low, key_rows), (V_OUT, dv_low, key_rows)] + halves:
            place = src.at[rows(to)]
            pltpu.make_async_copy(place, place, out_send.at[kind, to]).wait()
    for copy in stores:
        copy.wait()


def finish_kernel(
    dq_in, dk_in, dv_in, glob_in, dq_out, dk_out, dv_out, gk_out, gv_out, held, low, wide, load, save
):
    loads = [
        pltpu.make_async_copy(src, dst, load.at[at])
        for at, (src, dst) in enumerate(
            ((glob_in, low), (dq_in, held.at[0]), (dk_in, held.at[1]), (dv_in, held.at[2]))
        )
    ]
    for copy in loads:
        copy.start()
    saves = [
        pltpu.make_async_copy(src, dst, save.at[at])
        for at, (src, dst) in enumerate(
            (
                (wide.at[0], gk_out),
                (wide.at[1], gv_out),
                (held.at[0], dq_out),
                (held.at[1], dk_out),
                (held.at[2], dv_out),
            )
        )
    ]
    loads[0].wait()
    wide[...] = low[...].astype(jnp.float32)
    saves[0].start()
    saves[1].start()
    for ready, copy in zip(loads[1:], saves[2:]):
        ready.wait()
        copy.start()
    for copy in saves:
        copy.wait()


def whole_heads(peers, queries, keys, values, outputs, grad_out, log_norm, glob_keys, glob_values):
    row_count, col_count = queries.shape
    tokens = peers * BLOCK
    low, full = jnp.bfloat16, jnp.float32
    head_peers = lax.axis_size("head")
    result = jax.ShapeDtypeStruct((row_count, col_count), low)
    scores = tokens * (GLOB + (RAND + 3) * BLOCK)
    dq, dk, dv, glob = pl.pallas_call(
        functools.partial(head_kernel, peers),
        out_shape=(
            result,
            result,
            result,
            jax.ShapeDtypeStruct((2, GLOB // peers, col_count), low),
        ),
        in_specs=[pl.BlockSpec(memory_space=pl.ANY)] * 8,
        out_specs=[pl.BlockSpec(memory_space=pl.ANY)] * 4,
        scratch_shapes=[
            pltpu.VMEM((row_count, col_count), low),
            pltpu.VMEM((row_count, col_count), low),
            pltpu.VMEM((row_count, col_count), low),
            pltpu.VMEM(grad_out.shape, low),
            pltpu.VMEM((row_count, col_count), low),
            pltpu.VMEM((row_count, col_count), low),
            pltpu.VMEM((row_count, col_count), low),
            pltpu.VMEM((2, GLOB // peers, col_count), low),
            pltpu.VMEM((tokens, HEAD_DIM), low),
            pltpu.VMEM((tokens + GLOB, HEAD_DIM), low),
            pltpu.VMEM((tokens + GLOB, HEAD_DIM), low),
            pltpu.VMEM((tokens, HEAD_DIM), low),
            pltpu.VMEM((peers, 8, BLOCK), full),
            pltpu.VMEM((row_count, col_count), low),
            pltpu.VMEM((row_count, col_count), low),
            pltpu.VMEM(log_norm.shape, full),
            pltpu.VMEM((peers, 8, BLOCK), full),
            pltpu.VMEM((HEAD_DIM, tokens + GLOB), low),
            pltpu.VMEM((HEAD_DIM, tokens), full),
            pltpu.VMEM((tokens + GLOB, HEAD_DIM), full),
            pltpu.VMEM((tokens + GLOB, HEAD_DIM), full),
            pltpu.VMEM((tokens, HEAD_DIM), low),
            pltpu.VMEM((tokens + GLOB, HEAD_DIM), low),
            pltpu.VMEM((tokens + GLOB, HEAD_DIM), low),
            pltpu.VMEM((2, GLOB, HEAD_DIM), low),
            pltpu.SemaphoreType.DMA((12,)),
            pltpu.SemaphoreType.DMA((head_peers,)),
            pltpu.SemaphoreType.DMA((head_peers,)),
            pltpu.SemaphoreType.DMA((IN_KINDS, peers)),
            pltpu.SemaphoreType.DMA((IN_KINDS, peers)),
            pltpu.SemaphoreType.DMA((OUT_KINDS, peers)),
            pltpu.SemaphoreType.DMA((OUT_KINDS, peers)),
        ],
        compiler_params=pltpu.CompilerParams(
            collective_id=0, has_side_effects=True, vmem_limit_bytes=64 * 1024 * 1024
        ),
        cost_estimate=pl.CostEstimate(
            flops=10 * scores * HEAD_DIM, bytes_accessed=4 * 1024 * 1024, transcendentals=scores
        ),
        name="whole_heads",
    )(queries, keys, values, outputs, grad_out, log_norm, glob_keys, glob_values)
    share = jax.ShapeDtypeStruct((GLOB // peers, col_count), full)
    hbm = pl.BlockSpec(memory_space=pltpu.HBM)
    return pl.pallas_call(
        finish_kernel,
        out_shape=(result, result, result, share, share),
        in_specs=[pl.BlockSpec(memory_space=pl.ANY)] * 4,
        out_specs=[hbm] * 5,
        scratch_shapes=[
            pltpu.VMEM((3, row_count, col_count), low),
            pltpu.VMEM((2, GLOB // peers, col_count), low),
            pltpu.VMEM((2, GLOB // peers, col_count), full),
            pltpu.SemaphoreType.DMA((4,)),
            pltpu.SemaphoreType.DMA((5,)),
        ],
        compiler_params=pltpu.CompilerParams(vmem_limit_bytes=64 * 1024 * 1024),
        cost_estimate=pl.CostEstimate(
            flops=0, bytes_accessed=2 * 1024 * 1024, transcendentals=0
        ),
        name="finish",
    )(dq, dk, dv, glob)


def program(mesh):
    peers = mesh.shape["ctx"]

    def body(queries, keys, values, outputs, grad_out, log_norm, glob_keys, glob_values, key_lists):
        row_count, col_count = queries.shape
        one_head_each = (
            row_count == BLOCK
            and col_count == peers * HEAD_DIM
            and peers == CLASSES * (RAND + 1)
            and GLOB % (16 * peers) == 0
        )
        if one_head_each:
            return whole_heads(
                peers, queries, keys, values, outputs, grad_out, log_norm, glob_keys, glob_values
            )
        return shards(
            queries, keys, values, outputs, grad_out, log_norm, glob_keys, glob_values, key_lists
        )

    return body


def solution(mesh):
    in_specs = (
        P("ctx", "head"),
        P("ctx", "head"),
        P("ctx", "head"),
        P("ctx", "head"),
        P(("ctx", "head"), None),
        P("head", "ctx"),
        P(None, "head"),
        P(None, "head"),
        P(),
    )
    out_specs = (
        P("ctx", "head"),
        P("ctx", "head"),
        P("ctx", "head"),
        P("ctx", "head"),
        P("ctx", "head"),
    )
    return jax.shard_map(program(mesh), mesh=mesh, in_specs=in_specs, out_specs=out_specs, check_vma=False)
```
